32 devices in a mesh: group: 2 (over x), blk: 16 (over z, y, core).
Axes of the slice: x: 2, y: 2, z: 4, core: 2. Of those that a mesh axis runs over, the one named last changes fastest.
Arguments:
- adjoint: float32 [10, 256, 8, 128], P('group', 'blk'), parts along dimension 0, may hold values from -6 to 6
- jac_diag: float32 [10, 5, 256, 8, 128], P('group', None, 'blk'), parts along dimension 0, may hold values from -2.5 to 2.5
- conv_mats: float32 [3, 5, 5], replicated, may hold values from -2.5 to 2.5
- face_scale: float32 [6, 256, 8, 128], P('group', 'blk'), parts along dimension 0, may hold values from 0.5 to 2
- kappa: float32 [512, 8, 128], P(('group', 'blk')), parts along dimension 0, may hold values from 0.1 to 1
- source: float32 [10, 256, 8, 128], P('group', 'blk'), parts along dimension 0, may hold values from -6 to 6
- box_of_row: int32 [65536, 1], P(('group', 'blk')), parts along dimension 0, may hold values from 0 to 15; in each aligned block of 2048 rows (0 to 2047, 2048 to 4095, ...) at most 256 rows name the same one
- lattice_cell: int32 [65536], P(('group', 'blk')), parts along dimension 0, may hold values from 0 to 3374
- lattice_frac: float32 [3, 65536], P(None, ('group', 'blk')), parts along dimension 1, may hold values from 0 to 1
- dres_dx: float32 [5, 3, 65536], P(None, None, ('group', 'blk')), parts along dimension 2, may hold values from -2.5 to 2.5
- dobj_dx: float32 [3, 65536], P(None, ('group', 'blk')), parts along dimension 1, may hold values from -6 to 6
Outputs:
- residual: float32 [10, 256, 8, 128], P('group', 'blk'), parts along dimension 0
- box_sens: float32 [6, 65536], P('group', 'blk'), parts along dimension 0
The draws below stay inside these ranges and needn't reach their ends.
There are 2 independent parts, one for each index of `group`. The reference program is written for one: setup_inputs(seed, part) draws one part's arguments, and reference() takes and returns one part's arrays. A program takes and returns all parts, laid end to end along the dimension named above; an argument that names none is the same for every part. Nothing has to cross between parts.
Inputs may be any that keep to these rules, and one draw needn't show every extreme that they name: `box_of_row`: among the 2048 rows of one device no box is named more than 256 times, one box exactly 256 times in some devices' rows; every box is named somewhere.
All inputs are finite; a program needn't handle non-finite values.
Results may differ from the reference program's by a relative error of at most 0.0003.
Values sent between devices are 32-bit elements; how exact they have to be, the bound alone decides.
No kernel may reach another device: no remote copies, remote signals or barrier semaphores. Data moves between devices by JAX's collectives and lax.ppermute only.
A program may use at most 320 MiB of HBM per device.

```python
import math
import jax
import jax.numpy as jnp
import numpy as np

FIELDS = 5
CY = 8
CZ = 128
LAT = 16
CP = 4096
NX = 256
WALL = 2048
ROWS = 32768
BOXES = 16
CAP = 256


def with_ends(drawn, rng, smallest, high):
    longest = drawn.shape.index(max(drawn.shape))
    spots = []
    for shift in (0, 1):
        where = [jax.random.randint(jax.random.fold_in(rng, axis), (), 0, length) for axis, length in enumerate(drawn.shape)]
        where[longest] = (where[longest] + shift) % drawn.shape[longest]
        spots.append(tuple(where))
    return drawn.at[spots[0]].set(smallest).at[spots[1]].set(high)


def block_levels(own_key, dims, shards, smallest, largest):
    factor_of, own = 1.0, jax.random.fold_in(own_key, 6)
    for dim, blocks in shards:
        heights = jnp.exp(jax.random.uniform(jax.random.fold_in(own, dim), (blocks,), jnp.float32, smallest / len(shards), largest / len(shards)))
        factor_of = factor_of * jnp.repeat(heights, dims[dim] // blocks).reshape([-1 if axis == dim else 1 for axis in range(len(dims))])
    return factor_of


def deal_out(stream_key, own, number, rows, amount, top, most, lean):
    sequence = jax.random.permutation(stream_key, amount)
    packed, common = load_shares(amount, rows * top, most, lean, True), load_shares(amount, rows * top, most, lean, False)
    places = jnp.arange(amount)

    def named(lengths, turn):
        used = int((lengths > 0).sum())
        fixed = max(1, used // 4)
        moved = fixed + (places - fixed + turn * (used - fixed)) % max(1, amount - fixed)
        return jnp.zeros((amount,), jnp.int32).at[sequence[jnp.where(places < fixed, places, moved)]].set(jnp.asarray(lengths, jnp.int32))

    lengths = jnp.where(number % 4 == 0, named(packed, number // 4), named(common, number - number // 4 - 1))
    mixed = jax.random.permutation(jax.random.fold_in(own, 3), amount)
    donor, taker = mixed[0:amount // 2 * 2:2], mixed[1:amount // 2 * 2:2]
    room = jnp.minimum(lengths[donor] - 1, most - lengths[taker]) // 2
    room = jnp.where((donor == sequence[0]) | (taker == sequence[0]) | (lengths[taker] == 0), 0, jnp.maximum(room, 0))
    moved = jax.random.randint(jax.random.fold_in(own, 4), (amount // 2,), 0, 1 << 20) % (room + 1)
    lengths = lengths.at[donor].add(-moved).at[taker].add(moved)
    members = jnp.searchsorted(jnp.cumsum(lengths), jnp.arange(rows * top), side="right").astype(jnp.int32)
    grid = members.reshape(top, rows).T
    grid = grid[jax.random.permutation(jax.random.fold_in(own, 1), rows)]
    turn = jax.random.randint(jax.random.fold_in(own, 2), (rows, 1), 0, top)
    return jnp.take_along_axis(grid, (jnp.arange(top)[None, :] + turn) % top, axis=1)


def load_shares(number_of, total, reach, slope, full):
    portions = [(1 << 20) // math.isqrt(standing ** slope) + 1 for standing in range(1, number_of + 1)]
    largest = reach if full else min(reach, max(-(-total // number_of), total * portions[0] // sum(portions)))
    least = 1 if total - largest >= number_of - 1 else 0
    counts, spare = [largest] + [least] * (number_of - 1), total - largest - least * (number_of - 1)
    while spare > 0:
        movable = [i for i in range(1, number_of) if counts[i] < largest] or [i for i in range(1, number_of) if counts[i] < reach]
        pool, left = sum([portions[i] for i in movable]), spare
        for i in movable:
            extra = min(reach - counts[i], max(1, left * portions[i] // pool), spare)
            counts[i] = counts[i] + extra
            spare = spare - extra
    return np.array(counts)


def gaussian(stream_key, shape, deviation, bound, split=(), kind=jnp.bfloat16):
    factor_of = block_levels(stream_key, shape, split, -0.22, 0.18) if split else 1.0
    values = jax.random.normal(stream_key, shape, jnp.float32) * deviation * factor_of
    return jnp.minimum(jnp.maximum(values, -bound), bound).astype(kind)


def setup_inputs(seed: int = 0, part: int = 0) -> dict:
    streams_of = jax.random.split(jax.random.key(seed), 12)
    part_splits = jax.random.split(jax.random.fold_in(streams_of[11], part), 12)
    adjoint = gaussian(part_splits[0], (FIELDS, NX, CY, CZ), 1.0, 6.0, ((1, 16),), jnp.float32)
    jac_diag = gaussian(part_splits[1], (FIELDS, FIELDS, NX, CY, CZ), FIELDS ** -0.5, 2.5, ((2, 16),), jnp.float32)
    conv_mats = gaussian(streams_of[2], (3, FIELDS, FIELDS), FIELDS ** -0.5, 2.5, (), jnp.float32)
    face_scale = jnp.clip(jnp.exp(math.log(2.0) - 1.3862944 * jax.random.uniform(part_splits[3], (3, NX, CY, CZ), jnp.float32) ** block_levels(part_splits[3], (3, NX, CY, CZ), ((1, 16),), -0.2, 0.2)), 0.5, 2.0)
    kappa = jnp.clip(jnp.exp(math.log(1.0) - 2.3025851 * jax.random.uniform(part_splits[4], (NX, CY, CZ), jnp.float32) ** block_levels(part_splits[4], (NX, CY, CZ), ((0, 16),), -0.2, 0.2)), 0.1, 1.0)
    source = gaussian(part_splits[5], (FIELDS, NX, CY, CZ), 1.0, 6.0, ((1, 16),), jnp.float32)
    box_of_row_keys = jax.random.split(jax.random.fold_in(part_splits[6], 1), ROWS // WALL)
    box_of_row_turns = jax.random.permutation(jax.random.fold_in(part_splits[6], 3), ROWS // WALL)
    box_of_row = jax.vmap(lambda own, number: deal_out(jax.random.fold_in(part_splits[6], 2), own, number, WALL, BOXES, 1, CAP, 2))(box_of_row_keys, box_of_row_turns).reshape((ROWS, 1))
    lattice_cell = with_ends(jax.random.randint(part_splits[7], (ROWS,), 0, (LAT - 1) ** 3), jax.random.fold_in(part_splits[7], 1), 0, ((LAT - 1) ** 3) - 1).astype(jnp.int32)
    lattice_frac = jnp.clip(1.0 * jax.random.uniform(part_splits[8], (3, ROWS), jnp.float32) ** block_levels(part_splits[8], (3, ROWS), ((1, 16),), -0.2, 0.2), 0.0, 1.0)
    dres_dx = gaussian(part_splits[9], (FIELDS, 3, ROWS), FIELDS ** -0.5, 2.5, ((2, 16),), jnp.float32)
    dobj_dx = gaussian(part_splits[10], (3, ROWS), 1.0, 6.0, ((1, 16),), jnp.float32)
    return {"adjoint": adjoint, "jac_diag": jac_diag, "conv_mats": conv_mats, "face_scale": face_scale, "kappa": kappa, "source": source, "box_of_row": box_of_row, "lattice_cell": lattice_cell, "lattice_frac": lattice_frac, "dres_dx": dres_dx, "dobj_dx": dobj_dx}


def neighbour(arr, dim, off):
    parts = [slice(1, -1), slice(1, -1), slice(1, -1)]
    parts[dim] = slice(1 + off, arr.shape[dim + 1] - 1 + off)
    return arr[(slice(None),) + tuple(parts)]


def small_apply(coeff, fields):
    count = fields.shape[0]
    rows = []
    for out_index in range(count):
        total = coeff[0, out_index] * fields[0]
        for in_index in range(1, count):
            total = total + coeff[in_index, out_index] * fields[in_index]
        rows.append(total)
    return jnp.stack(rows, 0)


def sweep(padded, jac_diag, conv_mats, face_scale, source):
    psi_pad = padded[:-1]
    kap_pad = padded[-1:]
    centre = neighbour(psi_pad, 0, 0)
    kap_centre = neighbour(kap_pad, 0, 0)
    result = small_apply(jac_diag, centre)
    for direction in range(3):
        upper = neighbour(psi_pad, direction, 1)
        lower = neighbour(psi_pad, direction, -1)
        flux = small_apply(conv_mats[direction], upper - lower)
        result = result + 0.5 * face_scale[direction][None] * flux
        for off, beside in ((1, upper), (-1, lower)):
            weight = 0.5 * (kap_centre + neighbour(kap_pad, direction, off))
            result = result - weight * (beside - centre)
    return result - source


def corner_terms(sens, cell, frac):
    edge = LAT
    inner = LAT - 1
    first = cell // (inner * inner)
    second = (cell // inner) % inner
    third = cell % inner
    ids = []
    vals = []
    for step_a in (0, 1):
        for step_b in (0, 1):
            for step_c in (0, 1):
                ids.append((first + step_a) * edge * edge + (second + step_b) * edge + third + step_c)
                weight_a = frac[0] if step_a else 1.0 - frac[0]
                weight_b = frac[1] if step_b else 1.0 - frac[1]
                weight_c = frac[2] if step_c else 1.0 - frac[2]
                vals.append(sens * (weight_a * weight_b * weight_c)[None])
    return jnp.stack(ids, 0).astype(jnp.int32), jnp.stack(vals, 1)


def wall_sens(adjoint, dres_dx, dobj_dx):
    wall_psi = adjoint[:, :, 0, :].reshape(adjoint.shape[0], -1)
    total = dres_dx[0] * wall_psi[0][None]
    for index in range(1, wall_psi.shape[0]):
        total = total + dres_dx[index] * wall_psi[index][None]
    return dobj_dx - total


def reference(adjoint, jac_diag, conv_mats, face_scale, kappa, source, box_of_row, lattice_cell, lattice_frac, dres_dx, dobj_dx):
    stacked = jnp.concatenate([adjoint, kappa[None]], 0)
    padded = jnp.pad(stacked, ((0, 0), (1, 1), (1, 1), (1, 1)))
    residual = sweep(padded, jac_diag, conv_mats, face_scale, source)
    sens = wall_sens(adjoint, dres_dx, dobj_dx)
    ids, vals = corner_terms(sens, lattice_cell, lattice_frac)
    target = (box_of_row[:, 0][None, :] * CP + ids).reshape(-1)
    box_sens = jnp.zeros((3, BOXES * CP), jnp.float32).at[:, target].add(vals.reshape(3, -1))
    return residual, box_sens
```

```python
import functools

import jax
import jax.numpy as jnp
from jax import lax
from jax.experimental import pallas as pl
from jax.experimental.pallas import tpu as pltpu
from jax.sharding import PartitionSpec as P

LAT = 16
CHUNK = 256
F32 = jnp.float32
BF16 = jnp.bfloat16
NT = (((1,), (1,)), ((), ()))
NN = (((1,), (0,)), ((), ()))


def split_two(x):
    hi = x.astype(BF16)
    lo = (x - hi.astype(F32)).astype(BF16)
    return hi, lo


def pack_kernel(boxes, cap, adj_ref, box_ref, cell_ref, frac_ref, dres_ref, dobj_ref, out_ref, ranks_ref):
    fields, planes, _, lanes = adj_ref.shape
    rows = planes * lanes
    box = box_ref[...]

    chunks = rows // CHUNK
    names = lax.broadcasted_iota(jnp.int32, (boxes, CHUNK), 0)
    hot = [(box[:, j * CHUNK:(j + 1) * CHUNK] == names).astype(F32) for j in range(chunks)]
    earlier = (
        lax.broadcasted_iota(jnp.int32, (CHUNK, CHUNK), 0)
        < lax.broadcasted_iota(jnp.int32, (CHUNK, CHUNK), 1)
    ).astype(F32).astype(BF16)
    counts = lax.dot_general(
        jnp.concatenate(hot, 0).astype(BF16), earlier, NN, preferred_element_type=F32
    )
    offset = jnp.zeros((boxes, 1), F32)
    for j in range(chunks):
        here = counts[j * boxes:(j + 1) * boxes]
        ranks_ref[:, j * CHUNK:(j + 1) * CHUNK] = jnp.sum(
            hot[j] * (here + offset), axis=0, keepdims=True
        )
        offset = offset + here[:, CHUNK - 1:] + hot[j][:, CHUNK - 1:]

    total = jnp.zeros((boxes * 16, cap), F32)
    slots = lax.broadcasted_iota(jnp.int32, (cap, CHUNK), 0).astype(F32)
    per = CHUNK // lanes
    for j in range(chunks):
        part = slice(j * CHUNK, (j + 1) * CHUNK)
        acc = dobj_ref[:, part]
        for k in range(fields):
            psi = jnp.concatenate(
                [adj_ref[k, x, 0:1, :] for x in range(j * per, (j + 1) * per)], 1
            )
            acc = acc - dres_ref[k, :, part] * psi
        values = jnp.concatenate(
            [acc, frac_ref[:, part], cell_ref[:, part].astype(F32), jnp.zeros((1, CHUNK), F32)], 0
        )
        hi = values.astype(BF16).astype(F32)
        both = jnp.concatenate([hi, values - hi], 0)
        mine = box[:, part]
        lhs = jnp.concatenate(
            [jnp.where(mine == b, both, 0.0) for b in range(boxes)], 0
        ).astype(BF16)
        rhs = (slots == ranks_ref[:, part]).astype(F32).astype(BF16)
        total = total + lax.dot_general(lhs, rhs, NT, preferred_element_type=F32)
    for b in range(boxes):
        out_ref[b] = total[b * 16:b * 16 + 8] + total[b * 16 + 8:b * 16 + 16]


def sum_kernel(got_ref, out_ref):
    sources, _, cap = got_ref.shape
    inner = LAT - 1
    points = lax.broadcasted_iota(jnp.int32, (LAT, cap), 0).astype(F32)
    both = jnp.zeros((6 * LAT, LAT * LAT), F32)
    for s in range(sources):
        block = got_ref[s]
        cell = block[6:7]
        first = jnp.floor((cell + 0.5) * (1.0 / (inner * inner)))
        rest = cell - first * (inner * inner)
        second = jnp.floor((rest + 0.5) * (1.0 / inner))
        third = rest - second * inner
        tent = []
        for d, low in enumerate((first, second, third)):
            u = block[3 + d:4 + d]
            tent.append(
                jnp.where(points == low, 1.0 - u, 0.0) + jnp.where(points == low + 1.0, u, 0.0)
            )
        left = jnp.concatenate([tent[0] * block[c:c + 1] for c in range(3)], 0)
        right = jnp.concatenate([tent[1][b:b + 1] * tent[2] for b in range(LAT)], 0)
        left_hi, left_lo = split_two(left)
        right_hi, right_lo = split_two(right)
        lhs = jnp.concatenate([left_hi, left_lo], 0)
        both = both + lax.dot_general(lhs, right_hi, NT, preferred_element_type=F32)
        both = both + lax.dot_general(lhs, right_lo, NT, preferred_element_type=F32)
    result = both[:3 * LAT] + both[3 * LAT:]
    for c in range(3):
        for a in range(LAT):
            out_ref[c:c + 1, a * LAT * LAT:(a + 1) * LAT * LAT] = result[c * LAT + a:c * LAT + a + 1]


def sweep_kernel(conv_ref, adj_ref, jac_ref, face_ref, kap_ref, src_ref, low_ref, high_ref, out_ref):
    fields, planes, rows, lanes = adj_ref.shape
    row = lax.broadcasted_iota(jnp.int32, (rows, lanes), 0)
    lane = lax.broadcasted_iota(jnp.int32, (rows, lanes), 1)
    keep = (
        (row < rows - 1, row > 0),
        (lane < lanes - 1, lane > 0),
    )

    def at(field, x):
        if x < 0:
            return low_ref[field, 0]
        if x == planes:
            return high_ref[field, 0]
        return adj_ref[field, x] if field < fields else kap_ref[x]

    def shifted(value, dim):
        size = value.shape[dim]
        up = jnp.where(keep[dim][0], pltpu.roll(value, size - 1, dim), 0.0)
        down = jnp.where(keep[dim][1], pltpu.roll(value, 1, dim), 0.0)
        return up, down

    for x in range(planes):
        centre = [at(f, x) for f in range(fields)]
        kap = at(fields, x)
        result = []
        for f in range(fields):
            total = jac_ref[0, f, x] * centre[0]
            for k in range(1, fields):
                total = total + jac_ref[k, f, x] * centre[k]
            result.append(total - src_ref[f, x])
        for direction in range(3):
            if direction == 0:
                pair = [(at(f, x + 1), at(f, x - 1)) for f in range(fields + 1)]
            else:
                pair = [shifted(v, direction - 1) for v in centre + [kap]]
            scale = 0.5 * face_ref[direction, x]
            diff = [scale * (pair[k][0] - pair[k][1]) for k in range(fields)]
            up = 0.5 * (kap + pair[fields][0])
            down = 0.5 * (kap + pair[fields][1])
            for f in range(fields):
                total = result[f]
                for k in range(fields):
                    total = total + conv_ref[(direction * fields + k) * fields + f] * diff[k]
                total = total - up * (pair[f][0] - centre[f]) - down * (pair[f][1] - centre[f])
                result[f] = total
        for f in range(fields):
            out_ref[f, x] = result[f]


def local(
    adjoint,
    jac_diag,
    conv_mats,
    face_scale,
    kappa,
    source,
    box_of_row,
    lattice_cell,
    lattice_frac,
    dres_dx,
    dobj_dx,
):
    boxes = lax.axis_size("blk")
    rows = box_of_row.shape[0]
    cap = 2 * rows // boxes
    vmem = pl.BlockSpec(memory_space=pltpu.VMEM)
    smem = pl.BlockSpec(memory_space=pltpu.SMEM)

    ends = boxes - 1
    stacked = jnp.concatenate([adjoint, kappa[None]], 0)
    low = lax.ppermute(stacked[:, -1:], "blk", [(i, i + 1) for i in range(ends)])
    high = lax.ppermute(stacked[:, :1], "blk", [(i + 1, i) for i in range(ends)])

    packed = pl.pallas_call(
        functools.partial(pack_kernel, boxes, cap),
        out_shape=jax.ShapeDtypeStruct((boxes, 8, cap), F32),
        in_specs=[vmem] * 6,
        out_specs=vmem,
        scratch_shapes=[pltpu.VMEM((1, rows), F32)],
        name="pack_rows",
    )(
        adjoint,
        box_of_row.reshape(1, rows),
        lattice_cell.reshape(1, rows),
        lattice_frac,
        dres_dx,
        dobj_dx,
    )
    got = lax.all_to_all(packed, "blk", 0, 0, tiled=True)

    residual = pl.pallas_call(
        sweep_kernel,
        out_shape=jax.ShapeDtypeStruct(adjoint.shape, F32),
        in_specs=[smem] + [vmem] * 7,
        out_specs=vmem,
        name="sweep",
    )(conv_mats.reshape(-1), adjoint, jac_diag, face_scale, kappa, source, low, high)

    box_sens = pl.pallas_call(
        sum_kernel,
        out_shape=jax.ShapeDtypeStruct((3, LAT**3), F32),
        in_specs=[vmem],
        out_specs=vmem,
        name="sum_rows",
    )(got)
    return residual, box_sens


def solution(mesh):
    in_specs = (
        P("group", "blk", None, None),
        P("group", None, "blk", None, None),
        P(),
        P("group", "blk", None, None),
        P(("group", "blk"), None, None),
        P("group", "blk", None, None),
        P(("group", "blk"), None),
        P(("group", "blk")),
        P(None, ("group", "blk")),
        P(None, None, ("group", "blk")),
        P(None, ("group", "blk")),
    )
    out_specs = (P("group", "blk", None, None), P("group", "blk"))
    return jax.shard_map(local, mesh=mesh, in_specs=in_specs, out_specs=out_specs, check_vma=False)
```

```python
import functools

import jax
import jax.numpy as jnp
from jax import lax
from jax.experimental import pallas as pl
from jax.experimental.pallas import tpu as pltpu
from jax.sharding import PartitionSpec as P

LAT = 16
CHUNK = 256
SMALL = 8 * 2**20
F32 = jnp.float32
BF16 = jnp.bfloat16
NT = (((1,), (1,)), ((), ()))
NN = (((1,), (0,)), ((), ()))


def split_two(x):
    hi = x.astype(BF16)
    lo = (x - hi.astype(F32)).astype(BF16)
    return hi, lo


def pack_kernel(
    boxes,
    cap,
    adj_ref,
    kap_ref,
    box_ref,
    cell_ref,
    frac_ref,
    dres_ref,
    dobj_ref,
    out_ref,
    mate_ref,
    other_ref,
    ranks_ref,
):
    fields, planes, _, lanes = adj_ref.shape
    even = lax.axis_index("blk") % 2 == 0
    for f in range(fields + 1):
        first = adj_ref[f, 0] if f < fields else kap_ref[0]
        last = adj_ref[f, planes - 1] if f < fields else kap_ref[planes - 1]
        mate_ref[f] = jnp.where(even, last, first)
        other_ref[f] = jnp.where(even, first, last)
    rows = planes * lanes
    box = box_ref[...]

    chunks = rows // CHUNK
    names = lax.broadcasted_iota(jnp.int32, (boxes, CHUNK), 0)
    hot = [(box[:, j * CHUNK:(j + 1) * CHUNK] == names).astype(F32) for j in range(chunks)]
    earlier = (
        lax.broadcasted_iota(jnp.int32, (CHUNK, CHUNK), 0)
        < lax.broadcasted_iota(jnp.int32, (CHUNK, CHUNK), 1)
    ).astype(F32).astype(BF16)
    counts = lax.dot_general(
        jnp.concatenate(hot, 0).astype(BF16), earlier, NN, preferred_element_type=F32
    )
    offset = jnp.zeros((boxes, 1), F32)
    for j in range(chunks):
        here = counts[j * boxes:(j + 1) * boxes]
        ranks_ref[:, j * CHUNK:(j + 1) * CHUNK] = jnp.sum(
            hot[j] * (here + offset), axis=0, keepdims=True
        )
        offset = offset + here[:, CHUNK - 1:] + hot[j][:, CHUNK - 1:]

    total = jnp.zeros((boxes * 16, cap), F32)
    slots = lax.broadcasted_iota(jnp.int32, (cap, CHUNK), 0).astype(F32)
    per = CHUNK // lanes
    for j in range(chunks):
        part = slice(j * CHUNK, (j + 1) * CHUNK)
        acc = dobj_ref[:, part]
        for k in range(fields):
            psi = jnp.concatenate(
                [adj_ref[k, x, 0:1, :] for x in range(j * per, (j + 1) * per)], 1
            )
            acc = acc - dres_ref[k, :, part] * psi
        values = jnp.concatenate(
            [acc, frac_ref[:, part], cell_ref[:, part].astype(F32), jnp.zeros((1, CHUNK), F32)], 0
        )
        hi = values.astype(BF16).astype(F32)
        both = jnp.concatenate([hi, values - hi], 0)
        mine = box[:, part]
        lhs = jnp.concatenate(
            [jnp.where(mine == b, both, 0.0) for b in range(boxes)], 0
        ).astype(BF16)
        rhs = (slots == ranks_ref[:, part]).astype(F32).astype(BF16)
        total = total + lax.dot_general(lhs, rhs, NT, preferred_element_type=F32)
    for b in range(boxes):
        out_ref[b] = total[b * 16:b * 16 + 8] + total[b * 16 + 8:b * 16 + 16]


def sum_kernel(got_ref, out_ref):
    sources, _, cap = got_ref.shape
    inner = LAT - 1
    points = lax.broadcasted_iota(jnp.int32, (LAT, cap), 0).astype(F32)
    both = jnp.zeros((6 * LAT, LAT * LAT), F32)
    for s in range(sources):
        block = got_ref[s]
        cell = block[6:7]
        first = jnp.floor((cell + 0.5) * (1.0 / (inner * inner)))
        rest = cell - first * (inner * inner)
        second = jnp.floor((rest + 0.5) * (1.0 / inner))
        third = rest - second * inner
        tent = []
        for d, low in enumerate((first, second, third)):
            u = block[3 + d:4 + d]
            tent.append(
                jnp.where(points == low, 1.0 - u, 0.0) + jnp.where(points == low + 1.0, u, 0.0)
            )
        left = jnp.concatenate([tent[0] * block[c:c + 1] for c in range(3)], 0)
        right = jnp.concatenate([tent[1][b:b + 1] * tent[2] for b in range(LAT)], 0)
        left_hi, left_lo = split_two(left)
        right_hi, right_lo = split_two(right)
        lhs = jnp.concatenate([left_hi, left_lo], 0)
        both = both + lax.dot_general(lhs, right_hi, NT, preferred_element_type=F32)
        both = both + lax.dot_general(lhs, right_lo, NT, preferred_element_type=F32)
    result = both[:3 * LAT] + both[3 * LAT:]
    for c in range(3):
        for a in range(LAT):
            out_ref[c:c + 1, a * LAT * LAT:(a + 1) * LAT * LAT] = result[c * LAT + a:c * LAT + a + 1]


def sweep_kernel(
    conv_ref, adj_ref, jac_ref, face_ref, kap_ref, src_ref, mate_ref, other_ref, out_ref
):
    fields, planes, rows, lanes = adj_ref.shape
    even = lax.axis_index("blk") % 2 == 0
    row = lax.broadcasted_iota(jnp.int32, (rows, lanes), 0)
    lane = lax.broadcasted_iota(jnp.int32, (rows, lanes), 1)
    keep = (
        (row < rows - 1, row > 0),
        (lane < lanes - 1, lane > 0),
    )

    def at(field, x):
        if x < 0:
            return jnp.where(even, other_ref[field], mate_ref[field])
        if x == planes:
            return jnp.where(even, mate_ref[field], other_ref[field])
        return adj_ref[field, x] if field < fields else kap_ref[x]

    def shifted(value, dim):
        size = value.shape[dim]
        up = jnp.where(keep[dim][0], pltpu.roll(value, size - 1, dim), 0.0)
        down = jnp.where(keep[dim][1], pltpu.roll(value, 1, dim), 0.0)
        return up, down

    for x in range(planes):
        centre = [at(f, x) for f in range(fields)]
        kap = at(fields, x)
        result = []
        for f in range(fields):
            total = jac_ref[0, f, x] * centre[0]
            for k in range(1, fields):
                total = total + jac_ref[k, f, x] * centre[k]
            result.append(total - src_ref[f, x])
        for direction in range(3):
            if direction == 0:
                pair = [(at(f, x + 1), at(f, x - 1)) for f in range(fields + 1)]
            else:
                pair = [shifted(v, direction - 1) for v in centre + [kap]]
            scale = 0.5 * face_ref[direction, x]
            diff = [scale * (pair[k][0] - pair[k][1]) for k in range(fields)]
            up = 0.5 * (kap + pair[fields][0])
            down = 0.5 * (kap + pair[fields][1])
            for f in range(fields):
                total = result[f]
                for k in range(fields):
                    total = total + conv_ref[k, direction, f] * diff[k]
                total = total - up * (pair[f][0] - centre[f]) - down * (pair[f][1] - centre[f])
                result[f] = total
        for f in range(fields):
            out_ref[f, x] = result[f]


def local(
    adjoint,
    jac_diag,
    conv_mats,
    face_scale,
    kappa,
    source,
    box_of_row,
    lattice_cell,
    lattice_frac,
    dres_dx,
    dobj_dx,
):
    boxes = lax.axis_size("blk")
    rows = box_of_row.shape[0]
    cap = 2 * rows // boxes
    vmem = pl.BlockSpec(memory_space=pltpu.VMEM)
    smem = pl.BlockSpec(memory_space=pltpu.SMEM)

    halo = jax.ShapeDtypeStruct((adjoint.shape[0] + 1,) + adjoint.shape[2:], F32)
    packed, to_mate, to_other = pl.pallas_call(
        functools.partial(pack_kernel, boxes, cap),
        out_shape=(jax.ShapeDtypeStruct((boxes, 8, cap), F32), halo, halo),
        in_specs=[vmem] * 7,
        out_specs=(vmem, vmem, vmem),
        scratch_shapes=[pltpu.VMEM((1, rows), F32)],
        compiler_params=pltpu.CompilerParams(vmem_limit_bytes=SMALL),
        name="pack_rows",
    )(
        adjoint,
        kappa,
        box_of_row.reshape(1, rows),
        lattice_cell.reshape(1, rows),
        lattice_frac,
        dres_dx,
        dobj_dx,
    )
    pairs = [(i, i + 1) for i in range(boxes - 1)]
    both_ways = [[p for i, j in pairs if i % 2 == turn for p in ((i, j), (j, i))] for turn in (0, 1)]
    mate = lax.ppermute(to_mate, "blk", both_ways[0])
    other = lax.ppermute(to_other, "blk", both_ways[1])
    got = lax.all_to_all(packed, "blk", 0, 0, tiled=True)

    residual = pl.pallas_call(
        sweep_kernel,
        out_shape=jax.ShapeDtypeStruct(adjoint.shape, F32),
        in_specs=[smem] + [vmem] * 7,
        out_specs=vmem,
        compiler_params=pltpu.CompilerParams(vmem_limit_bytes=SMALL),
        name="sweep",
    )(conv_mats.transpose(1, 0, 2), adjoint, jac_diag, face_scale, kappa, source, mate, other)

    box_sens = pl.pallas_call(
        sum_kernel,
        out_shape=jax.ShapeDtypeStruct((3, LAT**3), F32),
        in_specs=[vmem],
        out_specs=vmem,
        compiler_params=pltpu.CompilerParams(vmem_limit_bytes=SMALL),
        name="sum_rows",
    )(got)
    return residual, box_sens


def solution(mesh):
    in_specs = (
        P("group", "blk", None, None),
        P("group", None, "blk", None, None),
        P(),
        P("group", "blk", None, None),
        P(("group", "blk"), None, None),
        P("group", "blk", None, None),
        P(("group", "blk"), None),
        P(("group", "blk")),
        P(None, ("group", "blk")),
        P(None, None, ("group", "blk")),
        P(None, ("group", "blk")),
    )
    out_specs = (P("group", "blk", None, None), P("group", "blk"))
    return jax.shard_map(local, mesh=mesh, in_specs=in_specs, out_specs=out_specs, check_vma=False)
```

```python
import functools

import jax
import jax.numpy as jnp
from jax import lax
from jax.experimental import pallas as pl
from jax.experimental.pallas import tpu as pltpu
from jax.sharding import PartitionSpec as P

LAT = 16
CHUNK = 256
SMALL = 12 * 2**20
F32 = jnp.float32
BF16 = jnp.bfloat16
NT = (((1,), (1,)), ((), ()))
NN = (((1,), (0,)), ((), ()))


def split_two(x):
    hi = x.astype(BF16)
    lo = (x - hi.astype(F32)).astype(BF16)
    return hi, lo


def on_even():
    return lax.axis_index("blk") % 2 == 0


def stay(*arrays):
    return [pltpu.with_memory_space_constraint(a, pltpu.HBM) for a in arrays]


def start_all(copies):
    for copy in copies:
        copy.start()
    return copies


def wait_all(copies):
    for copy in copies:
        copy.wait()


def pack_kernel(
    boxes,
    cap,
    adj_hbm,
    kap_hbm,
    box_hbm,
    cell_hbm,
    frac_hbm,
    dres_hbm,
    dobj_hbm,
    out_ref,
    mate_ref,
    other_ref,
    adj_ref,
    kap_ref,
    box_ref,
    cell_ref,
    frac_ref,
    dres_ref,
    dobj_ref,
    ranks_ref,
    sems,
):
    fields, planes, _, lanes = adj_hbm.shape
    rows = planes * lanes
    ends = (0, planes - 1)
    moves = [(box_hbm, box_ref), (dres_hbm, dres_ref), (adj_hbm, adj_ref)]
    moves += [(dobj_hbm, dobj_ref), (frac_hbm, frac_ref), (cell_hbm, cell_ref)]
    moves += [(kap_hbm.at[x], kap_ref.at[i]) for i, x in enumerate(ends)]
    copies = start_all(
        [pltpu.make_async_copy(src, dst, sems.at[i]) for i, (src, dst) in enumerate(moves)]
    )
    copies[0].wait()
    box = box_ref[...]

    chunks = rows // CHUNK
    names = lax.broadcasted_iota(jnp.int32, (boxes, CHUNK), 0)
    hot = [(box[:, j * CHUNK:(j + 1) * CHUNK] == names).astype(F32) for j in range(chunks)]
    earlier = (
        lax.broadcasted_iota(jnp.int32, (CHUNK, CHUNK), 0)
        < lax.broadcasted_iota(jnp.int32, (CHUNK, CHUNK), 1)
    ).astype(F32).astype(BF16)
    counts = lax.dot_general(
        jnp.concatenate(hot, 0).astype(BF16), earlier, NN, preferred_element_type=F32
    )
    offset = jnp.zeros((boxes, 1), F32)
    for j in range(chunks):
        here = counts[j * boxes:(j + 1) * boxes]
        ranks_ref[:, j * CHUNK:(j + 1) * CHUNK] = jnp.sum(
            hot[j] * (here + offset), axis=0, keepdims=True
        )
        offset = offset + here[:, CHUNK - 1:] + hot[j][:, CHUNK - 1:]

    wait_all(copies[1:])
    even = on_even()
    for f in range(fields + 1):
        first = adj_ref[f, 0] if f < fields else kap_ref[0]
        last = adj_ref[f, planes - 1] if f < fields else kap_ref[1]
        mate_ref[f] = jnp.where(even, last, first)
        other_ref[f] = jnp.where(even, first, last)

    total = jnp.zeros((boxes * 16, cap), F32)
    slots = lax.broadcasted_iota(jnp.int32, (cap, CHUNK), 0).astype(F32)
    per = CHUNK // lanes
    for j in range(chunks):
        part = slice(j * CHUNK, (j + 1) * CHUNK)
        acc = dobj_ref[:, part]
        for k in range(fields):
            psi = jnp.concatenate(
                [adj_ref[k, x, 0:1, :] for x in range(j * per, (j + 1) * per)], 1
            )
            acc = acc - dres_ref[k, :, part] * psi
        values = jnp.concatenate(
            [acc, frac_ref[:, part], cell_ref[:, part].astype(F32), jnp.zeros((1, CHUNK), F32)], 0
        )
        hi = values.astype(BF16).astype(F32)
        both = jnp.concatenate([hi, values - hi], 0)
        mine = box[:, part]
        lhs = jnp.concatenate(
            [jnp.where(mine == b, both, 0.0) for b in range(boxes)], 0
        ).astype(BF16)
        rhs = (slots == ranks_ref[:, part]).astype(F32).astype(BF16)
        total = total + lax.dot_general(lhs, rhs, NT, preferred_element_type=F32)
    for b in range(boxes):
        out_ref[b] = total[b * 16:b * 16 + 8] + total[b * 16 + 8:b * 16 + 16]


def plane_residual(psi, kap, below, above, jac, face, src, conv):
    fields = len(psi)
    rows, lanes = kap.shape
    row = lax.broadcasted_iota(jnp.int32, (rows, lanes), 0)
    lane = lax.broadcasted_iota(jnp.int32, (rows, lanes), 1)
    masks = ((row < rows - 1, row > 0), (lane < lanes - 1, lane > 0))

    def sides(value, dim):
        size = value.shape[dim]
        up = jnp.where(masks[dim][0], pltpu.roll(value, size - 1, dim), 0.0)
        down = jnp.where(masks[dim][1], pltpu.roll(value, 1, dim), 0.0)
        return up, down

    centre = list(psi) + [kap]
    result = []
    for f in range(fields):
        total = jac(0, f) * psi[0]
        for k in range(1, fields):
            total = total + jac(k, f) * psi[k]
        result.append(total - src(f))
    spread = None
    for d in range(3):
        pair = list(zip(above, below)) if d == 0 else [sides(v, d - 1) for v in centre]
        scale = 0.5 * face(d)
        diff = [scale * (pair[k][0] - pair[k][1]) for k in range(fields)]
        up = 0.5 * (kap + pair[fields][0])
        down = 0.5 * (kap + pair[fields][1])
        spread = up + down if spread is None else spread + up + down
        for f in range(fields):
            total = result[f]
            for k in range(fields):
                total = total + conv[k, d, f] * diff[k]
            result[f] = total - up * pair[f][0] - down * pair[f][1]
    return [result[f] + spread * psi[f] for f in range(fields)]


def inner_kernel(
    adj_hbm,
    jac_hbm,
    conv_hbm,
    face_hbm,
    kap_hbm,
    src_hbm,
    after_hbm,
    out_hbm,
    adj_ref,
    jac_ref,
    conv_ref,
    face_ref,
    kap_ref,
    src_ref,
    out_ref,
    sems,
    out_sems,
):
    fields, planes, _, _ = adj_hbm.shape
    steps = 4
    cuts = [1 + (planes - 2) * i // steps for i in range(steps + 1)]
    pieces = [slice(a, b) for a, b in zip(cuts[:-1], cuts[1:])]
    moves = [(adj_hbm, adj_ref), (kap_hbm, kap_ref), (conv_hbm, conv_ref)]
    for p in pieces:
        moves.append((jac_hbm.at[:, :, p], jac_ref.at[:, :, p]))
        moves.append((src_hbm.at[:, p], src_ref.at[:, p]))
        moves.append((face_hbm.at[:, p], face_ref.at[:, p]))
    copies = start_all(
        [pltpu.make_async_copy(src, dst, sems.at[i]) for i, (src, dst) in enumerate(moves)]
    )
    wait_all(copies[:3])
    sent = []
    for i, p in enumerate(pieces):
        wait_all(copies[3 + 3 * i:6 + 3 * i])
        for x in range(p.start, p.stop):
            def at(y):
                return [adj_ref[f, y] for f in range(fields)] + [kap_ref[y]]

            here = at(x)
            planes_of = plane_residual(
                here[:fields],
                here[fields],
                at(x - 1),
                at(x + 1),
                lambda k, f: jac_ref[k, f, x],
                lambda d: face_ref[d, x],
                lambda f: src_ref[f, x],
                conv_ref,
            )
            for f in range(fields):
                out_ref[f, x] = planes_of[f]
        copy = pltpu.make_async_copy(out_ref.at[:, p], out_hbm.at[:, p], out_sems.at[i])
        copy.start()
        sent.append(copy)
    wait_all(sent)


def sum_kernel(
    got_ref,
    adj_hbm,
    jac_hbm,
    conv_hbm,
    face_hbm,
    kap_hbm,
    src_hbm,
    mate_ref,
    other_ref,
    part_hbm,
    out_ref,
    res_hbm,
    adj_ref,
    jac_ref,
    conv_ref,
    face_ref,
    kap_ref,
    src_ref,
    res_ref,
    sems,
    out_sems,
):
    del part_hbm
    fields, planes, _, _ = adj_hbm.shape
    ends = (0, planes - 1)
    moves = [(conv_hbm, conv_ref)]
    for i, x in enumerate(ends):
        near = pl.ds(0 if i == 0 else planes - 2, 2)
        moves.append((adj_hbm.at[:, near], adj_ref.at[i]))
        moves.append((kap_hbm.at[near], kap_ref.at[i]))
        moves.append((jac_hbm.at[:, :, x], jac_ref.at[i]))
        moves.append((src_hbm.at[:, x], src_ref.at[i]))
        moves.append((face_hbm.at[:, x], face_ref.at[i]))
    copies = start_all(
        [pltpu.make_async_copy(src, dst, sems.at[i]) for i, (src, dst) in enumerate(moves)]
    )

    sources, _, cap = got_ref.shape
    inner = LAT - 1
    points = lax.broadcasted_iota(jnp.int32, (LAT, cap), 0).astype(F32)
    both = jnp.zeros((6 * LAT, LAT * LAT), F32)
    for s in range(sources):
        block = got_ref[s]
        cell = block[6:7]
        first = jnp.floor((cell + 0.5) * (1.0 / (inner * inner)))
        rest = cell - first * (inner * inner)
        second = jnp.floor((rest + 0.5) * (1.0 / inner))
        third = rest - second * inner
        tent = []
        for d, low in enumerate((first, second, third)):
            u = block[3 + d:4 + d]
            tent.append(
                jnp.where(points == low, 1.0 - u, 0.0) + jnp.where(points == low + 1.0, u, 0.0)
            )
        left = jnp.concatenate([tent[0] * block[c:c + 1] for c in range(3)], 0)
        right = jnp.concatenate([tent[1][b:b + 1] * tent[2] for b in range(LAT)], 0)
        left_hi, left_lo = split_two(left)
        right_hi, right_lo = split_two(right)
        lhs = jnp.concatenate([left_hi, left_lo], 0)
        both = both + lax.dot_general(lhs, right_hi, NT, preferred_element_type=F32)
        both = both + lax.dot_general(lhs, right_lo, NT, preferred_element_type=F32)

    wait_all(copies)
    even = on_even()
    sent = []
    for i, x in enumerate(ends):
        pair = [[adj_ref[i, f, j] for f in range(fields)] + [kap_ref[i, j]] for j in (0, 1)]
        beyond = [
            jnp.where(even == (i == 0), other_ref[f], mate_ref[f]) for f in range(fields + 1)
        ]
        here = pair[i]
        planes_of = plane_residual(
            here[:fields],
            here[fields],
            beyond if i == 0 else pair[0],
            pair[1] if i == 0 else beyond,
            lambda k, f: jac_ref[i, k, f],
            lambda d: face_ref[i, d],
            lambda f: src_ref[i, f],
            conv_ref,
        )
        for f in range(fields):
            res_ref[i, f] = planes_of[f]
        copy = pltpu.make_async_copy(res_ref.at[i], res_hbm.at[:, x], out_sems.at[i])
        copy.start()
        sent.append(copy)
    result = both[:3 * LAT] + both[3 * LAT:]
    for c in range(3):
        for a in range(LAT):
            out_ref[c:c + 1, a * LAT * LAT:(a + 1) * LAT * LAT] = result[c * LAT + a:c * LAT + a + 1]
    wait_all(sent)


def local(
    adjoint,
    jac_diag,
    conv_mats,
    face_scale,
    kappa,
    source,
    box_of_row,
    lattice_cell,
    lattice_frac,
    dres_dx,
    dobj_dx,
):
    boxes = lax.axis_size("blk")
    rows = box_of_row.shape[0]
    cap = 2 * rows // boxes
    fields, planes = adjoint.shape[:2]
    plane = adjoint.shape[2:]
    vmem = pl.BlockSpec(memory_space=pltpu.VMEM)
    hbm = pl.BlockSpec(memory_space=pltpu.HBM)
    params = pltpu.CompilerParams(vmem_limit_bytes=SMALL)
    conv = conv_mats.transpose(1, 0, 2)
    box_row = box_of_row.reshape(1, rows)
    cell_row = lattice_cell.reshape(1, rows)
    box_row, cell_row, conv, adjoint, jac_diag, face_scale, kappa, source = stay(
        box_row, cell_row, conv, adjoint, jac_diag, face_scale, kappa, source
    )
    lattice_frac, dres_dx, dobj_dx = stay(lattice_frac, dres_dx, dobj_dx)

    def shape(*dims):
        return jax.ShapeDtypeStruct(dims, F32)

    packed, to_mate, to_other = pl.pallas_call(
        functools.partial(pack_kernel, boxes, cap),
        out_shape=(shape(boxes, 8, cap), shape(fields + 1, *plane), shape(fields + 1, *plane)),
        in_specs=[hbm] * 7,
        out_specs=(vmem, vmem, vmem),
        scratch_shapes=[
            pltpu.VMEM(adjoint.shape, F32),
            pltpu.VMEM((2,) + plane, F32),
            pltpu.VMEM((1, rows), jnp.int32),
            pltpu.VMEM((1, rows), jnp.int32),
            pltpu.VMEM(lattice_frac.shape, F32),
            pltpu.VMEM(dres_dx.shape, F32),
            pltpu.VMEM(dobj_dx.shape, F32),
            pltpu.VMEM((1, rows), F32),
            pltpu.SemaphoreType.DMA((8,)),
        ],
        compiler_params=params,
        name="pack_rows",
    )(adjoint, kappa, box_row, cell_row, lattice_frac, dres_dx, dobj_dx)
    got = lax.all_to_all(packed, "blk", 0, 0, tiled=True)

    pairs = [(i, i + 1) for i in range(boxes - 1)]
    both_ways = [[p for i, j in pairs if i % 2 == turn for p in ((i, j), (j, i))] for turn in (0, 1)]
    mate = lax.ppermute(to_mate, "blk", both_ways[0])
    other = lax.ppermute(to_other, "blk", both_ways[1])

    inner = pl.pallas_call(
        inner_kernel,
        out_shape=shape(*adjoint.shape),
        in_specs=[hbm] * 6 + [pl.BlockSpec(memory_space=pl.ANY)],
        out_specs=hbm,
        scratch_shapes=[
            pltpu.VMEM(adjoint.shape, F32),
            pltpu.VMEM(jac_diag.shape, F32),
            pltpu.SMEM(conv.shape, F32),
            pltpu.VMEM(face_scale.shape, F32),
            pltpu.VMEM(kappa.shape, F32),
            pltpu.VMEM(source.shape, F32),
            pltpu.VMEM(adjoint.shape, F32),
            pltpu.SemaphoreType.DMA((15,)),
            pltpu.SemaphoreType.DMA((4,)),
        ],
        compiler_params=params,
        name="sweep_inner",
    )(adjoint, jac_diag, conv, face_scale, kappa, source, to_mate)

    box_sens, residual = pl.pallas_call(
        sum_kernel,
        out_shape=(shape(3, LAT**3), shape(*adjoint.shape)),
        in_specs=[vmem] + [hbm] * 6 + [vmem, vmem, hbm],
        out_specs=(vmem, hbm),
        scratch_shapes=[
            pltpu.VMEM((2, fields, 2) + plane, F32),
            pltpu.VMEM((2, fields, fields) + plane, F32),
            pltpu.SMEM(conv.shape, F32),
            pltpu.VMEM((2, 3) + plane, F32),
            pltpu.VMEM((2, 2) + plane, F32),
            pltpu.VMEM((2, fields) + plane, F32),
            pltpu.VMEM((2, fields) + plane, F32),
            pltpu.SemaphoreType.DMA((11,)),
            pltpu.SemaphoreType.DMA((2,)),
        ],
        input_output_aliases={9: 1},
        compiler_params=params,
        name="sum_rows",
    )(got, adjoint, jac_diag, conv, face_scale, kappa, source, mate, other, inner)
    return residual, box_sens


def solution(mesh):
    in_specs = (
        P("group", "blk", None, None),
        P("group", None, "blk", None, None),
        P(),
        P("group", "blk", None, None),
        P(("group", "blk"), None, None),
        P("group", "blk", None, None),
        P(("group", "blk"), None),
        P(("group", "blk")),
        P(None, ("group", "blk")),
        P(None, None, ("group", "blk")),
        P(None, ("group", "blk")),
    )
    out_specs = (P("group", "blk", None, None), P("group", "blk"))
    return jax.shard_map(local, mesh=mesh, in_specs=in_specs, out_specs=out_specs, check_vma=False)
```

```python
import functools

import jax
import jax.numpy as jnp
from jax import lax
from jax.experimental import pallas as pl
from jax.experimental.pallas import tpu as pltpu
from jax.sharding import PartitionSpec as P

LAT = 16
CHUNK = 256
SMALL = 12 * 2**20
F32 = jnp.float32
BF16 = jnp.bfloat16
NT = (((1,), (1,)), ((), ()))
NN = (((1,), (0,)), ((), ()))


def split_two(x):
    hi = x.astype(BF16)
    lo = (x - hi.astype(F32)).astype(BF16)
    return hi, lo


def on_even():
    return lax.axis_index("blk") % 2 == 0


def stay(*arrays):
    return [pltpu.with_memory_space_constraint(a, pltpu.HBM) for a in arrays]


def start_all(copies):
    for copy in copies:
        copy.start()
    return copies


def wait_all(copies):
    for copy in copies:
        copy.wait()


def pack_kernel(
    boxes,
    cap,
    adj_hbm,
    kap_hbm,
    box_hbm,
    cell_hbm,
    frac_hbm,
    dres_hbm,
    dobj_hbm,
    own_ref,
    give_ref,
    mate_ref,
    other_ref,
    adj_ref,
    kap_ref,
    box_ref,
    cell_ref,
    frac_ref,
    dres_ref,
    dobj_ref,
    ranks_ref,
    sems,
):
    fields, planes, _, lanes = adj_hbm.shape
    rows = planes * lanes
    ends = (0, planes - 1)
    moves = [(box_hbm, box_ref), (dres_hbm, dres_ref), (adj_hbm, adj_ref)]
    moves += [(dobj_hbm, dobj_ref), (frac_hbm, frac_ref), (cell_hbm, cell_ref)]
    moves += [(kap_hbm.at[x], kap_ref.at[i]) for i, x in enumerate(ends)]
    copies = start_all(
        [pltpu.make_async_copy(src, dst, sems.at[i]) for i, (src, dst) in enumerate(moves)]
    )
    copies[0].wait()
    box = box_ref[...]

    chunks = rows // CHUNK
    names = lax.broadcasted_iota(jnp.int32, (boxes, CHUNK), 0)
    hot = [(box[:, j * CHUNK:(j + 1) * CHUNK] == names).astype(F32) for j in range(chunks)]
    earlier = (
        lax.broadcasted_iota(jnp.int32, (CHUNK, CHUNK), 0)
        < lax.broadcasted_iota(jnp.int32, (CHUNK, CHUNK), 1)
    ).astype(F32).astype(BF16)
    counts = lax.dot_general(
        jnp.concatenate(hot, 0).astype(BF16), earlier, NN, preferred_element_type=F32
    )
    offset = jnp.zeros((boxes, 1), F32)
    for j in range(chunks):
        here = counts[j * boxes:(j + 1) * boxes]
        ranks_ref[:, j * CHUNK:(j + 1) * CHUNK] = jnp.sum(
            hot[j] * (here + offset), axis=0, keepdims=True
        )
        offset = offset + here[:, CHUNK - 1:] + hot[j][:, CHUNK - 1:]

    wait_all(copies[1:])
    even = on_even()
    core = lax.axis_index("blk") % 2
    order = [2 * j + core for j in range(boxes // 2)] + [2 * j + 1 - core for j in range(boxes // 2)]
    for f in range(fields + 1):
        first = adj_ref[f, 0] if f < fields else kap_ref[0]
        last = adj_ref[f, planes - 1] if f < fields else kap_ref[1]
        mate_ref[f] = jnp.where(even, last, first)
        other_ref[f] = jnp.where(even, first, last)

    total = jnp.zeros((boxes * 16, cap), F32)
    slots = lax.broadcasted_iota(jnp.int32, (cap, CHUNK), 0).astype(F32)
    per = CHUNK // lanes
    for j in range(chunks):
        part = slice(j * CHUNK, (j + 1) * CHUNK)
        acc = dobj_ref[:, part]
        for k in range(fields):
            psi = jnp.concatenate(
                [adj_ref[k, x, 0:1, :] for x in range(j * per, (j + 1) * per)], 1
            )
            acc = acc - dres_ref[k, :, part] * psi
        values = jnp.concatenate(
            [acc, frac_ref[:, part], cell_ref[:, part].astype(F32), jnp.zeros((1, CHUNK), F32)], 0
        )
        hi = values.astype(BF16).astype(F32)
        both = jnp.concatenate([hi, values - hi], 0)
        mine = box[:, part]
        lhs = jnp.concatenate(
            [jnp.where(mine == b, both, 0.0) for b in order], 0
        ).astype(BF16)
        rhs = (slots == ranks_ref[:, part]).astype(F32).astype(BF16)
        total = total + lax.dot_general(lhs, rhs, NT, preferred_element_type=F32)
    for b in range(boxes):
        target = own_ref if b < boxes // 2 else give_ref
        target[b % (boxes // 2)] = total[b * 16:b * 16 + 8] + total[b * 16 + 8:b * 16 + 16]


def merge_kernel(own_ref, got_ref, out_ref):
    for j in range(own_ref.shape[0]):
        out_ref[j, 0] = own_ref[j]
        out_ref[j, 1] = got_ref[j]


def plane_residual(psi, kap, below, above, jac, face, src, conv):
    fields = len(psi)
    rows, lanes = kap.shape
    row = lax.broadcasted_iota(jnp.int32, (rows, lanes), 0)
    lane = lax.broadcasted_iota(jnp.int32, (rows, lanes), 1)
    masks = ((row < rows - 1, row > 0), (lane < lanes - 1, lane > 0))

    def sides(value, dim):
        size = value.shape[dim]
        up = jnp.where(masks[dim][0], pltpu.roll(value, size - 1, dim), 0.0)
        down = jnp.where(masks[dim][1], pltpu.roll(value, 1, dim), 0.0)
        return up, down

    centre = list(psi) + [kap]
    result = []
    for f in range(fields):
        total = jac(0, f) * psi[0]
        for k in range(1, fields):
            total = total + jac(k, f) * psi[k]
        result.append(total - src(f))
    spread = None
    for d in range(3):
        pair = list(zip(above, below)) if d == 0 else [sides(v, d - 1) for v in centre]
        scale = 0.5 * face(d)
        diff = [scale * (pair[k][0] - pair[k][1]) for k in range(fields)]
        up = 0.5 * (kap + pair[fields][0])
        down = 0.5 * (kap + pair[fields][1])
        spread = up + down if spread is None else spread + up + down
        for f in range(fields):
            total = result[f]
            for k in range(fields):
                total = total + conv[k, d, f] * diff[k]
            result[f] = total - up * pair[f][0] - down * pair[f][1]
    return [result[f] + spread * psi[f] for f in range(fields)]


def inner_kernel(
    adj_hbm,
    jac_hbm,
    conv_hbm,
    face_hbm,
    kap_hbm,
    src_hbm,
    after_hbm,
    out_hbm,
    adj_ref,
    jac_ref,
    conv_ref,
    face_ref,
    kap_ref,
    src_ref,
    out_ref,
    sems,
    out_sems,
):
    fields, planes, _, _ = adj_hbm.shape
    steps = 4
    cuts = [1 + (planes - 2) * i // steps for i in range(steps + 1)]
    pieces = [slice(a, b) for a, b in zip(cuts[:-1], cuts[1:])]
    moves = [(adj_hbm, adj_ref), (kap_hbm, kap_ref), (conv_hbm, conv_ref)]
    for p in pieces:
        moves.append((jac_hbm.at[:, :, p], jac_ref.at[:, :, p]))
        moves.append((src_hbm.at[:, p], src_ref.at[:, p]))
        moves.append((face_hbm.at[:, p], face_ref.at[:, p]))
    copies = start_all(
        [pltpu.make_async_copy(src, dst, sems.at[i]) for i, (src, dst) in enumerate(moves)]
    )
    wait_all(copies[:3])
    sent = []
    for i, p in enumerate(pieces):
        wait_all(copies[3 + 3 * i:6 + 3 * i])
        for x in range(p.start, p.stop):
            def at(y):
                return [adj_ref[f, y] for f in range(fields)] + [kap_ref[y]]

            here = at(x)
            planes_of = plane_residual(
                here[:fields],
                here[fields],
                at(x - 1),
                at(x + 1),
                lambda k, f: jac_ref[k, f, x],
                lambda d: face_ref[d, x],
                lambda f: src_ref[f, x],
                conv_ref,
            )
            for f in range(fields):
                out_ref[f, x] = planes_of[f]
        copy = pltpu.make_async_copy(out_ref.at[:, p], out_hbm.at[:, p], out_sems.at[i])
        copy.start()
        sent.append(copy)
    wait_all(sent)


def sum_kernel(
    got_ref,
    adj_hbm,
    jac_hbm,
    conv_hbm,
    face_hbm,
    kap_hbm,
    src_hbm,
    mate_ref,
    other_ref,
    part_hbm,
    out_ref,
    res_hbm,
    adj_ref,
    jac_ref,
    conv_ref,
    face_ref,
    kap_ref,
    src_ref,
    res_ref,
    sems,
    out_sems,
):
    del part_hbm
    fields, planes, _, _ = adj_hbm.shape
    ends = (0, planes - 1)
    moves = [(conv_hbm, conv_ref)]
    for i, x in enumerate(ends):
        near = pl.ds(0 if i == 0 else planes - 2, 2)
        moves.append((adj_hbm.at[:, near], adj_ref.at[i]))
        moves.append((kap_hbm.at[near], kap_ref.at[i]))
        moves.append((jac_hbm.at[:, :, x], jac_ref.at[i]))
        moves.append((src_hbm.at[:, x], src_ref.at[i]))
        moves.append((face_hbm.at[:, x], face_ref.at[i]))
    copies = start_all(
        [pltpu.make_async_copy(src, dst, sems.at[i]) for i, (src, dst) in enumerate(moves)]
    )

    sources, _, cap = got_ref.shape
    inner = LAT - 1
    points = lax.broadcasted_iota(jnp.int32, (LAT, cap), 0).astype(F32)
    both = jnp.zeros((6 * LAT, LAT * LAT), F32)
    for s in range(sources):
        block = got_ref[s]
        cell = block[6:7]
        first = jnp.floor((cell + 0.5) * (1.0 / (inner * inner)))
        rest = cell - first * (inner * inner)
        second = jnp.floor((rest + 0.5) * (1.0 / inner))
        third = rest - second * inner
        tent = []
        for d, low in enumerate((first, second, third)):
            u = block[3 + d:4 + d]
            tent.append(
                jnp.where(points == low, 1.0 - u, 0.0) + jnp.where(points == low + 1.0, u, 0.0)
            )
        left = jnp.concatenate([tent[0] * block[c:c + 1] for c in range(3)], 0)
        right = jnp.concatenate([tent[1][b:b + 1] * tent[2] for b in range(LAT)], 0)
        left_hi, left_lo = split_two(left)
        right_hi, right_lo = split_two(right)
        lhs = jnp.concatenate([left_hi, left_lo], 0)
        both = both + lax.dot_general(lhs, right_hi, NT, preferred_element_type=F32)
        both = both + lax.dot_general(lhs, right_lo, NT, preferred_element_type=F32)

    wait_all(copies)
    even = on_even()
    sent = []
    for i, x in enumerate(ends):
        pair = [[adj_ref[i, f, j] for f in range(fields)] + [kap_ref[i, j]] for j in (0, 1)]
        beyond = [
            jnp.where(even == (i == 0), other_ref[f], mate_ref[f]) for f in range(fields + 1)
        ]
        here = pair[i]
        planes_of = plane_residual(
            here[:fields],
            here[fields],
            beyond if i == 0 else pair[0],
            pair[1] if i == 0 else beyond,
            lambda k, f: jac_ref[i, k, f],
            lambda d: face_ref[i, d],
            lambda f: src_ref[i, f],
            conv_ref,
        )
        for f in range(fields):
            res_ref[i, f] = planes_of[f]
        copy = pltpu.make_async_copy(res_ref.at[i], res_hbm.at[:, x], out_sems.at[i])
        copy.start()
        sent.append(copy)
    result = both[:3 * LAT] + both[3 * LAT:]
    for c in range(3):
        for a in range(LAT):
            out_ref[c:c + 1, a * LAT * LAT:(a + 1) * LAT * LAT] = result[c * LAT + a:c * LAT + a + 1]
    wait_all(sent)


def local(
    adjoint,
    jac_diag,
    conv_mats,
    face_scale,
    kappa,
    source,
    box_of_row,
    lattice_cell,
    lattice_frac,
    dres_dx,
    dobj_dx,
):
    boxes = lax.axis_size("blk")
    rows = box_of_row.shape[0]
    cap = 2 * rows // boxes
    fields, planes = adjoint.shape[:2]
    plane = adjoint.shape[2:]
    vmem = pl.BlockSpec(memory_space=pltpu.VMEM)
    hbm = pl.BlockSpec(memory_space=pltpu.HBM)
    params = pltpu.CompilerParams(vmem_limit_bytes=SMALL)
    conv = conv_mats.transpose(1, 0, 2)
    box_row = box_of_row.reshape(1, rows)
    cell_row = lattice_cell.reshape(1, rows)
    box_row, cell_row, conv, adjoint, jac_diag, face_scale, kappa, source = stay(
        box_row, cell_row, conv, adjoint, jac_diag, face_scale, kappa, source
    )
    lattice_frac, dres_dx, dobj_dx = stay(lattice_frac, dres_dx, dobj_dx)

    def shape(*dims):
        return jax.ShapeDtypeStruct(dims, F32)

    half = boxes // 2
    own, give, to_mate, to_other = pl.pallas_call(
        functools.partial(pack_kernel, boxes, cap),
        out_shape=(
            shape(half, 8, cap),
            shape(half, 8, cap),
            shape(fields + 1, *plane),
            shape(fields + 1, *plane),
        ),
        in_specs=[hbm] * 7,
        out_specs=(vmem,) * 4,
        scratch_shapes=[
            pltpu.VMEM(adjoint.shape, F32),
            pltpu.VMEM((2,) + plane, F32),
            pltpu.VMEM((1, rows), jnp.int32),
            pltpu.VMEM((1, rows), jnp.int32),
            pltpu.VMEM(lattice_frac.shape, F32),
            pltpu.VMEM(dres_dx.shape, F32),
            pltpu.VMEM(dobj_dx.shape, F32),
            pltpu.VMEM((1, rows), F32),
            pltpu.SemaphoreType.DMA((8,)),
        ],
        compiler_params=params,
        name="pack_rows",
    )(adjoint, kappa, box_row, cell_row, lattice_frac, dres_dx, dobj_dx)
    pairs = [(i, i + 1) for i in range(boxes - 1)]
    both_ways = [[p for i, j in pairs if i % 2 == turn for p in ((i, j), (j, i))] for turn in (0, 1)]
    taken = lax.ppermute(give, "blk", both_ways[0])
    mate = lax.ppermute(to_mate, "blk", both_ways[0])
    other = lax.ppermute(to_other, "blk", both_ways[1])

    merged = pl.pallas_call(
        merge_kernel,
        out_shape=shape(half, 2, 8, cap),
        in_specs=[vmem, vmem],
        out_specs=vmem,
        compiler_params=params,
        name="merge_rows",
    )(own, taken)
    same_core = [list(range(c, boxes, 2)) for c in (0, 1)]
    got = lax.all_to_all(merged, "blk", 0, 0, axis_index_groups=same_core, tiled=True)
    got = got.reshape(boxes, 8, cap)

    inner = pl.pallas_call(
        inner_kernel,
        out_shape=shape(*adjoint.shape),
        in_specs=[hbm] * 6 + [pl.BlockSpec(memory_space=pl.ANY)],
        out_specs=hbm,
        scratch_shapes=[
            pltpu.VMEM(adjoint.shape, F32),
            pltpu.VMEM(jac_diag.shape, F32),
            pltpu.SMEM(conv.shape, F32),
            pltpu.VMEM(face_scale.shape, F32),
            pltpu.VMEM(kappa.shape, F32),
            pltpu.VMEM(source.shape, F32),
            pltpu.VMEM(adjoint.shape, F32),
            pltpu.SemaphoreType.DMA((15,)),
            pltpu.SemaphoreType.DMA((4,)),
        ],
        compiler_params=params,
        name="sweep_inner",
    )(adjoint, jac_diag, conv, face_scale, kappa, source, merged)

    box_sens, residual = pl.pallas_call(
        sum_kernel,
        out_shape=(shape(3, LAT**3), shape(*adjoint.shape)),
        in_specs=[vmem] + [hbm] * 6 + [vmem, vmem, hbm],
        out_specs=(vmem, hbm),
        scratch_shapes=[
            pltpu.VMEM((2, fields, 2) + plane, F32),
            pltpu.VMEM((2, fields, fields) + plane, F32),
            pltpu.SMEM(conv.shape, F32),
            pltpu.VMEM((2, 3) + plane, F32),
            pltpu.VMEM((2, 2) + plane, F32),
            pltpu.VMEM((2, fields) + plane, F32),
            pltpu.VMEM((2, fields) + plane, F32),
            pltpu.SemaphoreType.DMA((11,)),
            pltpu.SemaphoreType.DMA((2,)),
        ],
        input_output_aliases={9: 1},
        compiler_params=params,
        name="sum_rows",
    )(got, adjoint, jac_diag, conv, face_scale, kappa, source, mate, other, inner)
    return residual, box_sens


def solution(mesh):
    in_specs = (
        P("group", "blk", None, None),
        P("group", None, "blk", None, None),
        P(),
        P("group", "blk", None, None),
        P(("group", "blk"), None, None),
        P("group", "blk", None, None),
        P(("group", "blk"), None),
        P(("group", "blk")),
        P(None, ("group", "blk")),
        P(None, None, ("group", "blk")),
        P(None, ("group", "blk")),
    )
    out_specs = (P("group", "blk", None, None), P("group", "blk"))
    return jax.shard_map(local, mesh=mesh, in_specs=in_specs, out_specs=out_specs, check_vma=False)
```

```python
import functools

import jax
import jax.numpy as jnp
from jax import lax
from jax.experimental import pallas as pl
from jax.experimental.pallas import tpu as pltpu
from jax.sharding import PartitionSpec as P

LAT = 16
CHUNK = 256
SMALL = 12 * 2**20
F32 = jnp.float32
BF16 = jnp.bfloat16
NT = (((1,), (1,)), ((), ()))
NN = (((1,), (0,)), ((), ()))


def split_two(x):
    hi = x.astype(BF16)
    lo = (x - hi.astype(F32)).astype(BF16)
    return hi, lo


def on_even():
    return lax.axis_index("blk") % 2 == 0


def stay(*arrays):
    return [pltpu.with_memory_space_constraint(a, pltpu.HBM) for a in arrays]


def start_all(copies):
    for copy in copies:
        copy.start()
    return copies


def wait_all(copies):
    for copy in copies:
        copy.wait()


def halo_kernel(adj_hbm, kap_hbm, mate_ref, other_ref, sems):
    fields, planes = adj_hbm.shape[:2]
    even = (lax.axis_index("blk") + 1) % 2
    copies = []
    for i, (ref, x) in enumerate(
        ((mate_ref, even * (planes - 1)), (other_ref, (1 - even) * (planes - 1)))
    ):
        copies.append(
            pltpu.make_async_copy(adj_hbm.at[:, x], ref.at[pl.ds(0, fields)], sems.at[2 * i])
        )
        copies.append(pltpu.make_async_copy(kap_hbm.at[x], ref.at[fields], sems.at[2 * i + 1]))
    wait_all(start_all(copies))


def plane_residual(psi, kap, below, above, jac, face, src, conv):
    fields = len(psi)
    rows, lanes = kap.shape
    row = lax.broadcasted_iota(jnp.int32, (rows, lanes), 0)
    lane = lax.broadcasted_iota(jnp.int32, (rows, lanes), 1)
    masks = ((row < rows - 1, row > 0), (lane < lanes - 1, lane > 0))

    def sides(value, dim):
        size = value.shape[dim]
        up = jnp.where(masks[dim][0], pltpu.roll(value, size - 1, dim), 0.0)
        down = jnp.where(masks[dim][1], pltpu.roll(value, 1, dim), 0.0)
        return up, down

    centre = list(psi) + [kap]
    result = []
    for f in range(fields):
        total = jac(0, f) * psi[0]
        for k in range(1, fields):
            total = total + jac(k, f) * psi[k]
        result.append(total - src(f))
    spread = None
    for d in range(3):
        pair = list(zip(above, below)) if d == 0 else [sides(v, d - 1) for v in centre]
        scale = 0.5 * face(d)
        diff = [scale * (pair[k][0] - pair[k][1]) for k in range(fields)]
        up = 0.5 * (kap + pair[fields][0])
        down = 0.5 * (kap + pair[fields][1])
        spread = up + down if spread is None else spread + up + down
        for f in range(fields):
            total = result[f]
            for k in range(fields):
                total = total + conv[k, d, f] * diff[k]
            result[f] = total - up * pair[f][0] - down * pair[f][1]
    return [result[f] + spread * psi[f] for f in range(fields)]


def work_kernel(
    boxes,
    cap,
    adj_hbm,
    jac_hbm,
    conv_hbm,
    face_hbm,
    kap_hbm,
    src_hbm,
    box_hbm,
    cell_hbm,
    frac_hbm,
    dres_hbm,
    dobj_hbm,
    mate_hbm,
    other_hbm,
    out_ref,
    res_hbm,
    adj_ref,
    jac_ref,
    conv_ref,
    face_ref,
    kap_ref,
    src_ref,
    box_ref,
    cell_ref,
    frac_ref,
    dres_ref,
    dobj_ref,
    mate_ref,
    other_ref,
    ranks_ref,
    res_ref,
    sems,
    out_sems,
):
    fields, planes, _, lanes = adj_hbm.shape
    rows = planes * lanes
    moves = [(box_hbm, box_ref), (dres_hbm, dres_ref), (adj_hbm, adj_ref)]
    moves += [(dobj_hbm, dobj_ref), (frac_hbm, frac_ref), (cell_hbm, cell_ref)]
    moves += [(kap_hbm, kap_ref), (conv_hbm, conv_ref), (jac_hbm, jac_ref)]
    moves += [(src_hbm, src_ref), (face_hbm, face_ref), (mate_hbm, mate_ref), (other_hbm, other_ref)]
    copies = start_all(
        [pltpu.make_async_copy(src, dst, sems.at[i]) for i, (src, dst) in enumerate(moves)]
    )
    copies[0].wait()
    box = box_ref[...]

    chunks = rows // CHUNK
    names = lax.broadcasted_iota(jnp.int32, (boxes, CHUNK), 0)
    hot = [(box[:, j * CHUNK:(j + 1) * CHUNK] == names).astype(F32) for j in range(chunks)]
    earlier = (
        lax.broadcasted_iota(jnp.int32, (CHUNK, CHUNK), 0)
        < lax.broadcasted_iota(jnp.int32, (CHUNK, CHUNK), 1)
    ).astype(F32).astype(BF16)
    counts = lax.dot_general(
        jnp.concatenate(hot, 0).astype(BF16), earlier, NN, preferred_element_type=F32
    )
    offset = jnp.zeros((boxes, 1), F32)
    for j in range(chunks):
        here = counts[j * boxes:(j + 1) * boxes]
        ranks_ref[:, j * CHUNK:(j + 1) * CHUNK] = jnp.sum(
            hot[j] * (here + offset), axis=0, keepdims=True
        )
        offset = offset + here[:, CHUNK - 1:] + hot[j][:, CHUNK - 1:]

    wait_all(copies[1:6])
    total = jnp.zeros((boxes * 16, cap), F32)
    slots = lax.broadcasted_iota(jnp.int32, (cap, CHUNK), 0).astype(F32)
    per = CHUNK // lanes
    for j in range(chunks):
        part = slice(j * CHUNK, (j + 1) * CHUNK)
        acc = dobj_ref[:, part]
        for k in range(fields):
            psi = jnp.concatenate(
                [adj_ref[k, x, 0:1, :] for x in range(j * per, (j + 1) * per)], 1
            )
            acc = acc - dres_ref[k, :, part] * psi
        values = jnp.concatenate(
            [acc, frac_ref[:, part], cell_ref[:, part].astype(F32), jnp.zeros((1, CHUNK), F32)], 0
        )
        hi = values.astype(BF16).astype(F32)
        both = jnp.concatenate([hi, values - hi], 0)
        mine = box[:, part]
        lhs = jnp.concatenate(
            [jnp.where(mine == b, both, 0.0) for b in range(boxes)], 0
        ).astype(BF16)
        rhs = (slots == ranks_ref[:, part]).astype(F32).astype(BF16)
        total = total + lax.dot_general(lhs, rhs, NT, preferred_element_type=F32)
    for b in range(boxes):
        out_ref[b] = total[b * 16:b * 16 + 8] + total[b * 16 + 8:b * 16 + 16]

    wait_all(copies[6:])
    even = on_even()
    sent = []
    steps = 4
    for i in range(steps):
        p = slice(planes * i // steps, planes * (i + 1) // steps)
        for x in range(p.start, p.stop):
            def at(y):
                if 0 <= y < planes:
                    return [adj_ref[f, y] for f in range(fields)] + [kap_ref[y]]
                return [
                    jnp.where(even == (y < 0), other_ref[f], mate_ref[f]) for f in range(fields + 1)
                ]

            here = at(x)
            planes_of = plane_residual(
                here[:fields],
                here[fields],
                at(x - 1),
                at(x + 1),
                lambda k, f: jac_ref[k, f, x],
                lambda d: face_ref[d, x],
                lambda f: src_ref[f, x],
                conv_ref,
            )
            for f in range(fields):
                res_ref[f, x] = planes_of[f]
        copy = pltpu.make_async_copy(res_ref.at[:, p], res_hbm.at[:, p], out_sems.at[i])
        copy.start()
        sent.append(copy)
    wait_all(sent)


def sum_kernel(got_ref, out_ref):
    sources, _, cap = got_ref.shape
    inner = LAT - 1
    points = lax.broadcasted_iota(jnp.int32, (LAT, cap), 0).astype(F32)
    both = jnp.zeros((6 * LAT, LAT * LAT), F32)
    for s in range(sources):
        block = got_ref[s]
        cell = block[6:7]
        first = jnp.floor((cell + 0.5) * (1.0 / (inner * inner)))
        rest = cell - first * (inner * inner)
        second = jnp.floor((rest + 0.5) * (1.0 / inner))
        third = rest - second * inner
        tent = []
        for d, low in enumerate((first, second, third)):
            u = block[3 + d:4 + d]
            tent.append(
                jnp.where(points == low, 1.0 - u, 0.0) + jnp.where(points == low + 1.0, u, 0.0)
            )
        left = jnp.concatenate([tent[0] * block[c:c + 1] for c in range(3)], 0)
        right = jnp.concatenate([tent[1][b:b + 1] * tent[2] for b in range(LAT)], 0)
        left_hi, left_lo = split_two(left)
        right_hi, right_lo = split_two(right)
        lhs = jnp.concatenate([left_hi, left_lo], 0)
        both = both + lax.dot_general(lhs, right_hi, NT, preferred_element_type=F32)
        both = both + lax.dot_general(lhs, right_lo, NT, preferred_element_type=F32)
    result = both[:3 * LAT] + both[3 * LAT:]
    for c in range(3):
        for a in range(LAT):
            out_ref[c:c + 1, a * LAT * LAT:(a + 1) * LAT * LAT] = result[c * LAT + a:c * LAT + a + 1]


def local(
    adjoint,
    jac_diag,
    conv_mats,
    face_scale,
    kappa,
    source,
    box_of_row,
    lattice_cell,
    lattice_frac,
    dres_dx,
    dobj_dx,
):
    boxes = lax.axis_size("blk")
    rows = box_of_row.shape[0]
    cap = 2 * rows // boxes
    fields, planes = adjoint.shape[:2]
    plane = adjoint.shape[2:]
    vmem = pl.BlockSpec(memory_space=pltpu.VMEM)
    hbm = pl.BlockSpec(memory_space=pltpu.HBM)
    params = pltpu.CompilerParams(vmem_limit_bytes=SMALL)
    conv = conv_mats.transpose(1, 0, 2)
    box_row = box_of_row.reshape(1, rows)
    cell_row = lattice_cell.reshape(1, rows)
    box_row, cell_row, conv, adjoint, jac_diag, face_scale, kappa, source = stay(
        box_row, cell_row, conv, adjoint, jac_diag, face_scale, kappa, source
    )
    lattice_frac, dres_dx, dobj_dx = stay(lattice_frac, dres_dx, dobj_dx)

    def shape(*dims):
        return jax.ShapeDtypeStruct(dims, F32)

    halo = (fields + 1,) + plane
    to_mate, to_other = pl.pallas_call(
        halo_kernel,
        out_shape=(shape(*halo), shape(*halo)),
        in_specs=[hbm, hbm],
        out_specs=(vmem, vmem),
        scratch_shapes=[pltpu.SemaphoreType.DMA((4,))],
        compiler_params=params,
        name="halo_planes",
    )(adjoint, kappa)
    pairs = [(i, i + 1) for i in range(boxes - 1)]
    both_ways = [[p for i, j in pairs if i % 2 == turn for p in ((i, j), (j, i))] for turn in (0, 1)]
    mate = lax.ppermute(to_mate, "blk", both_ways[0])
    other = lax.ppermute(to_other, "blk", both_ways[1])

    packed, residual = pl.pallas_call(
        functools.partial(work_kernel, boxes, cap),
        out_shape=(shape(boxes, 8, cap), shape(*adjoint.shape)),
        in_specs=[hbm] * 11 + [pl.BlockSpec(memory_space=pl.ANY)] * 2,
        out_specs=(vmem, hbm),
        scratch_shapes=[
            pltpu.VMEM(adjoint.shape, F32),
            pltpu.VMEM(jac_diag.shape, F32),
            pltpu.SMEM(conv.shape, F32),
            pltpu.VMEM(face_scale.shape, F32),
            pltpu.VMEM(kappa.shape, F32),
            pltpu.VMEM(source.shape, F32),
            pltpu.VMEM((1, rows), jnp.int32),
            pltpu.VMEM((1, rows), jnp.int32),
            pltpu.VMEM(lattice_frac.shape, F32),
            pltpu.VMEM(dres_dx.shape, F32),
            pltpu.VMEM(dobj_dx.shape, F32),
            pltpu.VMEM(halo, F32),
            pltpu.VMEM(halo, F32),
            pltpu.VMEM((1, rows), F32),
            pltpu.VMEM(adjoint.shape, F32),
            pltpu.SemaphoreType.DMA((13,)),
            pltpu.SemaphoreType.DMA((4,)),
        ],
        compiler_params=params,
        name="pack_and_sweep",
    )(
        adjoint,
        jac_diag,
        conv,
        face_scale,
        kappa,
        source,
        box_row,
        cell_row,
        lattice_frac,
        dres_dx,
        dobj_dx,
        mate,
        other,
    )
    got = lax.all_to_all(packed, "blk", 0, 0, tiled=True)

    box_sens = pl.pallas_call(
        sum_kernel,
        out_shape=shape(3, LAT**3),
        in_specs=[vmem],
        out_specs=vmem,
        compiler_params=params,
        name="sum_rows",
    )(got)
    return residual, box_sens


def solution(mesh):
    in_specs = (
        P("group", "blk", None, None),
        P("group", None, "blk", None, None),
        P(),
        P("group", "blk", None, None),
        P(("group", "blk"), None, None),
        P("group", "blk", None, None),
        P(("group", "blk"), None),
        P(("group", "blk")),
        P(None, ("group", "blk")),
        P(None, None, ("group", "blk")),
        P(None, ("group", "blk")),
    )
    out_specs = (P("group", "blk", None, None), P("group", "blk"))
    return jax.shard_map(local, mesh=mesh, in_specs=in_specs, out_specs=out_specs, check_vma=False)
```

```python
import functools

import jax
import jax.numpy as jnp
from jax import lax
from jax.experimental import pallas as pl
from jax.experimental.pallas import tpu as pltpu
from jax.sharding import PartitionSpec as P

LAT = 16
CHUNK = 256
SMALL = 12 * 2**20
F32 = jnp.float32
BF16 = jnp.bfloat16
NT = (((1,), (1,)), ((), ()))
NN = (((1,), (0,)), ((), ()))


def split_two(x):
    hi = x.astype(BF16)
    lo = (x - hi.astype(F32)).astype(BF16)
    return hi, lo


def on_even():
    return lax.axis_index("blk") % 2 == 0


def stay(*arrays):
    return [pltpu.with_memory_space_constraint(a, pltpu.HBM) for a in arrays]


def spread(count):
    quarter = count // 4
    order = []
    for k in range(quarter):
        order += [
            3 * quarter + k,
            (k + 2) % quarter,
            2 * quarter + (k + 3) % quarter,
            quarter + (k + 1) % quarter,
        ]
    return order


def start_all(copies):
    for copy in copies:
        copy.start()
    return copies


def wait_all(copies):
    for copy in copies:
        copy.wait()


def pack_kernel(
    boxes,
    cap,
    adj_hbm,
    kap_hbm,
    box_hbm,
    cell_hbm,
    frac_hbm,
    dres_hbm,
    dobj_hbm,
    out_ref,
    mate_ref,
    other_ref,
    adj_ref,
    kap_ref,
    box_ref,
    cell_ref,
    frac_ref,
    dres_ref,
    dobj_ref,
    ranks_ref,
    sems,
):
    fields, planes, _, lanes = adj_hbm.shape
    rows = planes * lanes
    ends = (0, planes - 1)
    moves = [(box_hbm, box_ref), (dres_hbm, dres_ref), (adj_hbm, adj_ref)]
    moves += [(dobj_hbm, dobj_ref), (frac_hbm, frac_ref), (cell_hbm, cell_ref)]
    moves += [(kap_hbm.at[x], kap_ref.at[i]) for i, x in enumerate(ends)]
    copies = start_all(
        [pltpu.make_async_copy(src, dst, sems.at[i]) for i, (src, dst) in enumerate(moves)]
    )
    copies[0].wait()
    box = box_ref[...]

    chunks = rows // CHUNK
    names = lax.broadcasted_iota(jnp.int32, (boxes, CHUNK), 0)
    hot = [(box[:, j * CHUNK:(j + 1) * CHUNK] == names).astype(F32) for j in range(chunks)]
    earlier = (
        lax.broadcasted_iota(jnp.int32, (CHUNK, CHUNK), 0)
        < lax.broadcasted_iota(jnp.int32, (CHUNK, CHUNK), 1)
    ).astype(F32).astype(BF16)
    counts = lax.dot_general(
        jnp.concatenate(hot, 0).astype(BF16), earlier, NN, preferred_element_type=F32
    )
    offset = jnp.zeros((boxes, 1), F32)
    for j in range(chunks):
        here = counts[j * boxes:(j + 1) * boxes]
        ranks_ref[:, j * CHUNK:(j + 1) * CHUNK] = jnp.sum(
            hot[j] * (here + offset), axis=0, keepdims=True
        )
        offset = offset + here[:, CHUNK - 1:] + hot[j][:, CHUNK - 1:]

    wait_all(copies[1:])
    even = on_even()
    for f in range(fields + 1):
        first = adj_ref[f, 0] if f < fields else kap_ref[0]
        last = adj_ref[f, planes - 1] if f < fields else kap_ref[1]
        mate_ref[f] = jnp.where(even, last, first)
        other_ref[f] = jnp.where(even, first, last)

    total = jnp.zeros((boxes * 16, cap), F32)
    slots = lax.broadcasted_iota(jnp.int32, (cap, CHUNK), 0).astype(F32)
    per = CHUNK // lanes
    for j in range(chunks):
        part = slice(j * CHUNK, (j + 1) * CHUNK)
        acc = dobj_ref[:, part]
        for k in range(fields):
            psi = jnp.concatenate(
                [adj_ref[k, x, 0:1, :] for x in range(j * per, (j + 1) * per)], 1
            )
            acc = acc - dres_ref[k, :, part] * psi
        values = jnp.concatenate(
            [acc, frac_ref[:, part], cell_ref[:, part].astype(F32), jnp.zeros((1, CHUNK), F32)], 0
        )
        hi = values.astype(BF16).astype(F32)
        both = jnp.concatenate([hi, values - hi], 0)
        mine = box[:, part]
        lhs = jnp.concatenate(
            [jnp.where(mine == b, both, 0.0) for b in spread(boxes)], 0
        ).astype(BF16)
        rhs = (slots == ranks_ref[:, part]).astype(F32).astype(BF16)
        total = total + lax.dot_general(lhs, rhs, NT, preferred_element_type=F32)
    for b in range(boxes):
        out_ref[b] = total[b * 16:b * 16 + 8] + total[b * 16 + 8:b * 16 + 16]


def plane_residual(psi, kap, below, above, jac, face, src, conv):
    fields = len(psi)
    rows, lanes = kap.shape
    row = lax.broadcasted_iota(jnp.int32, (rows, lanes), 0)
    lane = lax.broadcasted_iota(jnp.int32, (rows, lanes), 1)
    masks = ((row < rows - 1, row > 0), (lane < lanes - 1, lane > 0))

    def sides(value, dim):
        size = value.shape[dim]
        up = jnp.where(masks[dim][0], pltpu.roll(value, size - 1, dim), 0.0)
        down = jnp.where(masks[dim][1], pltpu.roll(value, 1, dim), 0.0)
        return up, down

    centre = list(psi) + [kap]
    result = []
    for f in range(fields):
        total = jac(0, f) * psi[0]
        for k in range(1, fields):
            total = total + jac(k, f) * psi[k]
        result.append(total - src(f))
    spread = None
    for d in range(3):
        pair = list(zip(above, below)) if d == 0 else [sides(v, d - 1) for v in centre]
        scale = 0.5 * face(d)
        diff = [scale * (pair[k][0] - pair[k][1]) for k in range(fields)]
        up = 0.5 * (kap + pair[fields][0])
        down = 0.5 * (kap + pair[fields][1])
        spread = up + down if spread is None else spread + up + down
        for f in range(fields):
            total = result[f]
            for k in range(fields):
                total = total + conv[k, d, f] * diff[k]
            result[f] = total - up * pair[f][0] - down * pair[f][1]
    return [result[f] + spread * psi[f] for f in range(fields)]


def inner_kernel(
    adj_hbm,
    jac_hbm,
    conv_hbm,
    face_hbm,
    kap_hbm,
    src_hbm,
    after_hbm,
    out_hbm,
    adj_ref,
    jac_ref,
    conv_ref,
    face_ref,
    kap_ref,
    src_ref,
    out_ref,
    sems,
    out_sems,
):
    fields, planes, _, _ = adj_hbm.shape
    steps = 4
    cuts = [1 + (planes - 2) * i // steps for i in range(steps + 1)]
    pieces = [slice(a, b) for a, b in zip(cuts[:-1], cuts[1:])]
    moves = [(adj_hbm, adj_ref), (kap_hbm, kap_ref), (conv_hbm, conv_ref)]
    for p in pieces:
        moves.append((jac_hbm.at[:, :, p], jac_ref.at[:, :, p]))
        moves.append((src_hbm.at[:, p], src_ref.at[:, p]))
        moves.append((face_hbm.at[:, p], face_ref.at[:, p]))
    copies = start_all(
        [pltpu.make_async_copy(src, dst, sems.at[i]) for i, (src, dst) in enumerate(moves)]
    )
    wait_all(copies[:3])
    sent = []
    for i, p in enumerate(pieces):
        wait_all(copies[3 + 3 * i:6 + 3 * i])
        for x in range(p.start, p.stop):
            def at(y):
                return [adj_ref[f, y] for f in range(fields)] + [kap_ref[y]]

            here = at(x)
            planes_of = plane_residual(
                here[:fields],
                here[fields],
                at(x - 1),
                at(x + 1),
                lambda k, f: jac_ref[k, f, x],
                lambda d: face_ref[d, x],
                lambda f: src_ref[f, x],
                conv_ref,
            )
            for f in range(fields):
                out_ref[f, x] = planes_of[f]
        copy = pltpu.make_async_copy(out_ref.at[:, p], out_hbm.at[:, p], out_sems.at[i])
        copy.start()
        sent.append(copy)
    wait_all(sent)


def sum_kernel(
    got_ref,
    adj_hbm,
    jac_hbm,
    conv_hbm,
    face_hbm,
    kap_hbm,
    src_hbm,
    mate_ref,
    other_ref,
    part_hbm,
    out_ref,
    res_hbm,
    adj_ref,
    jac_ref,
    conv_ref,
    face_ref,
    kap_ref,
    src_ref,
    res_ref,
    sems,
    out_sems,
):
    del part_hbm
    fields, planes, _, _ = adj_hbm.shape
    ends = (0, planes - 1)
    moves = [(conv_hbm, conv_ref)]
    for i, x in enumerate(ends):
        near = pl.ds(0 if i == 0 else planes - 2, 2)
        moves.append((adj_hbm.at[:, near], adj_ref.at[i]))
        moves.append((kap_hbm.at[near], kap_ref.at[i]))
        moves.append((jac_hbm.at[:, :, x], jac_ref.at[i]))
        moves.append((src_hbm.at[:, x], src_ref.at[i]))
        moves.append((face_hbm.at[:, x], face_ref.at[i]))
    copies = start_all(
        [pltpu.make_async_copy(src, dst, sems.at[i]) for i, (src, dst) in enumerate(moves)]
    )

    sources, _, cap = got_ref.shape
    inner = LAT - 1
    points = lax.broadcasted_iota(jnp.int32, (LAT, cap), 0).astype(F32)
    both = jnp.zeros((6 * LAT, LAT * LAT), F32)
    for s in range(sources):
        block = got_ref[s]
        cell = block[6:7]
        first = jnp.floor((cell + 0.5) * (1.0 / (inner * inner)))
        rest = cell - first * (inner * inner)
        second = jnp.floor((rest + 0.5) * (1.0 / inner))
        third = rest - second * inner
        tent = []
        for d, low in enumerate((first, second, third)):
            u = block[3 + d:4 + d]
            tent.append(
                jnp.where(points == low, 1.0 - u, 0.0) + jnp.where(points == low + 1.0, u, 0.0)
            )
        left = jnp.concatenate([tent[0] * block[c:c + 1] for c in range(3)], 0)
        right = jnp.concatenate([tent[1][b:b + 1] * tent[2] for b in range(LAT)], 0)
        left_hi, left_lo = split_two(left)
        right_hi, right_lo = split_two(right)
        lhs = jnp.concatenate([left_hi, left_lo], 0)
        both = both + lax.dot_general(lhs, right_hi, NT, preferred_element_type=F32)
        both = both + lax.dot_general(lhs, right_lo, NT, preferred_element_type=F32)

    wait_all(copies)
    even = on_even()
    sent = []
    for i, x in enumerate(ends):
        pair = [[adj_ref[i, f, j] for f in range(fields)] + [kap_ref[i, j]] for j in (0, 1)]
        beyond = [
            jnp.where(even == (i == 0), other_ref[f], mate_ref[f]) for f in range(fields + 1)
        ]
        here = pair[i]
        planes_of = plane_residual(
            here[:fields],
            here[fields],
            beyond if i == 0 else pair[0],
            pair[1] if i == 0 else beyond,
            lambda k, f: jac_ref[i, k, f],
            lambda d: face_ref[i, d],
            lambda f: src_ref[i, f],
            conv_ref,
        )
        for f in range(fields):
            res_ref[i, f] = planes_of[f]
        copy = pltpu.make_async_copy(res_ref.at[i], res_hbm.at[:, x], out_sems.at[i])
        copy.start()
        sent.append(copy)
    result = both[:3 * LAT] + both[3 * LAT:]
    for c in range(3):
        for a in range(LAT):
            out_ref[c:c + 1, a * LAT * LAT:(a + 1) * LAT * LAT] = result[c * LAT + a:c * LAT + a + 1]
    wait_all(sent)


def local(
    adjoint,
    jac_diag,
    conv_mats,
    face_scale,
    kappa,
    source,
    box_of_row,
    lattice_cell,
    lattice_frac,
    dres_dx,
    dobj_dx,
):
    boxes = lax.axis_size("blk")
    rows = box_of_row.shape[0]
    cap = 2 * rows // boxes
    fields, planes = adjoint.shape[:2]
    plane = adjoint.shape[2:]
    vmem = pl.BlockSpec(memory_space=pltpu.VMEM)
    hbm = pl.BlockSpec(memory_space=pltpu.HBM)
    params = pltpu.CompilerParams(vmem_limit_bytes=SMALL)
    conv = conv_mats.transpose(1, 0, 2)
    box_row = box_of_row.reshape(1, rows)
    cell_row = lattice_cell.reshape(1, rows)
    box_row, cell_row, conv, adjoint, jac_diag, face_scale, kappa, source = stay(
        box_row, cell_row, conv, adjoint, jac_diag, face_scale, kappa, source
    )
    lattice_frac, dres_dx, dobj_dx = stay(lattice_frac, dres_dx, dobj_dx)

    def shape(*dims):
        return jax.ShapeDtypeStruct(dims, F32)

    packed, to_mate, to_other = pl.pallas_call(
        functools.partial(pack_kernel, boxes, cap),
        out_shape=(shape(boxes, 8, cap), shape(fields + 1, *plane), shape(fields + 1, *plane)),
        in_specs=[hbm] * 7,
        out_specs=(vmem, vmem, vmem),
        scratch_shapes=[
            pltpu.VMEM(adjoint.shape, F32),
            pltpu.VMEM((2,) + plane, F32),
            pltpu.VMEM((1, rows), jnp.int32),
            pltpu.VMEM((1, rows), jnp.int32),
            pltpu.VMEM(lattice_frac.shape, F32),
            pltpu.VMEM(dres_dx.shape, F32),
            pltpu.VMEM(dobj_dx.shape, F32),
            pltpu.VMEM((1, rows), F32),
            pltpu.SemaphoreType.DMA((8,)),
        ],
        compiler_params=params,
        name="pack_rows",
    )(adjoint, kappa, box_row, cell_row, lattice_frac, dres_dx, dobj_dx)
    got = lax.all_to_all(packed, "blk", 0, 0, axis_index_groups=[spread(boxes)], tiled=True)

    pairs = [(i, i + 1) for i in range(boxes - 1)]
    both_ways = [[p for i, j in pairs if i % 2 == turn for p in ((i, j), (j, i))] for turn in (0, 1)]
    mate = lax.ppermute(to_mate, "blk", both_ways[0])
    other = lax.ppermute(to_other, "blk", both_ways[1])

    inner = pl.pallas_call(
        inner_kernel,
        out_shape=shape(*adjoint.shape),
        in_specs=[hbm] * 6 + [pl.BlockSpec(memory_space=pl.ANY)],
        out_specs=hbm,
        scratch_shapes=[
            pltpu.VMEM(adjoint.shape, F32),
            pltpu.VMEM(jac_diag.shape, F32),
            pltpu.SMEM(conv.shape, F32),
            pltpu.VMEM(face_scale.shape, F32),
            pltpu.VMEM(kappa.shape, F32),
            pltpu.VMEM(source.shape, F32),
            pltpu.VMEM(adjoint.shape, F32),
            pltpu.SemaphoreType.DMA((15,)),
            pltpu.SemaphoreType.DMA((4,)),
        ],
        compiler_params=params,
        name="sweep_inner",
    )(adjoint, jac_diag, conv, face_scale, kappa, source, to_mate)

    box_sens, residual = pl.pallas_call(
        sum_kernel,
        out_shape=(shape(3, LAT**3), shape(*adjoint.shape)),
        in_specs=[vmem] + [hbm] * 6 + [vmem, vmem, hbm],
        out_specs=(vmem, hbm),
        scratch_shapes=[
            pltpu.VMEM((2, fields, 2) + plane, F32),
            pltpu.VMEM((2, fields, fields) + plane, F32),
            pltpu.SMEM(conv.shape, F32),
            pltpu.VMEM((2, 3) + plane, F32),
            pltpu.VMEM((2, 2) + plane, F32),
            pltpu.VMEM((2, fields) + plane, F32),
            pltpu.VMEM((2, fields) + plane, F32),
            pltpu.SemaphoreType.DMA((11,)),
            pltpu.SemaphoreType.DMA((2,)),
        ],
        input_output_aliases={9: 1},
        compiler_params=params,
        name="sum_rows",
    )(got, adjoint, jac_diag, conv, face_scale, kappa, source, mate, other, inner)
    return residual, box_sens


def solution(mesh):
    in_specs = (
        P("group", "blk", None, None),
        P("group", None, "blk", None, None),
        P(),
        P("group", "blk", None, None),
        P(("group", "blk"), None, None),
        P("group", "blk", None, None),
        P(("group", "blk"), None),
        P(("group", "blk")),
        P(None, ("group", "blk")),
        P(None, None, ("group", "blk")),
        P(None, ("group", "blk")),
    )
    out_specs = (P("group", "blk", None, None), P("group", "blk"))
    return jax.shard_map(local, mesh=mesh, in_specs=in_specs, out_specs=out_specs, check_vma=False)
```

```python
import functools

import jax
import jax.numpy as jnp
from jax import lax
from jax.experimental import pallas as pl
from jax.experimental.pallas import tpu as pltpu
from jax.sharding import PartitionSpec as P

LAT = 16
CHUNK = 256
ROW = 7
SMALL = 12 * 2**20
F32 = jnp.float32
BF16 = jnp.bfloat16
NT = (((1,), (1,)), ((), ()))
NN = (((1,), (0,)), ((), ()))


def split_two(x):
    hi = x.astype(BF16)
    lo = (x - hi.astype(F32)).astype(BF16)
    return hi, lo


def on_even():
    return lax.axis_index("blk") % 2 == 0


def stay(*arrays):
    return [pltpu.with_memory_space_constraint(a, pltpu.HBM) for a in arrays]


def spread(count):
    quarter = count // 4
    order = []
    for k in range(quarter):
        order += [
            quarter + k,
            3 * quarter + (k + 2) % quarter,
            (k + 3) % quarter,
            2 * quarter + (k + 1) % quarter,
        ]
    return order


def start_all(copies):
    for copy in copies:
        copy.start()
    return copies


def wait_all(copies):
    for copy in copies:
        copy.wait()


def pack_kernel(
    boxes,
    cap,
    adj_hbm,
    kap_hbm,
    box_hbm,
    cell_hbm,
    frac_hbm,
    dres_hbm,
    dobj_hbm,
    out_ref,
    mate_ref,
    other_ref,
    adj_ref,
    kap_ref,
    box_ref,
    cell_ref,
    frac_ref,
    dres_ref,
    dobj_ref,
    ranks_ref,
    sems,
):
    fields, planes, _, lanes = adj_hbm.shape
    rows = planes * lanes
    ends = (0, planes - 1)
    moves = [(box_hbm, box_ref), (dres_hbm, dres_ref), (adj_hbm, adj_ref)]
    moves += [(dobj_hbm, dobj_ref), (frac_hbm, frac_ref), (cell_hbm, cell_ref)]
    moves += [(kap_hbm.at[x], kap_ref.at[i]) for i, x in enumerate(ends)]
    copies = start_all(
        [pltpu.make_async_copy(src, dst, sems.at[i]) for i, (src, dst) in enumerate(moves)]
    )
    copies[0].wait()
    box = box_ref[...]

    chunks = rows // CHUNK
    names = lax.broadcasted_iota(jnp.int32, (boxes, CHUNK), 0)
    hot = [(box[:, j * CHUNK:(j + 1) * CHUNK] == names).astype(F32) for j in range(chunks)]
    earlier = (
        lax.broadcasted_iota(jnp.int32, (CHUNK, CHUNK), 0)
        < lax.broadcasted_iota(jnp.int32, (CHUNK, CHUNK), 1)
    ).astype(F32).astype(BF16)
    counts = lax.dot_general(
        jnp.concatenate(hot, 0).astype(BF16), earlier, NN, preferred_element_type=F32
    )
    offset = jnp.zeros((boxes, 1), F32)
    for j in range(chunks):
        here = counts[j * boxes:(j + 1) * boxes]
        ranks_ref[:, j * CHUNK:(j + 1) * CHUNK] = jnp.sum(
            hot[j] * (here + offset), axis=0, keepdims=True
        )
        offset = offset + here[:, CHUNK - 1:] + hot[j][:, CHUNK - 1:]

    wait_all(copies[1:])
    even = on_even()
    for f in range(fields + 1):
        first = adj_ref[f, 0] if f < fields else kap_ref[0]
        last = adj_ref[f, planes - 1] if f < fields else kap_ref[1]
        mate_ref[f] = jnp.where(even, last, first)
        other_ref[f] = jnp.where(even, first, last)

    total = jnp.zeros((boxes * 16, cap), F32)
    slots = lax.broadcasted_iota(jnp.int32, (cap, CHUNK), 0).astype(F32)
    per = CHUNK // lanes
    for j in range(chunks):
        part = slice(j * CHUNK, (j + 1) * CHUNK)
        acc = dobj_ref[:, part]
        for k in range(fields):
            psi = jnp.concatenate(
                [adj_ref[k, x, 0:1, :] for x in range(j * per, (j + 1) * per)], 1
            )
            acc = acc - dres_ref[k, :, part] * psi
        values = jnp.concatenate(
            [acc, frac_ref[:, part], cell_ref[:, part].astype(F32), jnp.zeros((1, CHUNK), F32)], 0
        )
        hi = values.astype(BF16).astype(F32)
        both = jnp.concatenate([hi, values - hi], 0)
        mine = box[:, part]
        lhs = jnp.concatenate(
            [jnp.where(mine == b, both, 0.0) for b in spread(boxes)], 0
        ).astype(BF16)
        rhs = (slots == ranks_ref[:, part]).astype(F32).astype(BF16)
        total = total + lax.dot_general(lhs, rhs, NT, preferred_element_type=F32)
    width = out_ref.shape[-1]
    for b in range(boxes):
        block = total[b * 16:b * 16 + ROW] + total[b * 16 + 8:b * 16 + 8 + ROW]
        for i in range(cap // width):
            out_ref[b, :, i, :] = block[:, i * width:(i + 1) * width]


def plane_residual(psi, kap, below, above, jac, face, src, conv):
    fields = len(psi)
    rows, lanes = kap.shape
    row = lax.broadcasted_iota(jnp.int32, (rows, lanes), 0)
    lane = lax.broadcasted_iota(jnp.int32, (rows, lanes), 1)
    masks = ((row < rows - 1, row > 0), (lane < lanes - 1, lane > 0))

    def sides(value, dim):
        size = value.shape[dim]
        up = jnp.where(masks[dim][0], pltpu.roll(value, size - 1, dim), 0.0)
        down = jnp.where(masks[dim][1], pltpu.roll(value, 1, dim), 0.0)
        return up, down

    centre = list(psi) + [kap]
    result = []
    for f in range(fields):
        total = jac(0, f) * psi[0]
        for k in range(1, fields):
            total = total + jac(k, f) * psi[k]
        result.append(total - src(f))
    spread = None
    for d in range(3):
        pair = list(zip(above, below)) if d == 0 else [sides(v, d - 1) for v in centre]
        scale = 0.5 * face(d)
        diff = [scale * (pair[k][0] - pair[k][1]) for k in range(fields)]
        up = 0.5 * (kap + pair[fields][0])
        down = 0.5 * (kap + pair[fields][1])
        spread = up + down if spread is None else spread + up + down
        for f in range(fields):
            total = result[f]
            for k in range(fields):
                total = total + conv[k, d, f] * diff[k]
            result[f] = total - up * pair[f][0] - down * pair[f][1]
    return [result[f] + spread * psi[f] for f in range(fields)]


def sweep_kernel(
    adj_hbm,
    jac_hbm,
    conv_hbm,
    face_hbm,
    kap_hbm,
    src_hbm,
    after_hbm,
    out_hbm,
    edge_ref,
    adj_ref,
    jac_ref,
    conv_ref,
    face_ref,
    kap_ref,
    src_ref,
    out_ref,
    sems,
    out_sems,
):
    fields, planes, _, _ = adj_hbm.shape
    steps = 4
    cuts = [planes * i // steps for i in range(steps + 1)]
    pieces = [slice(a, b) for a, b in zip(cuts[:-1], cuts[1:])]
    moves = [(adj_hbm, adj_ref), (kap_hbm, kap_ref), (conv_hbm, conv_ref)]
    for p in pieces:
        moves.append((jac_hbm.at[:, :, p], jac_ref.at[:, :, p]))
        moves.append((src_hbm.at[:, p], src_ref.at[:, p]))
        moves.append((face_hbm.at[:, p], face_ref.at[:, p]))
    copies = start_all(
        [pltpu.make_async_copy(src, dst, sems.at[i]) for i, (src, dst) in enumerate(moves)]
    )
    wait_all(copies[:3])
    nothing = [jnp.zeros(adj_hbm.shape[2:], F32)] * (fields + 1)
    sent = []
    for i, p in enumerate(pieces):
        wait_all(copies[3 + 3 * i:6 + 3 * i])
        for x in range(p.start, p.stop):
            def at(y):
                if 0 <= y < planes:
                    return [adj_ref[f, y] for f in range(fields)] + [kap_ref[y]]
                return nothing

            here = at(x)
            planes_of = plane_residual(
                here[:fields],
                here[fields],
                at(x - 1),
                at(x + 1),
                lambda k, f: jac_ref[k, f, x],
                lambda d: face_ref[d, x],
                lambda f: src_ref[f, x],
                conv_ref,
            )
            for f in range(fields):
                out_ref[f, x] = planes_of[f]
            if x in (0, planes - 1):
                e = 0 if x == 0 else 1
                for f in range(fields):
                    edge_ref[e, f] = planes_of[f]
                    edge_ref[e, fields + f] = here[f]
                edge_ref[e, 2 * fields] = here[fields]
                edge_ref[e, 2 * fields + 1] = face_ref[0, x]
        copy = pltpu.make_async_copy(out_ref.at[:, p], out_hbm.at[:, p], out_sems.at[i])
        copy.start()
        sent.append(copy)
    wait_all(sent)


def sum_kernel(
    got_ref,
    edge_ref,
    mate_ref,
    other_ref,
    conv_hbm,
    part_hbm,
    out_ref,
    res_hbm,
    conv_ref,
    res_ref,
    sem,
    out_sems,
):
    del part_hbm
    fields, planes = res_hbm.shape[:2]
    conv_copy = pltpu.make_async_copy(conv_hbm, conv_ref, sem)
    conv_copy.start()

    def edges():
        conv_copy.wait()
        even = on_even()
        copies = []
        for e in (0, 1):
            beyond = [
                jnp.where(even == (e == 0), other_ref[f], mate_ref[f]) for f in range(fields + 1)
            ]
            kap = edge_ref[e, 2 * fields]
            scale = edge_ref[e, 2 * fields + 1] * (0.5 if e else -0.5)
            terms = [scale * beyond[k] for k in range(fields)]
            weight = 0.5 * (kap + beyond[fields])
            extra = 0.5 * beyond[fields]
            for f in range(fields):
                total = edge_ref[e, f] - weight * beyond[f] + extra * edge_ref[e, fields + f]
                for k in range(fields):
                    total = total + conv_ref[k, 0, f] * terms[k]
                res_ref[e, f] = total
            copies.append(
                pltpu.make_async_copy(res_ref.at[e], res_hbm.at[:, e * (planes - 1)], out_sems.at[e])
            )
        return start_all(copies)

    sources, _, cuts, width = got_ref.shape
    cap = cuts * width
    inner = LAT - 1
    points = lax.broadcasted_iota(jnp.int32, (LAT, cap), 0).astype(F32)
    both = jnp.zeros((6 * LAT, LAT * LAT), F32)
    for s in range(sources):
        if s == sources // 2:
            sent = edges()
        block = jnp.concatenate([got_ref[s, :, i, :] for i in range(cuts)], 1)
        cell = block[6:7]
        first = jnp.floor((cell + 0.5) * (1.0 / (inner * inner)))
        rest = cell - first * (inner * inner)
        second = jnp.floor((rest + 0.5) * (1.0 / inner))
        third = rest - second * inner
        tent = []
        for d, low in enumerate((first, second, third)):
            u = block[3 + d:4 + d]
            tent.append(
                jnp.where(points == low, 1.0 - u, 0.0) + jnp.where(points == low + 1.0, u, 0.0)
            )
        left = jnp.concatenate([tent[0] * block[c:c + 1] for c in range(3)], 0)
        right = jnp.concatenate([tent[1][b:b + 1] * tent[2] for b in range(LAT)], 0)
        left_hi, left_lo = split_two(left)
        right_hi, right_lo = split_two(right)
        lhs = jnp.concatenate([left_hi, left_lo], 0)
        both = both + lax.dot_general(lhs, right_hi, NT, preferred_element_type=F32)
        both = both + lax.dot_general(lhs, right_lo, NT, preferred_element_type=F32)
    result = both[:3 * LAT] + both[3 * LAT:]
    for c in range(3):
        for a in range(LAT):
            out_ref[c:c + 1, a * LAT * LAT:(a + 1) * LAT * LAT] = result[c * LAT + a:c * LAT + a + 1]
    wait_all(sent)


def local(
    adjoint,
    jac_diag,
    conv_mats,
    face_scale,
    kappa,
    source,
    box_of_row,
    lattice_cell,
    lattice_frac,
    dres_dx,
    dobj_dx,
):
    boxes = lax.axis_size("blk")
    rows = box_of_row.shape[0]
    cap = 2 * rows // boxes
    fields, planes = adjoint.shape[:2]
    plane = adjoint.shape[2:]
    vmem = pl.BlockSpec(memory_space=pltpu.VMEM)
    hbm = pl.BlockSpec(memory_space=pltpu.HBM)
    params = pltpu.CompilerParams(vmem_limit_bytes=SMALL)
    conv = conv_mats.transpose(1, 0, 2)
    box_row = box_of_row.reshape(1, rows)
    cell_row = lattice_cell.reshape(1, rows)
    box_row, cell_row, conv, adjoint, jac_diag, face_scale, kappa, source = stay(
        box_row, cell_row, conv, adjoint, jac_diag, face_scale, kappa, source
    )
    lattice_frac, dres_dx, dobj_dx = stay(lattice_frac, dres_dx, dobj_dx)

    width = min(128, cap)
    payload = (boxes, ROW, cap // width, width)

    def shape(*dims):
        return jax.ShapeDtypeStruct(dims, F32)

    packed, to_mate, to_other = pl.pallas_call(
        functools.partial(pack_kernel, boxes, cap),
        out_shape=(shape(*payload), shape(fields + 1, *plane), shape(fields + 1, *plane)),
        in_specs=[hbm] * 7,
        out_specs=(vmem, vmem, vmem),
        scratch_shapes=[
            pltpu.VMEM(adjoint.shape, F32),
            pltpu.VMEM((2,) + plane, F32),
            pltpu.VMEM((1, rows), jnp.int32),
            pltpu.VMEM((1, rows), jnp.int32),
            pltpu.VMEM(lattice_frac.shape, F32),
            pltpu.VMEM(dres_dx.shape, F32),
            pltpu.VMEM(dobj_dx.shape, F32),
            pltpu.VMEM((1, rows), F32),
            pltpu.SemaphoreType.DMA((8,)),
        ],
        compiler_params=params,
        name="pack_rows",
    )(adjoint, kappa, box_row, cell_row, lattice_frac, dres_dx, dobj_dx)
    got = lax.all_to_all(packed, "blk", 0, 0, axis_index_groups=[spread(boxes)], tiled=True)

    pairs = [(i, i + 1) for i in range(boxes - 1)]
    both_ways = [[p for i, j in pairs if i % 2 == turn for p in ((i, j), (j, i))] for turn in (0, 1)]
    mate = lax.ppermute(to_mate, "blk", both_ways[0])
    other = lax.ppermute(to_other, "blk", both_ways[1])

    inner, edge = pl.pallas_call(
        sweep_kernel,
        out_shape=(shape(*adjoint.shape), shape(2, 2 * fields + 2, *plane)),
        in_specs=[hbm] * 6 + [pl.BlockSpec(memory_space=pl.ANY)],
        out_specs=(hbm, vmem),
        scratch_shapes=[
            pltpu.VMEM(adjoint.shape, F32),
            pltpu.VMEM(jac_diag.shape, F32),
            pltpu.SMEM(conv.shape, F32),
            pltpu.VMEM(face_scale.shape, F32),
            pltpu.VMEM(kappa.shape, F32),
            pltpu.VMEM(source.shape, F32),
            pltpu.VMEM(adjoint.shape, F32),
            pltpu.SemaphoreType.DMA((15,)),
            pltpu.SemaphoreType.DMA((4,)),
        ],
        compiler_params=params,
        name="sweep_planes",
    )(adjoint, jac_diag, conv, face_scale, kappa, source, to_mate)

    box_sens, residual = pl.pallas_call(
        sum_kernel,
        out_shape=(shape(3, LAT**3), shape(*adjoint.shape)),
        in_specs=[vmem] * 4 + [hbm, hbm],
        out_specs=(vmem, hbm),
        scratch_shapes=[
            pltpu.SMEM(conv.shape, F32),
            pltpu.VMEM((2, fields) + plane, F32),
            pltpu.SemaphoreType.DMA,
            pltpu.SemaphoreType.DMA((2,)),
        ],
        input_output_aliases={5: 1},
        compiler_params=params,
        name="sum_rows",
    )(got, edge, mate, other, conv, inner)
    return residual, box_sens


def solution(mesh):
    in_specs = (
        P("group", "blk", None, None),
        P("group", None, "blk", None, None),
        P(),
        P("group", "blk", None, None),
        P(("group", "blk"), None, None),
        P("group", "blk", None, None),
        P(("group", "blk"), None),
        P(("group", "blk")),
        P(None, ("group", "blk")),
        P(None, None, ("group", "blk")),
        P(None, ("group", "blk")),
    )
    out_specs = (P("group", "blk", None, None), P("group", "blk"))
    return jax.shard_map(local, mesh=mesh, in_specs=in_specs, out_specs=out_specs, check_vma=False)
```

```python
import functools

import jax
import jax.numpy as jnp
from jax import lax
from jax.experimental import pallas as pl
from jax.experimental.pallas import tpu as pltpu
from jax.sharding import PartitionSpec as P

LAT = 16
CHUNK = 256
ROW = 7
SMALL = 12 * 2**20
F32 = jnp.float32
BF16 = jnp.bfloat16
NT = (((1,), (1,)), ((), ()))
NN = (((1,), (0,)), ((), ()))


def split_two(x):
    hi = x.astype(BF16)
    lo = (x - hi.astype(F32)).astype(BF16)
    return hi, lo


def on_even():
    return lax.axis_index("blk") % 2 == 0


def stay(*arrays):
    return [pltpu.with_memory_space_constraint(a, pltpu.HBM) for a in arrays]


def spread(count):
    quarter = count // 4
    order = []
    for k in range(quarter):
        order += [
            quarter + k,
            3 * quarter + (k + 2) % quarter,
            (k + 3) % quarter,
            2 * quarter + (k + 1) % quarter,
        ]
    return order


def start_all(copies):
    for copy in copies:
        copy.start()
    return copies


def wait_all(copies):
    for copy in copies:
        copy.wait()


def pack_kernel(
    boxes,
    cap,
    adj_hbm,
    kap_hbm,
    box_hbm,
    cell_hbm,
    frac_hbm,
    dres_hbm,
    dobj_hbm,
    conv_hbm,
    jac_hbm,
    src_hbm,
    face_hbm,
    out_ref,
    mate_ref,
    other_ref,
    adj_ref,
    kap_ref,
    fill_ref,
    jac_ref,
    src_ref,
    face_ref,
    conv_ref,
    box_ref,
    cell_ref,
    frac_ref,
    dres_ref,
    dobj_ref,
    ranks_ref,
    sems,
):
    fields, planes, _, lanes = adj_hbm.shape
    rows = planes * lanes
    moves = [(box_hbm, box_ref), (dres_hbm, dres_ref), (adj_hbm, adj_ref)]
    moves += [(dobj_hbm, dobj_ref), (frac_hbm, frac_ref), (cell_hbm, cell_ref)]
    moves += [(kap_hbm, kap_ref), (conv_hbm, conv_ref), (jac_hbm, jac_ref)]
    moves += [(src_hbm, src_ref), (face_hbm, face_ref)]
    copies = start_all(
        [pltpu.make_async_copy(src, dst, sems.at[i]) for i, (src, dst) in enumerate(moves)]
    )
    copies[0].wait()
    box = box_ref[...]

    chunks = rows // CHUNK
    names = lax.broadcasted_iota(jnp.int32, (boxes, CHUNK), 0)
    hot = [(box[:, j * CHUNK:(j + 1) * CHUNK] == names).astype(F32) for j in range(chunks)]
    earlier = (
        lax.broadcasted_iota(jnp.int32, (CHUNK, CHUNK), 0)
        < lax.broadcasted_iota(jnp.int32, (CHUNK, CHUNK), 1)
    ).astype(F32).astype(BF16)
    counts = lax.dot_general(
        jnp.concatenate(hot, 0).astype(BF16), earlier, NN, preferred_element_type=F32
    )
    offset = jnp.zeros((boxes, 1), F32)
    for j in range(chunks):
        here = counts[j * boxes:(j + 1) * boxes]
        ranks_ref[:, j * CHUNK:(j + 1) * CHUNK] = jnp.sum(
            hot[j] * (here + offset), axis=0, keepdims=True
        )
        offset = offset + here[:, CHUNK - 1:] + hot[j][:, CHUNK - 1:]

    wait_all(copies[1:7])
    even = on_even()
    for f in range(fields + 1):
        first = adj_ref[f, 0] if f < fields else kap_ref[0]
        last = adj_ref[f, planes - 1] if f < fields else kap_ref[planes - 1]
        mate_ref[f] = jnp.where(even, last, first)
        other_ref[f] = jnp.where(even, first, last)

    total = jnp.zeros((boxes * 16, cap), F32)
    slots = lax.broadcasted_iota(jnp.int32, (cap, CHUNK), 0).astype(F32)
    per = CHUNK // lanes
    for j in range(chunks):
        part = slice(j * CHUNK, (j + 1) * CHUNK)
        acc = dobj_ref[:, part]
        for k in range(fields):
            psi = jnp.concatenate(
                [adj_ref[k, x, 0:1, :] for x in range(j * per, (j + 1) * per)], 1
            )
            acc = acc - dres_ref[k, :, part] * psi
        values = jnp.concatenate(
            [acc, frac_ref[:, part], cell_ref[:, part].astype(F32), jnp.zeros((1, CHUNK), F32)], 0
        )
        hi = values.astype(BF16).astype(F32)
        both = jnp.concatenate([hi, values - hi], 0)
        mine = box[:, part]
        lhs = jnp.concatenate(
            [jnp.where(mine == b, both, 0.0) for b in spread(boxes)], 0
        ).astype(BF16)
        rhs = (slots == ranks_ref[:, part]).astype(F32).astype(BF16)
        total = total + lax.dot_general(lhs, rhs, NT, preferred_element_type=F32)
    width = out_ref.shape[-1]
    for b in range(boxes):
        block = total[b * 16:b * 16 + ROW] + total[b * 16 + 8:b * 16 + 8 + ROW]
        for i in range(cap // width):
            out_ref[b, :, i, :] = block[:, i * width:(i + 1) * width]
    wait_all(copies[7:])
    for k in range(fields):
        for d in range(3):
            for f in range(fields):
                fill_ref[k, d, f] = jnp.full(kap_ref.shape[1:], conv_ref[k, d, f], F32)


def plane_residual(psi, kap, below, above, jac, face, src, conv):
    fields = len(psi)
    rows, lanes = kap.shape
    row = lax.broadcasted_iota(jnp.int32, (rows, lanes), 0)
    lane = lax.broadcasted_iota(jnp.int32, (rows, lanes), 1)
    masks = ((row < rows - 1, row > 0), (lane < lanes - 1, lane > 0))

    def sides(value, dim):
        size = value.shape[dim]
        up = jnp.where(masks[dim][0], pltpu.roll(value, size - 1, dim), 0.0)
        down = jnp.where(masks[dim][1], pltpu.roll(value, 1, dim), 0.0)
        return up, down

    centre = list(psi) + [kap]
    result = []
    for f in range(fields):
        total = jac(0, f) * psi[0]
        for k in range(1, fields):
            total = total + jac(k, f) * psi[k]
        result.append(total - src(f))
    spread = None
    for d in range(3):
        pair = list(zip(above, below)) if d == 0 else [sides(v, d - 1) for v in centre]
        scale = 0.5 * face(d)
        diff = [scale * (pair[k][0] - pair[k][1]) for k in range(fields)]
        up = 0.5 * (kap + pair[fields][0])
        down = 0.5 * (kap + pair[fields][1])
        spread = up + down if spread is None else spread + up + down
        for f in range(fields):
            total = result[f]
            for k in range(fields):
                total = total + conv(k, d, f) * diff[k]
            result[f] = total - up * pair[f][0] - down * pair[f][1]
    return [result[f] + spread * psi[f] for f in range(fields)]


def sweep_kernel(
    adj_ref,
    jac_ref,
    fill_ref,
    face_ref,
    kap_ref,
    src_ref,
    out_hbm,
    edge_ref,
    out_ref,
    out_sems,
):
    fields, planes = adj_ref.shape[:2]
    steps = 4
    cuts = [planes * i // steps for i in range(steps + 1)]
    pieces = [slice(a, b) for a, b in zip(cuts[:-1], cuts[1:])]
    nothing = [jnp.zeros(kap_ref.shape[1:], F32)] * (fields + 1)
    sent = []
    for i, p in enumerate(pieces):
        for x in range(p.start, p.stop):
            def at(y):
                if 0 <= y < planes:
                    return [adj_ref[f, y] for f in range(fields)] + [kap_ref[y]]
                return nothing

            here = at(x)
            planes_of = plane_residual(
                here[:fields],
                here[fields],
                at(x - 1),
                at(x + 1),
                lambda k, f: jac_ref[k, f, x],
                lambda d: face_ref[d, x],
                lambda f: src_ref[f, x],
                lambda k, d, f: fill_ref[k, d, f],
            )
            for f in range(fields):
                out_ref[f, x] = planes_of[f]
            if x in (0, planes - 1):
                e = 0 if x == 0 else 2 * fields + 2
                for f in range(fields):
                    edge_ref[e + f] = planes_of[f]
                    edge_ref[e + fields + f] = here[f]
                edge_ref[e + 2 * fields] = here[fields]
                edge_ref[e + 2 * fields + 1] = face_ref[0, x]
        copy = pltpu.make_async_copy(out_ref.at[:, p], out_hbm.at[:, p], out_sems.at[i])
        copy.start()
        sent.append(copy)
    for k in range(fields):
        for f in range(fields):
            edge_ref[4 * fields + 4 + k * fields + f] = fill_ref[k, 0, f]
    wait_all(sent)


def sum_kernel(
    got_ref,
    edge_ref,
    mate_ref,
    other_ref,
    part_hbm,
    out_ref,
    res_hbm,
    res_ref,
    out_sems,
):
    del part_hbm
    fields, planes = res_hbm.shape[:2]

    def edges():
        even = on_even()
        copies = []
        for e in (0, 1):
            beyond = [
                jnp.where(even == (e == 0), other_ref[f], mate_ref[f]) for f in range(fields + 1)
            ]
            base = e * (2 * fields + 2)
            kap = edge_ref[base + 2 * fields]
            scale = edge_ref[base + 2 * fields + 1] * (0.5 if e else -0.5)
            terms = [scale * beyond[k] for k in range(fields)]
            weight = 0.5 * (kap + beyond[fields])
            extra = 0.5 * beyond[fields]
            for f in range(fields):
                total = edge_ref[base + f] - weight * beyond[f] + extra * edge_ref[base + fields + f]
                for k in range(fields):
                    total = total + edge_ref[4 * fields + 4 + k * fields + f] * terms[k]
                res_ref[e, f] = total
            copies.append(
                pltpu.make_async_copy(res_ref.at[e], res_hbm.at[:, e * (planes - 1)], out_sems.at[e])
            )
        return start_all(copies)

    sources, _, cuts, width = got_ref.shape
    cap = cuts * width
    inner = LAT - 1
    points = lax.broadcasted_iota(jnp.int32, (LAT, cap), 0).astype(F32)
    both = jnp.zeros((6 * LAT, LAT * LAT), F32)
    for s in range(sources):
        if s == sources // 4:
            sent = edges()
        block = jnp.concatenate([got_ref[s, :, i, :] for i in range(cuts)], 1)
        cell = block[6:7]
        first = jnp.floor((cell + 0.5) * (1.0 / (inner * inner)))
        rest = cell - first * (inner * inner)
        second = jnp.floor((rest + 0.5) * (1.0 / inner))
        third = rest - second * inner
        tent = []
        for d, low in enumerate((first, second, third)):
            u = block[3 + d:4 + d]
            tent.append(
                jnp.where(points == low, 1.0 - u, 0.0) + jnp.where(points == low + 1.0, u, 0.0)
            )
        left = jnp.concatenate([tent[0] * block[c:c + 1] for c in range(3)], 0)
        right = jnp.concatenate([tent[1][b:b + 1] * tent[2] for b in range(LAT)], 0)
        left_hi, left_lo = split_two(left)
        right_hi, right_lo = split_two(right)
        lhs = jnp.concatenate([left_hi, left_lo], 0)
        both = both + lax.dot_general(lhs, right_hi, NT, preferred_element_type=F32)
        both = both + lax.dot_general(lhs, right_lo, NT, preferred_element_type=F32)
    result = both[:3 * LAT] + both[3 * LAT:]
    for c in range(3):
        for a in range(LAT):
            out_ref[c:c + 1, a * LAT * LAT:(a + 1) * LAT * LAT] = result[c * LAT + a:c * LAT + a + 1]
    wait_all(sent)


def local(
    adjoint,
    jac_diag,
    conv_mats,
    face_scale,
    kappa,
    source,
    box_of_row,
    lattice_cell,
    lattice_frac,
    dres_dx,
    dobj_dx,
):
    boxes = lax.axis_size("blk")
    rows = box_of_row.shape[0]
    cap = 2 * rows // boxes
    fields, planes = adjoint.shape[:2]
    plane = adjoint.shape[2:]
    vmem = pl.BlockSpec(memory_space=pltpu.VMEM)
    hbm = pl.BlockSpec(memory_space=pltpu.HBM)
    params = pltpu.CompilerParams(vmem_limit_bytes=SMALL)
    conv = conv_mats.transpose(1, 0, 2)
    box_row = box_of_row.reshape(1, rows)
    cell_row = lattice_cell.reshape(1, rows)
    box_row, cell_row, conv, adjoint, jac_diag, face_scale, kappa, source = stay(
        box_row, cell_row, conv, adjoint, jac_diag, face_scale, kappa, source
    )
    lattice_frac, dres_dx, dobj_dx = stay(lattice_frac, dres_dx, dobj_dx)

    width = min(128, cap)
    payload = (boxes, ROW, cap // width, width)

    def shape(*dims):
        return jax.ShapeDtypeStruct(dims, F32)

    halo = shape(fields + 1, *plane)
    packed, to_mate, to_other, adj, kap, fill, jac, src, face = pl.pallas_call(
        functools.partial(pack_kernel, boxes, cap),
        out_shape=(
            shape(*payload),
            halo,
            halo,
            shape(*adjoint.shape),
            shape(*kappa.shape),
            shape(*conv.shape, *plane),
            shape(*jac_diag.shape),
            shape(*source.shape),
            shape(*face_scale.shape),
        ),
        in_specs=[hbm] * 11,
        out_specs=(vmem,) * 9,
        scratch_shapes=[
            pltpu.SMEM(conv.shape, F32),
            pltpu.VMEM((1, rows), jnp.int32),
            pltpu.VMEM((1, rows), jnp.int32),
            pltpu.VMEM(lattice_frac.shape, F32),
            pltpu.VMEM(dres_dx.shape, F32),
            pltpu.VMEM(dobj_dx.shape, F32),
            pltpu.VMEM((1, rows), F32),
            pltpu.SemaphoreType.DMA((11,)),
        ],
        compiler_params=params,
        name="pack_rows",
    )(
        adjoint,
        kappa,
        box_row,
        cell_row,
        lattice_frac,
        dres_dx,
        dobj_dx,
        conv,
        jac_diag,
        source,
        face_scale,
    )
    got = lax.all_to_all(packed, "blk", 0, 0, axis_index_groups=[spread(boxes)], tiled=True)

    pairs = [(i, i + 1) for i in range(boxes - 1)]
    both_ways = [[p for i, j in pairs if i % 2 == turn for p in ((i, j), (j, i))] for turn in (0, 1)]
    mate = lax.ppermute(to_mate, "blk", both_ways[0])
    other = lax.ppermute(to_other, "blk", both_ways[1])

    inner, edge = pl.pallas_call(
        sweep_kernel,
        out_shape=(
            shape(*adjoint.shape),
            shape(2 * (2 * fields + 2) + fields * fields, *plane),
        ),
        in_specs=[vmem] * 6,
        out_specs=(hbm, vmem),
        scratch_shapes=[
            pltpu.VMEM(adjoint.shape, F32),
            pltpu.SemaphoreType.DMA((4,)),
        ],
        compiler_params=params,
        name="sweep_planes",
    )(adj, jac, fill, face, kap, src)

    box_sens, residual = pl.pallas_call(
        sum_kernel,
        out_shape=(shape(3, LAT**3), shape(*adjoint.shape)),
        in_specs=[vmem] * 4 + [hbm],
        out_specs=(vmem, hbm),
        scratch_shapes=[
            pltpu.VMEM((2, fields) + plane, F32),
            pltpu.SemaphoreType.DMA((2,)),
        ],
        input_output_aliases={4: 1},
        compiler_params=params,
        name="sum_rows",
    )(got, edge, mate, other, inner)
    return residual, box_sens


def solution(mesh):
    in_specs = (
        P("group", "blk", None, None),
        P("group", None, "blk", None, None),
        P(),
        P("group", "blk", None, None),
        P(("group", "blk"), None, None),
        P("group", "blk", None, None),
        P(("group", "blk"), None),
        P(("group", "blk")),
        P(None, ("group", "blk")),
        P(None, None, ("group", "blk")),
        P(None, ("group", "blk")),
    )
    out_specs = (P("group", "blk", None, None), P("group", "blk"))
    return jax.shard_map(local, mesh=mesh, in_specs=in_specs, out_specs=out_specs, check_vma=False)
```

```python
import functools

import jax
import jax.numpy as jnp
from jax import lax
from jax.experimental import pallas as pl
from jax.experimental.pallas import tpu as pltpu
from jax.sharding import PartitionSpec as P

LAT = 16
CHUNK = 256
ROW = 7
GROUP = 4
SMALL = 12 * 2**20
F32 = jnp.float32
BF16 = jnp.bfloat16
NT = (((1,), (1,)), ((), ()))
NN = (((1,), (0,)), ((), ()))


def split_two(x):
    hi = x.astype(BF16)
    lo = (x - hi.astype(F32)).astype(BF16)
    return hi, lo


def on_even():
    return lax.axis_index("blk") % 2 == 0


def stay(*arrays):
    return [pltpu.with_memory_space_constraint(a, pltpu.HBM) for a in arrays]


def spread(count):
    quarter = count // 4
    order = []
    for k in range(quarter):
        order += [
            quarter + k,
            3 * quarter + (k + 2) % quarter,
            (k + 3) % quarter,
            2 * quarter + (k + 1) % quarter,
        ]
    return order


def start_all(copies):
    for copy in copies:
        copy.start()
    return copies


def wait_all(copies):
    for copy in copies:
        copy.wait()


def pack_kernel(
    boxes,
    cap,
    adj_hbm,
    kap_hbm,
    box_hbm,
    cell_hbm,
    frac_hbm,
    dres_hbm,
    dobj_hbm,
    conv_hbm,
    jac_hbm,
    src_hbm,
    face_hbm,
    out_ref,
    mate_ref,
    other_ref,
    adj_ref,
    kap_ref,
    fill_ref,
    jac_ref,
    src_ref,
    face_ref,
    conv_ref,
    box_ref,
    cell_ref,
    frac_ref,
    dres_ref,
    dobj_ref,
    ranks_ref,
    sems,
):
    fields, planes, _, lanes = adj_hbm.shape
    rows = planes * lanes
    moves = [(box_hbm, box_ref), (dres_hbm, dres_ref), (adj_hbm, adj_ref)]
    moves += [(dobj_hbm, dobj_ref), (frac_hbm, frac_ref), (cell_hbm, cell_ref)]
    moves += [(kap_hbm, kap_ref), (conv_hbm, conv_ref), (jac_hbm, jac_ref)]
    moves += [(src_hbm, src_ref), (face_hbm, face_ref)]
    copies = start_all(
        [pltpu.make_async_copy(src, dst, sems.at[i]) for i, (src, dst) in enumerate(moves)]
    )
    copies[0].wait()
    box = box_ref[...]

    chunks = rows // CHUNK
    names = lax.broadcasted_iota(jnp.int32, (boxes, CHUNK), 0)
    hot = [(box[:, j * CHUNK:(j + 1) * CHUNK] == names).astype(F32) for j in range(chunks)]
    earlier = (
        lax.broadcasted_iota(jnp.int32, (CHUNK, CHUNK), 0)
        < lax.broadcasted_iota(jnp.int32, (CHUNK, CHUNK), 1)
    ).astype(F32).astype(BF16)
    counts = lax.dot_general(
        jnp.concatenate(hot, 0).astype(BF16), earlier, NN, preferred_element_type=F32
    )
    offset = jnp.zeros((boxes, 1), F32)
    for j in range(chunks):
        here = counts[j * boxes:(j + 1) * boxes]
        ranks_ref[:, j * CHUNK:(j + 1) * CHUNK] = jnp.sum(
            hot[j] * (here + offset), axis=0, keepdims=True
        )
        offset = offset + here[:, CHUNK - 1:] + hot[j][:, CHUNK - 1:]

    wait_all(copies[1:7])
    even = on_even()
    for f in range(fields + 1):
        first = adj_ref[f, 0] if f < fields else kap_ref[0]
        last = adj_ref[f, planes - 1] if f < fields else kap_ref[planes - 1]
        mate_ref[f] = jnp.where(even, last, first)
        other_ref[f] = jnp.where(even, first, last)

    total = jnp.zeros((boxes * 16, cap), F32)
    slots = lax.broadcasted_iota(jnp.int32, (cap, CHUNK), 0).astype(F32)
    per = CHUNK // lanes
    lefts, rights = [], []
    for j in range(chunks):
        part = slice(j * CHUNK, (j + 1) * CHUNK)
        acc = dobj_ref[:, part]
        for k in range(fields):
            psi = jnp.concatenate(
                [adj_ref[k, x, 0:1, :] for x in range(j * per, (j + 1) * per)], 1
            )
            acc = acc - dres_ref[k, :, part] * psi
        values = jnp.concatenate(
            [acc, frac_ref[:, part], cell_ref[:, part].astype(F32), jnp.zeros((1, CHUNK), F32)], 0
        )
        hi = values.astype(BF16).astype(F32)
        both = jnp.concatenate([hi, values - hi], 0)
        mine = box[:, part]
        lefts.append(
            jnp.concatenate([jnp.where(mine == b, both, 0.0) for b in spread(boxes)], 0).astype(BF16)
        )
        rights.append((slots == ranks_ref[:, part]).astype(F32).astype(BF16))
        if len(lefts) == GROUP:
            total = total + lax.dot_general(
                jnp.concatenate(lefts, 1),
                jnp.concatenate(rights, 1),
                NT,
                preferred_element_type=F32,
            )
            lefts, rights = [], []
    width = out_ref.shape[-1]
    for b in range(boxes):
        block = total[b * 16:b * 16 + ROW] + total[b * 16 + 8:b * 16 + 8 + ROW]
        for i in range(cap // width):
            out_ref[b, :, i, :] = block[:, i * width:(i + 1) * width]
    wait_all(copies[7:])
    for k in range(fields):
        for d in range(3):
            for f in range(fields):
                fill_ref[k, d, f] = jnp.full(kap_ref.shape[1:], conv_ref[k, d, f], F32)


def plane_residual(psi, kap, below, above, jac, face, src, conv):
    fields = len(psi)
    rows, lanes = kap.shape
    row = lax.broadcasted_iota(jnp.int32, (rows, lanes), 0)
    lane = lax.broadcasted_iota(jnp.int32, (rows, lanes), 1)
    masks = ((row < rows - 1, row > 0), (lane < lanes - 1, lane > 0))

    def sides(value, dim):
        size = value.shape[dim]
        up = jnp.where(masks[dim][0], pltpu.roll(value, size - 1, dim), 0.0)
        down = jnp.where(masks[dim][1], pltpu.roll(value, 1, dim), 0.0)
        return up, down

    centre = list(psi) + [kap]
    result = []
    for f in range(fields):
        total = jac(0, f) * psi[0]
        for k in range(1, fields):
            total = total + jac(k, f) * psi[k]
        result.append(total - src(f))
    spread = None
    for d in range(3):
        pair = list(zip(above, below)) if d == 0 else [sides(v, d - 1) for v in centre]
        scale = 0.5 * face(d)
        diff = [scale * (pair[k][0] - pair[k][1]) for k in range(fields)]
        up = 0.5 * (kap + pair[fields][0])
        down = 0.5 * (kap + pair[fields][1])
        spread = up + down if spread is None else spread + up + down
        for f in range(fields):
            total = result[f]
            for k in range(fields):
                total = total + conv(k, d, f) * diff[k]
            result[f] = total - up * pair[f][0] - down * pair[f][1]
    return [result[f] + spread * psi[f] for f in range(fields)]


def sweep_kernel(
    adj_ref,
    jac_ref,
    fill_ref,
    face_ref,
    kap_ref,
    src_ref,
    out_hbm,
    edge_ref,
    out_ref,
    out_sems,
):
    fields, planes = adj_ref.shape[:2]
    steps = 4
    cuts = [planes * i // steps for i in range(steps + 1)]
    pieces = [slice(a, b) for a, b in zip(cuts[:-1], cuts[1:])]
    nothing = [jnp.zeros(kap_ref.shape[1:], F32)] * (fields + 1)
    sent = []
    for i, p in enumerate(pieces):
        for x in range(p.start, p.stop):
            def at(y):
                if 0 <= y < planes:
                    return [adj_ref[f, y] for f in range(fields)] + [kap_ref[y]]
                return nothing

            here = at(x)
            planes_of = plane_residual(
                here[:fields],
                here[fields],
                at(x - 1),
                at(x + 1),
                lambda k, f: jac_ref[k, f, x],
                lambda d: face_ref[d, x],
                lambda f: src_ref[f, x],
                lambda k, d, f: fill_ref[k, d, f],
            )
            for f in range(fields):
                out_ref[f, x] = planes_of[f]
            if x in (0, planes - 1):
                e = 0 if x == 0 else 2 * fields + 2
                for f in range(fields):
                    edge_ref[e + f] = planes_of[f]
                    edge_ref[e + fields + f] = here[f]
                edge_ref[e + 2 * fields] = here[fields]
                edge_ref[e + 2 * fields + 1] = face_ref[0, x]
        copy = pltpu.make_async_copy(out_ref.at[:, p], out_hbm.at[:, p], out_sems.at[i])
        copy.start()
        sent.append(copy)
    for k in range(fields):
        for f in range(fields):
            edge_ref[4 * fields + 4 + k * fields + f] = fill_ref[k, 0, f]
    wait_all(sent)


def sum_kernel(
    got_ref,
    edge_ref,
    mate_ref,
    other_ref,
    part_hbm,
    out_ref,
    res_hbm,
    res_ref,
    out_sems,
):
    del part_hbm
    fields, planes = res_hbm.shape[:2]

    def edges():
        even = on_even()
        copies = []
        for e in (0, 1):
            beyond = [
                jnp.where(even == (e == 0), other_ref[f], mate_ref[f]) for f in range(fields + 1)
            ]
            base = e * (2 * fields + 2)
            kap = edge_ref[base + 2 * fields]
            scale = edge_ref[base + 2 * fields + 1] * (0.5 if e else -0.5)
            terms = [scale * beyond[k] for k in range(fields)]
            weight = 0.5 * (kap + beyond[fields])
            extra = 0.5 * beyond[fields]
            for f in range(fields):
                total = edge_ref[base + f] - weight * beyond[f] + extra * edge_ref[base + fields + f]
                for k in range(fields):
                    total = total + edge_ref[4 * fields + 4 + k * fields + f] * terms[k]
                res_ref[e, f] = total
            copies.append(
                pltpu.make_async_copy(res_ref.at[e], res_hbm.at[:, e * (planes - 1)], out_sems.at[e])
            )
        return start_all(copies)

    sources, _, cuts, width = got_ref.shape
    cap = cuts * width
    inner = LAT - 1
    points = lax.broadcasted_iota(jnp.int32, (LAT, cap), 0).astype(F32)
    both = jnp.zeros((6 * LAT, LAT * LAT), F32)
    sent = edges()
    lefts, rights_hi, rights_lo = [], [], []
    for s in range(sources):
        block = jnp.concatenate([got_ref[s, :, i, :] for i in range(cuts)], 1)
        cell = block[6:7]
        first = jnp.floor((cell + 0.5) * (1.0 / (inner * inner)))
        rest = cell - first * (inner * inner)
        second = jnp.floor((rest + 0.5) * (1.0 / inner))
        third = rest - second * inner
        tent = []
        for d, low in enumerate((first, second, third)):
            u = block[3 + d:4 + d]
            tent.append(
                jnp.where(points == low, 1.0 - u, 0.0) + jnp.where(points == low + 1.0, u, 0.0)
            )
        left = jnp.concatenate([tent[0] * block[c:c + 1] for c in range(3)], 0)
        right = jnp.concatenate([tent[1][b:b + 1] * tent[2] for b in range(LAT)], 0)
        lefts.append(jnp.concatenate(split_two(left), 0))
        right_hi, right_lo = split_two(right)
        rights_hi.append(right_hi)
        rights_lo.append(right_lo)
        if len(lefts) == GROUP:
            lhs = jnp.concatenate(lefts, 1)
            for rights in (rights_hi, rights_lo):
                both = both + lax.dot_general(
                    lhs, jnp.concatenate(rights, 1), NT, preferred_element_type=F32
                )
            lefts, rights_hi, rights_lo = [], [], []
    result = both[:3 * LAT] + both[3 * LAT:]
    for c in range(3):
        for a in range(LAT):
            out_ref[c:c + 1, a * LAT * LAT:(a + 1) * LAT * LAT] = result[c * LAT + a:c * LAT + a + 1]
    wait_all(sent)


def local(
    adjoint,
    jac_diag,
    conv_mats,
    face_scale,
    kappa,
    source,
    box_of_row,
    lattice_cell,
    lattice_frac,
    dres_dx,
    dobj_dx,
):
    boxes = lax.axis_size("blk")
    rows = box_of_row.shape[0]
    cap = 2 * rows // boxes
    fields, planes = adjoint.shape[:2]
    plane = adjoint.shape[2:]
    vmem = pl.BlockSpec(memory_space=pltpu.VMEM)
    hbm = pl.BlockSpec(memory_space=pltpu.HBM)
    params = pltpu.CompilerParams(vmem_limit_bytes=SMALL)
    conv = conv_mats.transpose(1, 0, 2)
    box_row = box_of_row.reshape(1, rows)
    cell_row = lattice_cell.reshape(1, rows)
    box_row, cell_row, conv, adjoint, jac_diag, face_scale, kappa, source = stay(
        box_row, cell_row, conv, adjoint, jac_diag, face_scale, kappa, source
    )
    lattice_frac, dres_dx, dobj_dx = stay(lattice_frac, dres_dx, dobj_dx)

    width = min(128, cap)
    payload = (boxes, ROW, cap // width, width)

    def shape(*dims):
        return jax.ShapeDtypeStruct(dims, F32)

    halo = shape(fields + 1, *plane)
    packed, to_mate, to_other, adj, kap, fill, jac, src, face = pl.pallas_call(
        functools.partial(pack_kernel, boxes, cap),
        out_shape=(
            pltpu.VMEM(payload, F32),
            halo,
            halo,
            shape(*adjoint.shape),
            shape(*kappa.shape),
            shape(*conv.shape, *plane),
            shape(*jac_diag.shape),
            shape(*source.shape),
            shape(*face_scale.shape),
        ),
        in_specs=[hbm] * 11,
        out_specs=(vmem,) * 9,
        scratch_shapes=[
            pltpu.SMEM(conv.shape, F32),
            pltpu.VMEM((1, rows), jnp.int32),
            pltpu.VMEM((1, rows), jnp.int32),
            pltpu.VMEM(lattice_frac.shape, F32),
            pltpu.VMEM(dres_dx.shape, F32),
            pltpu.VMEM(dobj_dx.shape, F32),
            pltpu.VMEM((1, rows), F32),
            pltpu.SemaphoreType.DMA((11,)),
        ],
        compiler_params=params,
        name="pack_rows",
    )(
        adjoint,
        kappa,
        box_row,
        cell_row,
        lattice_frac,
        dres_dx,
        dobj_dx,
        conv,
        jac_diag,
        source,
        face_scale,
    )
    got = lax.all_to_all(packed, "blk", 0, 0, axis_index_groups=[spread(boxes)], tiled=True)

    pairs = [(i, i + 1) for i in range(boxes - 1)]
    both_ways = [[p for i, j in pairs if i % 2 == turn for p in ((i, j), (j, i))] for turn in (0, 1)]
    mate = lax.ppermute(to_mate, "blk", both_ways[0])
    other = lax.ppermute(to_other, "blk", both_ways[1])

    inner, edge = pl.pallas_call(
        sweep_kernel,
        out_shape=(
            shape(*adjoint.shape),
            shape(2 * (2 * fields + 2) + fields * fields, *plane),
        ),
        in_specs=[vmem] * 6,
        out_specs=(hbm, vmem),
        scratch_shapes=[
            pltpu.VMEM(adjoint.shape, F32),
            pltpu.SemaphoreType.DMA((4,)),
        ],
        compiler_params=params,
        name="sweep_planes",
    )(adj, jac, fill, face, kap, src)

    box_sens, residual = pl.pallas_call(
        sum_kernel,
        out_shape=(shape(3, LAT**3), shape(*adjoint.shape)),
        in_specs=[vmem] * 4 + [hbm],
        out_specs=(vmem, hbm),
        scratch_shapes=[
            pltpu.VMEM((2, fields) + plane, F32),
            pltpu.SemaphoreType.DMA((2,)),
        ],
        input_output_aliases={4: 1},
        compiler_params=params,
        name="sum_rows",
    )(got, edge, mate, other, inner)
    return residual, box_sens


def solution(mesh):
    in_specs = (
        P("group", "blk", None, None),
        P("group", None, "blk", None, None),
        P(),
        P("group", "blk", None, None),
        P(("group", "blk"), None, None),
        P("group", "blk", None, None),
        P(("group", "blk"), None),
        P(("group", "blk")),
        P(None, ("group", "blk")),
        P(None, None, ("group", "blk")),
        P(None, ("group", "blk")),
    )
    out_specs = (P("group", "blk", None, None), P("group", "blk"))
    return jax.shard_map(local, mesh=mesh, in_specs=in_specs, out_specs=out_specs, check_vma=False)
```

```python
import functools

import jax
import jax.numpy as jnp
from jax import lax
from jax.experimental import pallas as pl
from jax.experimental.pallas import tpu as pltpu
from jax.sharding import PartitionSpec as P

LAT = 16
CHUNK = 256
ROW = 7
SMALL = 12 * 2**20
F32 = jnp.float32
BF16 = jnp.bfloat16
NT = (((1,), (1,)), ((), ()))
NN = (((1,), (0,)), ((), ()))


def split_two(x):
    hi = x.astype(BF16)
    lo = (x - hi.astype(F32)).astype(BF16)
    return hi, lo


def on_even():
    return lax.axis_index("blk") % 2 == 0


def stay(*arrays):
    return [pltpu.with_memory_space_constraint(a, pltpu.HBM) for a in arrays]


def spread(count):
    quarter = count // 4
    order = []
    for k in range(quarter):
        order += [
            k,
            3 * quarter + (k + 2) % quarter,
            quarter + (k + 3) % quarter,
            2 * quarter + (k + 1) % quarter,
        ]
    return order


def start_all(copies):
    for copy in copies:
        copy.start()
    return copies


def wait_all(copies):
    for copy in copies:
        copy.wait()


def pack_kernel(
    boxes,
    cap,
    adj_hbm,
    kap_hbm,
    box_hbm,
    cell_hbm,
    frac_hbm,
    dres_hbm,
    dobj_hbm,
    conv_hbm,
    jac_hbm,
    src_hbm,
    face_hbm,
    out_ref,
    mate_ref,
    other_ref,
    adj_ref,
    kap_ref,
    fill_ref,
    jac_ref,
    src_ref,
    face_ref,
    conv_ref,
    box_ref,
    cell_ref,
    frac_ref,
    dres_ref,
    dobj_ref,
    ranks_ref,
    sems,
):
    fields, planes, _, lanes = adj_hbm.shape
    rows = planes * lanes
    moves = [(box_hbm, box_ref), (dres_hbm, dres_ref), (adj_hbm, adj_ref)]
    moves += [(dobj_hbm, dobj_ref), (frac_hbm, frac_ref), (cell_hbm, cell_ref)]
    moves += [(kap_hbm, kap_ref), (conv_hbm, conv_ref), (jac_hbm, jac_ref)]
    moves += [(src_hbm, src_ref), (face_hbm, face_ref)]
    copies = start_all(
        [pltpu.make_async_copy(src, dst, sems.at[i]) for i, (src, dst) in enumerate(moves)]
    )
    copies[0].wait()
    box = box_ref[...]

    chunks = rows // CHUNK
    names = lax.broadcasted_iota(jnp.int32, (boxes, CHUNK), 0)
    hot = [(box[:, j * CHUNK:(j + 1) * CHUNK] == names).astype(F32) for j in range(chunks)]
    earlier = (
        lax.broadcasted_iota(jnp.int32, (CHUNK, CHUNK), 0)
        < lax.broadcasted_iota(jnp.int32, (CHUNK, CHUNK), 1)
    ).astype(F32).astype(BF16)
    counts = lax.dot_general(
        jnp.concatenate(hot, 0).astype(BF16), earlier, NN, preferred_element_type=F32
    )
    offset = jnp.zeros((boxes, 1), F32)
    for j in range(chunks):
        here = counts[j * boxes:(j + 1) * boxes]
        ranks_ref[:, j * CHUNK:(j + 1) * CHUNK] = jnp.sum(
            hot[j] * (here + offset), axis=0, keepdims=True
        )
        offset = offset + here[:, CHUNK - 1:] + hot[j][:, CHUNK - 1:]

    wait_all(copies[1:7])
    even = on_even()
    for f in range(fields + 1):
        first = adj_ref[f, 0] if f < fields else kap_ref[0]
        last = adj_ref[f, planes - 1] if f < fields else kap_ref[planes - 1]
        mate_ref[f] = jnp.where(even, last, first)
        other_ref[f] = jnp.where(even, first, last)

    total = jnp.zeros((boxes * 16, cap), F32)
    slots = lax.broadcasted_iota(jnp.int32, (cap, CHUNK), 0).astype(F32)
    per = CHUNK // lanes
    for j in range(chunks):
        part = slice(j * CHUNK, (j + 1) * CHUNK)
        acc = dobj_ref[:, part]
        for k in range(fields):
            psi = jnp.concatenate(
                [adj_ref[k, x, 0:1, :] for x in range(j * per, (j + 1) * per)], 1
            )
            acc = acc - dres_ref[k, :, part] * psi
        values = jnp.concatenate(
            [acc, frac_ref[:, part], cell_ref[:, part].astype(F32), jnp.zeros((1, CHUNK), F32)], 0
        )
        hi = values.astype(BF16).astype(F32)
        both = jnp.concatenate([hi, values - hi], 0)
        mine = box[:, part]
        lhs = jnp.concatenate(
            [jnp.where(mine == b, both, 0.0) for b in spread(boxes)], 0
        ).astype(BF16)
        rhs = (slots == ranks_ref[:, part]).astype(F32).astype(BF16)
        total = total + lax.dot_general(lhs, rhs, NT, preferred_element_type=F32)
    width = out_ref.shape[-1]
    for b in range(boxes):
        block = total[b * 16:b * 16 + ROW] + total[b * 16 + 8:b * 16 + 8 + ROW]
        for i in range(cap // width):
            out_ref[b, :, i, :] = block[:, i * width:(i + 1) * width]
    wait_all(copies[7:])
    for k in range(fields):
        for d in range(3):
            for f in range(fields):
                fill_ref[k, d, f] = jnp.full(kap_ref.shape[1:], conv_ref[k, d, f], F32)


def plane_residual(psi, kap, below, above, jac, face, src, conv):
    fields = len(psi)
    rows, lanes = kap.shape
    row = lax.broadcasted_iota(jnp.int32, (rows, lanes), 0)
    lane = lax.broadcasted_iota(jnp.int32, (rows, lanes), 1)
    masks = ((row < rows - 1, row > 0), (lane < lanes - 1, lane > 0))

    def sides(value, dim):
        size = value.shape[dim]
        up = jnp.where(masks[dim][0], pltpu.roll(value, size - 1, dim), 0.0)
        down = jnp.where(masks[dim][1], pltpu.roll(value, 1, dim), 0.0)
        return up, down

    centre = list(psi) + [kap]
    result = []
    for f in range(fields):
        total = jac(0, f) * psi[0]
        for k in range(1, fields):
            total = total + jac(k, f) * psi[k]
        result.append(total - src(f))
    spread = None
    for d in range(3):
        pair = list(zip(above, below)) if d == 0 else [sides(v, d - 1) for v in centre]
        scale = 0.5 * face(d)
        diff = [scale * (pair[k][0] - pair[k][1]) for k in range(fields)]
        up = 0.5 * (kap + pair[fields][0])
        down = 0.5 * (kap + pair[fields][1])
        spread = up + down if spread is None else spread + up + down
        for f in range(fields):
            total = result[f]
            for k in range(fields):
                total = total + conv(k, d, f) * diff[k]
            result[f] = total - up * pair[f][0] - down * pair[f][1]
    return [result[f] + spread * psi[f] for f in range(fields)]


def sweep_kernel(
    adj_ref,
    jac_ref,
    fill_ref,
    face_ref,
    kap_ref,
    src_ref,
    out_hbm,
    edge_ref,
    out_ref,
    out_sems,
):
    fields, planes = adj_ref.shape[:2]
    steps = 4
    cuts = [planes * i // steps for i in range(steps + 1)]
    pieces = [slice(a, b) for a, b in zip(cuts[:-1], cuts[1:])]
    nothing = [jnp.zeros(kap_ref.shape[1:], F32)] * (fields + 1)
    sent = []
    for i, p in enumerate(pieces):
        for x in range(p.start, p.stop):
            def at(y):
                if 0 <= y < planes:
                    return [adj_ref[f, y] for f in range(fields)] + [kap_ref[y]]
                return nothing

            here = at(x)
            planes_of = plane_residual(
                here[:fields],
                here[fields],
                at(x - 1),
                at(x + 1),
                lambda k, f: jac_ref[k, f, x],
                lambda d: face_ref[d, x],
                lambda f: src_ref[f, x],
                lambda k, d, f: fill_ref[k, d, f],
            )
            for f in range(fields):
                out_ref[f, x] = planes_of[f]
            if x in (0, planes - 1):
                e = 0 if x == 0 else 2 * fields + 2
                for f in range(fields):
                    edge_ref[e + f] = planes_of[f]
                    edge_ref[e + fields + f] = here[f]
                edge_ref[e + 2 * fields] = here[fields]
                edge_ref[e + 2 * fields + 1] = face_ref[0, x]
        copy = pltpu.make_async_copy(out_ref.at[:, p], out_hbm.at[:, p], out_sems.at[i])
        copy.start()
        sent.append(copy)
    for k in range(fields):
        for f in range(fields):
            edge_ref[4 * fields + 4 + k * fields + f] = fill_ref[k, 0, f]
    wait_all(sent)


def sum_kernel(
    got_ref,
    edge_ref,
    mate_ref,
    other_ref,
    part_hbm,
    out_ref,
    res_hbm,
    res_ref,
    out_sems,
):
    del part_hbm
    fields, planes = res_hbm.shape[:2]

    def edges():
        even = on_even()
        copies = []
        for e in (0, 1):
            beyond = [
                jnp.where(even == (e == 0), other_ref[f], mate_ref[f]) for f in range(fields + 1)
            ]
            base = e * (2 * fields + 2)
            kap = edge_ref[base + 2 * fields]
            scale = edge_ref[base + 2 * fields + 1] * (0.5 if e else -0.5)
            terms = [scale * beyond[k] for k in range(fields)]
            weight = 0.5 * (kap + beyond[fields])
            extra = 0.5 * beyond[fields]
            for f in range(fields):
                total = edge_ref[base + f] - weight * beyond[f] + extra * edge_ref[base + fields + f]
                for k in range(fields):
                    total = total + edge_ref[4 * fields + 4 + k * fields + f] * terms[k]
                res_ref[e, f] = total
            copies.append(
                pltpu.make_async_copy(res_ref.at[e], res_hbm.at[:, e * (planes - 1)], out_sems.at[e])
            )
        return start_all(copies)

    sources, _, cuts, width = got_ref.shape
    cap = cuts * width
    inner = LAT - 1
    points = lax.broadcasted_iota(jnp.int32, (LAT, cap), 0).astype(F32)
    both = jnp.zeros((6 * LAT, LAT * LAT), F32)
    for s in range(sources):
        if s == sources // 4:
            sent = edges()
        block = jnp.concatenate([got_ref[s, :, i, :] for i in range(cuts)], 1)
        cell = block[6:7]
        first = jnp.floor((cell + 0.5) * (1.0 / (inner * inner)))
        rest = cell - first * (inner * inner)
        second = jnp.floor((rest + 0.5) * (1.0 / inner))
        third = rest - second * inner
        tent = []
        for d, low in enumerate((first, second, third)):
            u = block[3 + d:4 + d]
            tent.append(
                jnp.where(points == low, 1.0 - u, 0.0) + jnp.where(points == low + 1.0, u, 0.0)
            )
        left = jnp.concatenate([tent[0] * block[c:c + 1] for c in range(3)], 0)
        right = jnp.concatenate([tent[1][b:b + 1] * tent[2] for b in range(LAT)], 0)
        left_hi, left_lo = split_two(left)
        right_hi, right_lo = split_two(right)
        lhs = jnp.concatenate([left_hi, left_lo], 0)
        both = both + lax.dot_general(lhs, right_hi, NT, preferred_element_type=F32)
        both = both + lax.dot_general(lhs, right_lo, NT, preferred_element_type=F32)
    result = both[:3 * LAT] + both[3 * LAT:]
    for c in range(3):
        for a in range(LAT):
            out_ref[c:c + 1, a * LAT * LAT:(a + 1) * LAT * LAT] = result[c * LAT + a:c * LAT + a + 1]
    wait_all(sent)


def local(
    adjoint,
    jac_diag,
    conv_mats,
    face_scale,
    kappa,
    source,
    box_of_row,
    lattice_cell,
    lattice_frac,
    dres_dx,
    dobj_dx,
):
    boxes = lax.axis_size("blk")
    rows = box_of_row.shape[0]
    cap = 2 * rows // boxes
    fields, planes = adjoint.shape[:2]
    plane = adjoint.shape[2:]
    vmem = pl.BlockSpec(memory_space=pltpu.VMEM)
    hbm = pl.BlockSpec(memory_space=pltpu.HBM)
    params = pltpu.CompilerParams(vmem_limit_bytes=SMALL)
    conv = conv_mats.transpose(1, 0, 2)
    box_row = box_of_row.reshape(1, rows)
    cell_row = lattice_cell.reshape(1, rows)
    box_row, cell_row, conv, adjoint, jac_diag, face_scale, kappa, source = stay(
        box_row, cell_row, conv, adjoint, jac_diag, face_scale, kappa, source
    )
    lattice_frac, dres_dx, dobj_dx = stay(lattice_frac, dres_dx, dobj_dx)

    width = min(128, cap)
    payload = (boxes, ROW, cap // width, width)

    def shape(*dims):
        return jax.ShapeDtypeStruct(dims, F32)

    halo = shape(fields + 1, *plane)
    packed, to_mate, to_other, adj, kap, fill, jac, src, face = pl.pallas_call(
        functools.partial(pack_kernel, boxes, cap),
        out_shape=(
            shape(*payload),
            halo,
            halo,
            shape(*adjoint.shape),
            shape(*kappa.shape),
            shape(*conv.shape, *plane),
            shape(*jac_diag.shape),
            shape(*source.shape),
            shape(*face_scale.shape),
        ),
        in_specs=[hbm] * 11,
        out_specs=(vmem,) * 9,
        scratch_shapes=[
            pltpu.SMEM(conv.shape, F32),
            pltpu.VMEM((1, rows), jnp.int32),
            pltpu.VMEM((1, rows), jnp.int32),
            pltpu.VMEM(lattice_frac.shape, F32),
            pltpu.VMEM(dres_dx.shape, F32),
            pltpu.VMEM(dobj_dx.shape, F32),
            pltpu.VMEM((1, rows), F32),
            pltpu.SemaphoreType.DMA((11,)),
        ],
        compiler_params=params,
        name="pack_rows",
    )(
        adjoint,
        kappa,
        box_row,
        cell_row,
        lattice_frac,
        dres_dx,
        dobj_dx,
        conv,
        jac_diag,
        source,
        face_scale,
    )
    got = lax.all_to_all(packed, "blk", 0, 0, axis_index_groups=[spread(boxes)], tiled=True)

    pairs = [(i, i + 1) for i in range(boxes - 1)]
    both_ways = [[p for i, j in pairs if i % 2 == turn for p in ((i, j), (j, i))] for turn in (0, 1)]
    mate = lax.ppermute(to_mate, "blk", both_ways[0])
    other = lax.ppermute(to_other, "blk", both_ways[1])

    inner, edge = pl.pallas_call(
        sweep_kernel,
        out_shape=(
            shape(*adjoint.shape),
            shape(2 * (2 * fields + 2) + fields * fields, *plane),
        ),
        in_specs=[vmem] * 6,
        out_specs=(hbm, vmem),
        scratch_shapes=[
            pltpu.VMEM(adjoint.shape, F32),
            pltpu.SemaphoreType.DMA((4,)),
        ],
        compiler_params=params,
        name="sweep_planes",
    )(adj, jac, fill, face, kap, src)

    box_sens, residual = pl.pallas_call(
        sum_kernel,
        out_shape=(shape(3, LAT**3), shape(*adjoint.shape)),
        in_specs=[vmem] * 4 + [hbm],
        out_specs=(vmem, hbm),
        scratch_shapes=[
            pltpu.VMEM((2, fields) + plane, F32),
            pltpu.SemaphoreType.DMA((2,)),
        ],
        input_output_aliases={4: 1},
        compiler_params=params,
        name="sum_rows",
    )(got, edge, mate, other, inner)
    return residual, box_sens


def solution(mesh):
    in_specs = (
        P("group", "blk", None, None),
        P("group", None, "blk", None, None),
        P(),
        P("group", "blk", None, None),
        P(("group", "blk"), None, None),
        P("group", "blk", None, None),
        P(("group", "blk"), None),
        P(("group", "blk")),
        P(None, ("group", "blk")),
        P(None, None, ("group", "blk")),
        P(None, ("group", "blk")),
    )
    out_specs = (P("group", "blk", None, None), P("group", "blk"))
    return jax.shard_map(local, mesh=mesh, in_specs=in_specs, out_specs=out_specs, check_vma=False)
```

```python
import functools

import jax
import jax.numpy as jnp
from jax import lax
from jax.experimental import pallas as pl
from jax.experimental.pallas import tpu as pltpu
from jax.sharding import PartitionSpec as P

LAT = 16
CHUNK = 256
ROW = 7
SMALL = 12 * 2**20
F32 = jnp.float32
BF16 = jnp.bfloat16
NT = (((1,), (1,)), ((), ()))
NN = (((1,), (0,)), ((), ()))


def split_two(x):
    hi = x.astype(BF16)
    lo = (x - hi.astype(F32)).astype(BF16)
    return hi, lo


def on_even():
    return lax.axis_index("blk") % 2 == 0


def stay(*arrays):
    return [pltpu.with_memory_space_constraint(a, pltpu.HBM) for a in arrays]


def spread(count):
    quarter = count // 4
    order = []
    for k in range(quarter):
        order += [
            count - 1 - k,
            (k + 2) % quarter,
            2 * quarter + (k + 3) % quarter,
            quarter + (k + 1) % quarter,
        ]
    return order


def start_all(copies):
    for copy in copies:
        copy.start()
    return copies


def wait_all(copies):
    for copy in copies:
        copy.wait()


def pack_kernel(
    boxes,
    cap,
    adj_hbm,
    kap_hbm,
    box_hbm,
    cell_hbm,
    frac_hbm,
    dres_hbm,
    dobj_hbm,
    conv_hbm,
    jac_hbm,
    src_hbm,
    face_hbm,
    out_ref,
    mate_ref,
    other_ref,
    adj_ref,
    kap_ref,
    fill_ref,
    jac_ref,
    src_ref,
    face_ref,
    conv_ref,
    box_ref,
    cell_ref,
    frac_ref,
    dres_ref,
    dobj_ref,
    ranks_ref,
    sems,
):
    fields, planes, _, lanes = adj_hbm.shape
    rows = planes * lanes
    moves = [(box_hbm, box_ref), (dres_hbm, dres_ref), (adj_hbm, adj_ref)]
    moves += [(dobj_hbm, dobj_ref), (frac_hbm, frac_ref), (cell_hbm, cell_ref)]
    moves += [(kap_hbm, kap_ref), (conv_hbm, conv_ref), (jac_hbm, jac_ref)]
    moves += [(src_hbm, src_ref), (face_hbm, face_ref)]
    copies = start_all(
        [pltpu.make_async_copy(src, dst, sems.at[i]) for i, (src, dst) in enumerate(moves)]
    )
    copies[0].wait()
    box = box_ref[...]

    chunks = rows // CHUNK
    names = lax.broadcasted_iota(jnp.int32, (boxes, CHUNK), 0)
    hot = [(box[:, j * CHUNK:(j + 1) * CHUNK] == names).astype(F32) for j in range(chunks)]
    earlier = (
        lax.broadcasted_iota(jnp.int32, (CHUNK, CHUNK), 0)
        < lax.broadcasted_iota(jnp.int32, (CHUNK, CHUNK), 1)
    ).astype(F32).astype(BF16)
    counts = lax.dot_general(
        jnp.concatenate(hot, 0).astype(BF16), earlier, NN, preferred_element_type=F32
    )
    offset = jnp.zeros((boxes, 1), F32)
    for j in range(chunks):
        here = counts[j * boxes:(j + 1) * boxes]
        ranks_ref[:, j * CHUNK:(j + 1) * CHUNK] = jnp.sum(
            hot[j] * (here + offset), axis=0, keepdims=True
        )
        offset = offset + here[:, CHUNK - 1:] + hot[j][:, CHUNK - 1:]

    wait_all(copies[1:7])
    even = on_even()
    for f in range(fields + 1):
        first = adj_ref[f, 0] if f < fields else kap_ref[0]
        last = adj_ref[f, planes - 1] if f < fields else kap_ref[planes - 1]
        mate_ref[f] = jnp.where(even, last, first)
        other_ref[f] = jnp.where(even, first, last)

    total = jnp.zeros((boxes * 16, cap), F32)
    slots = lax.broadcasted_iota(jnp.int32, (cap, CHUNK), 0).astype(F32)
    per = CHUNK // lanes
    for j in range(chunks):
        part = slice(j * CHUNK, (j + 1) * CHUNK)
        acc = dobj_ref[:, part]
        for k in range(fields):
            psi = jnp.concatenate(
                [adj_ref[k, x, 0:1, :] for x in range(j * per, (j + 1) * per)], 1
            )
            acc = acc - dres_ref[k, :, part] * psi
        values = jnp.concatenate(
            [acc, frac_ref[:, part], cell_ref[:, part].astype(F32), jnp.zeros((1, CHUNK), F32)], 0
        )
        hi = values.astype(BF16).astype(F32)
        both = jnp.concatenate([hi, values - hi], 0)
        mine = box[:, part]
        lhs = jnp.concatenate(
            [jnp.where(mine == b, both, 0.0) for b in spread(boxes)], 0
        ).astype(BF16)
        rhs = (slots == ranks_ref[:, part]).astype(F32).astype(BF16)
        total = total + lax.dot_general(lhs, rhs, NT, preferred_element_type=F32)
    width = out_ref.shape[-1]
    for b in range(boxes):
        block = total[b * 16:b * 16 + ROW] + total[b * 16 + 8:b * 16 + 8 + ROW]
        for i in range(cap // width):
            out_ref[b, :, i, :] = block[:, i * width:(i + 1) * width]
    wait_all(copies[7:])
    for k in range(fields):
        for d in range(3):
            for f in range(fields):
                fill_ref[k, d, f] = jnp.full(kap_ref.shape[1:], conv_ref[k, d, f], F32)


def plane_residual(psi, kap, below, above, jac, face, src, conv):
    fields = len(psi)
    rows, lanes = kap.shape
    row = lax.broadcasted_iota(jnp.int32, (rows, lanes), 0)
    lane = lax.broadcasted_iota(jnp.int32, (rows, lanes), 1)
    masks = ((row < rows - 1, row > 0), (lane < lanes - 1, lane > 0))

    def sides(value, dim):
        size = value.shape[dim]
        up = jnp.where(masks[dim][0], pltpu.roll(value, size - 1, dim), 0.0)
        down = jnp.where(masks[dim][1], pltpu.roll(value, 1, dim), 0.0)
        return up, down

    centre = list(psi) + [kap]
    result = []
    for f in range(fields):
        total = jac(0, f) * psi[0]
        for k in range(1, fields):
            total = total + jac(k, f) * psi[k]
        result.append(total - src(f))
    spread = None
    for d in range(3):
        pair = list(zip(above, below)) if d == 0 else [sides(v, d - 1) for v in centre]
        scale = 0.5 * face(d)
        diff = [scale * (pair[k][0] - pair[k][1]) for k in range(fields)]
        up = 0.5 * (kap + pair[fields][0])
        down = 0.5 * (kap + pair[fields][1])
        spread = up + down if spread is None else spread + up + down
        for f in range(fields):
            total = result[f]
            for k in range(fields):
                total = total + conv(k, d, f) * diff[k]
            result[f] = total - up * pair[f][0] - down * pair[f][1]
    return [result[f] + spread * psi[f] for f in range(fields)]


def sweep_kernel(
    adj_ref,
    jac_ref,
    fill_ref,
    face_ref,
    kap_ref,
    src_ref,
    out_hbm,
    edge_ref,
    out_ref,
    out_sems,
):
    fields, planes = adj_ref.shape[:2]
    steps = 4
    cuts = [planes * i // steps for i in range(steps + 1)]
    pieces = [slice(a, b) for a, b in zip(cuts[:-1], cuts[1:])]
    nothing = [jnp.zeros(kap_ref.shape[1:], F32)] * (fields + 1)
    sent = []
    for i, p in enumerate(pieces):
        for x in range(p.start, p.stop):
            def at(y):
                if 0 <= y < planes:
                    return [adj_ref[f, y] for f in range(fields)] + [kap_ref[y]]
                return nothing

            here = at(x)
            planes_of = plane_residual(
                here[:fields],
                here[fields],
                at(x - 1),
                at(x + 1),
                lambda k, f: jac_ref[k, f, x],
                lambda d: face_ref[d, x],
                lambda f: src_ref[f, x],
                lambda k, d, f: fill_ref[k, d, f],
            )
            for f in range(fields):
                out_ref[f, x] = planes_of[f]
            if x in (0, planes - 1):
                e = 0 if x == 0 else 2 * fields + 2
                for f in range(fields):
                    edge_ref[e + f] = planes_of[f]
                    edge_ref[e + fields + f] = here[f]
                edge_ref[e + 2 * fields] = here[fields]
                edge_ref[e + 2 * fields + 1] = face_ref[0, x]
        copy = pltpu.make_async_copy(out_ref.at[:, p], out_hbm.at[:, p], out_sems.at[i])
        copy.start()
        sent.append(copy)
    for k in range(fields):
        for f in range(fields):
            edge_ref[4 * fields + 4 + k * fields + f] = fill_ref[k, 0, f]
    wait_all(sent)


def edge_kernel(edge_ref, mate_ref, other_ref, after_ref, part_hbm, res_hbm, res_ref, out_sems):
    del after_ref, part_hbm
    fields, planes = res_hbm.shape[:2]
    even = on_even()
    copies = []
    for e in (0, 1):
        beyond = [jnp.where(even == (e == 0), other_ref[f], mate_ref[f]) for f in range(fields + 1)]
        base = e * (2 * fields + 2)
        kap = edge_ref[base + 2 * fields]
        scale = edge_ref[base + 2 * fields + 1] * (0.5 if e else -0.5)
        terms = [scale * beyond[k] for k in range(fields)]
        weight = 0.5 * (kap + beyond[fields])
        extra = 0.5 * beyond[fields]
        for f in range(fields):
            total = edge_ref[base + f] - weight * beyond[f] + extra * edge_ref[base + fields + f]
            for k in range(fields):
                total = total + edge_ref[4 * fields + 4 + k * fields + f] * terms[k]
            res_ref[e, f] = total
        copy = pltpu.make_async_copy(res_ref.at[e], res_hbm.at[:, e * (planes - 1)], out_sems.at[e])
        copy.start()
        copies.append(copy)
    wait_all(copies)


def sum_kernel(got_ref, out_ref):
    sources, _, cuts, width = got_ref.shape
    cap = cuts * width
    inner = LAT - 1
    points = lax.broadcasted_iota(jnp.int32, (LAT, cap), 0).astype(F32)
    both = jnp.zeros((6 * LAT, LAT * LAT), F32)
    for s in range(sources):
        block = jnp.concatenate([got_ref[s, :, i, :] for i in range(cuts)], 1)
        cell = block[6:7]
        first = jnp.floor((cell + 0.5) * (1.0 / (inner * inner)))
        rest = cell - first * (inner * inner)
        second = jnp.floor((rest + 0.5) * (1.0 / inner))
        third = rest - second * inner
        tent = []
        for d, low in enumerate((first, second, third)):
            u = block[3 + d:4 + d]
            tent.append(
                jnp.where(points == low, 1.0 - u, 0.0) + jnp.where(points == low + 1.0, u, 0.0)
            )
        left = jnp.concatenate([tent[0] * block[c:c + 1] for c in range(3)], 0)
        right = jnp.concatenate([tent[1][b:b + 1] * tent[2] for b in range(LAT)], 0)
        left_hi, left_lo = split_two(left)
        right_hi, right_lo = split_two(right)
        lhs = jnp.concatenate([left_hi, left_lo], 0)
        both = both + lax.dot_general(lhs, right_hi, NT, preferred_element_type=F32)
        both = both + lax.dot_general(lhs, right_lo, NT, preferred_element_type=F32)
    result = both[:3 * LAT] + both[3 * LAT:]
    for c in range(3):
        for a in range(LAT):
            out_ref[c:c + 1, a * LAT * LAT:(a + 1) * LAT * LAT] = result[c * LAT + a:c * LAT + a + 1]


def local(
    adjoint,
    jac_diag,
    conv_mats,
    face_scale,
    kappa,
    source,
    box_of_row,
    lattice_cell,
    lattice_frac,
    dres_dx,
    dobj_dx,
):
    boxes = lax.axis_size("blk")
    rows = box_of_row.shape[0]
    cap = 2 * rows // boxes
    fields, planes = adjoint.shape[:2]
    plane = adjoint.shape[2:]
    vmem = pl.BlockSpec(memory_space=pltpu.VMEM)
    hbm = pl.BlockSpec(memory_space=pltpu.HBM)
    params = pltpu.CompilerParams(vmem_limit_bytes=SMALL)
    conv = conv_mats.transpose(1, 0, 2)
    box_row = box_of_row.reshape(1, rows)
    cell_row = lattice_cell.reshape(1, rows)
    box_row, cell_row, conv, adjoint, jac_diag, face_scale, kappa, source = stay(
        box_row, cell_row, conv, adjoint, jac_diag, face_scale, kappa, source
    )
    lattice_frac, dres_dx, dobj_dx = stay(lattice_frac, dres_dx, dobj_dx)

    width = min(128, cap)
    payload = (boxes, ROW, cap // width, width)

    def shape(*dims):
        return jax.ShapeDtypeStruct(dims, F32)

    halo = shape(fields + 1, *plane)
    packed, to_mate, to_other, adj, kap, fill, jac, src, face = pl.pallas_call(
        functools.partial(pack_kernel, boxes, cap),
        out_shape=(
            shape(*payload),
            halo,
            halo,
            shape(*adjoint.shape),
            shape(*kappa.shape),
            shape(*conv.shape, *plane),
            shape(*jac_diag.shape),
            shape(*source.shape),
            shape(*face_scale.shape),
        ),
        in_specs=[hbm] * 11,
        out_specs=(vmem,) * 9,
        scratch_shapes=[
            pltpu.SMEM(conv.shape, F32),
            pltpu.VMEM((1, rows), jnp.int32),
            pltpu.VMEM((1, rows), jnp.int32),
            pltpu.VMEM(lattice_frac.shape, F32),
            pltpu.VMEM(dres_dx.shape, F32),
            pltpu.VMEM(dobj_dx.shape, F32),
            pltpu.VMEM((1, rows), F32),
            pltpu.SemaphoreType.DMA((11,)),
        ],
        compiler_params=params,
        name="pack_rows",
    )(
        adjoint,
        kappa,
        box_row,
        cell_row,
        lattice_frac,
        dres_dx,
        dobj_dx,
        conv,
        jac_diag,
        source,
        face_scale,
    )
    got = lax.all_to_all(packed, "blk", 0, 0, axis_index_groups=[spread(boxes)], tiled=True)

    pairs = [(i, i + 1) for i in range(boxes - 1)]
    both_ways = [[p for i, j in pairs if i % 2 == turn for p in ((i, j), (j, i))] for turn in (0, 1)]
    mate = lax.ppermute(to_mate, "blk", both_ways[0])
    other = lax.ppermute(to_other, "blk", both_ways[1])

    inner, edge = pl.pallas_call(
        sweep_kernel,
        out_shape=(
            shape(*adjoint.shape),
            shape(2 * (2 * fields + 2) + fields * fields, *plane),
        ),
        in_specs=[vmem] * 6,
        out_specs=(hbm, vmem),
        scratch_shapes=[
            pltpu.VMEM(adjoint.shape, F32),
            pltpu.SemaphoreType.DMA((4,)),
        ],
        compiler_params=params,
        name="sweep_planes",
    )(adj, jac, fill, face, kap, src)

    box_sens = pl.pallas_call(
        sum_kernel,
        out_shape=shape(3, LAT**3),
        in_specs=[vmem],
        out_specs=vmem,
        compiler_params=params,
        name="sum_rows",
    )(got)

    residual = pl.pallas_call(
        edge_kernel,
        out_shape=shape(*adjoint.shape),
        in_specs=[vmem] * 3 + [pl.BlockSpec(memory_space=pl.ANY), hbm],
        out_specs=hbm,
        scratch_shapes=[
            pltpu.VMEM((2, fields) + plane, F32),
            pltpu.SemaphoreType.DMA((2,)),
        ],
        input_output_aliases={4: 0},
        compiler_params=params,
        name="edge_planes",
    )(edge, mate, other, box_sens, inner)
    return residual, box_sens


def solution(mesh):
    in_specs = (
        P("group", "blk", None, None),
        P("group", None, "blk", None, None),
        P(),
        P("group", "blk", None, None),
        P(("group", "blk"), None, None),
        P("group", "blk", None, None),
        P(("group", "blk"), None),
        P(("group", "blk")),
        P(None, ("group", "blk")),
        P(None, None, ("group", "blk")),
        P(None, ("group", "blk")),
    )
    out_specs = (P("group", "blk", None, None), P("group", "blk"))
    return jax.shard_map(local, mesh=mesh, in_specs=in_specs, out_specs=out_specs, check_vma=False)
```

```python
import functools

import jax
import jax.numpy as jnp
from jax import lax
from jax.experimental import pallas as pl
from jax.experimental.pallas import tpu as pltpu
from jax.sharding import PartitionSpec as P

LAT = 16
CHUNK = 256
ROW = 7
SMALL = 12 * 2**20
F32 = jnp.float32
BF16 = jnp.bfloat16
NT = (((1,), (1,)), ((), ()))
NN = (((1,), (0,)), ((), ()))


def split_two(x):
    hi = x.astype(BF16)
    lo = (x - hi.astype(F32)).astype(BF16)
    return hi, lo


def on_even():
    return lax.axis_index("blk") % 2 == 0


def stay(*arrays):
    return [pltpu.with_memory_space_constraint(a, pltpu.HBM) for a in arrays]


def spread(count):
    quarter = count // 4
    order = []
    for k in range(quarter):
        order += [
            count - 1 - k,
            (k + 2) % quarter,
            2 * quarter + (k + 3) % quarter,
            quarter + (k + 1) % quarter,
        ]
    return order


def start_all(copies):
    for copy in copies:
        copy.start()
    return copies


def wait_all(copies):
    for copy in copies:
        copy.wait()


def pack_kernel(
    boxes,
    cap,
    adj_hbm,
    kap_hbm,
    box_hbm,
    cell_hbm,
    frac_hbm,
    dres_hbm,
    dobj_hbm,
    conv_hbm,
    jac_hbm,
    src_hbm,
    face_hbm,
    out_hbm,
    mate_ref,
    other_ref,
    adj_ref,
    kap_ref,
    fill_ref,
    jac_ref,
    src_ref,
    face_ref,
    out_ref,
    conv_ref,
    box_ref,
    cell_ref,
    frac_ref,
    dres_ref,
    dobj_ref,
    ranks_ref,
    sems,
    out_sem,
):
    fields, planes, _, lanes = adj_hbm.shape
    rows = planes * lanes
    moves = [(box_hbm, box_ref), (dres_hbm, dres_ref), (adj_hbm, adj_ref)]
    moves += [(dobj_hbm, dobj_ref), (frac_hbm, frac_ref), (cell_hbm, cell_ref)]
    moves += [(kap_hbm, kap_ref), (conv_hbm, conv_ref), (jac_hbm, jac_ref)]
    moves += [(src_hbm, src_ref), (face_hbm, face_ref)]
    copies = start_all(
        [pltpu.make_async_copy(src, dst, sems.at[i]) for i, (src, dst) in enumerate(moves)]
    )
    copies[0].wait()
    box = box_ref[...]

    chunks = rows // CHUNK
    names = lax.broadcasted_iota(jnp.int32, (boxes, CHUNK), 0)
    hot = [(box[:, j * CHUNK:(j + 1) * CHUNK] == names).astype(F32) for j in range(chunks)]
    earlier = (
        lax.broadcasted_iota(jnp.int32, (CHUNK, CHUNK), 0)
        < lax.broadcasted_iota(jnp.int32, (CHUNK, CHUNK), 1)
    ).astype(F32).astype(BF16)
    counts = lax.dot_general(
        jnp.concatenate(hot, 0).astype(BF16), earlier, NN, preferred_element_type=F32
    )
    offset = jnp.zeros((boxes, 1), F32)
    for j in range(chunks):
        here = counts[j * boxes:(j + 1) * boxes]
        ranks_ref[:, j * CHUNK:(j + 1) * CHUNK] = jnp.sum(
            hot[j] * (here + offset), axis=0, keepdims=True
        )
        offset = offset + here[:, CHUNK - 1:] + hot[j][:, CHUNK - 1:]

    wait_all(copies[1:7])
    even = on_even()
    for f in range(fields + 1):
        first = adj_ref[f, 0] if f < fields else kap_ref[0]
        last = adj_ref[f, planes - 1] if f < fields else kap_ref[planes - 1]
        mate_ref[f] = jnp.where(even, last, first)
        other_ref[f] = jnp.where(even, first, last)

    total = jnp.zeros((boxes * 16, cap), F32)
    slots = lax.broadcasted_iota(jnp.int32, (cap, CHUNK), 0).astype(F32)
    per = CHUNK // lanes
    for j in range(chunks):
        part = slice(j * CHUNK, (j + 1) * CHUNK)
        acc = dobj_ref[:, part]
        for k in range(fields):
            psi = jnp.concatenate(
                [adj_ref[k, x, 0:1, :] for x in range(j * per, (j + 1) * per)], 1
            )
            acc = acc - dres_ref[k, :, part] * psi
        values = jnp.concatenate(
            [acc, frac_ref[:, part], cell_ref[:, part].astype(F32), jnp.zeros((1, CHUNK), F32)], 0
        )
        hi = values.astype(BF16).astype(F32)
        both = jnp.concatenate([hi, values - hi], 0)
        mine = box[:, part]
        lhs = jnp.concatenate(
            [jnp.where(mine == b, both, 0.0) for b in spread(boxes)], 0
        ).astype(BF16)
        rhs = (slots == ranks_ref[:, part]).astype(F32).astype(BF16)
        total = total + lax.dot_general(lhs, rhs, NT, preferred_element_type=F32)
    width = out_ref.shape[-1]
    for b in range(boxes):
        block = total[b * 16:b * 16 + ROW] + total[b * 16 + 8:b * 16 + 8 + ROW]
        for i in range(cap // width):
            out_ref[b, :, i, :] = block[:, i * width:(i + 1) * width]
    out_copy = pltpu.make_async_copy(out_ref, out_hbm, out_sem)
    out_copy.start()
    wait_all(copies[7:])
    for k in range(fields):
        for d in range(3):
            for f in range(fields):
                fill_ref[k, d, f] = jnp.full(kap_ref.shape[1:], conv_ref[k, d, f], F32)
    out_copy.wait()


def plane_residual(psi, kap, below, above, jac, face, src, conv):
    fields = len(psi)
    rows, lanes = kap.shape
    row = lax.broadcasted_iota(jnp.int32, (rows, lanes), 0)
    lane = lax.broadcasted_iota(jnp.int32, (rows, lanes), 1)
    masks = ((row < rows - 1, row > 0), (lane < lanes - 1, lane > 0))

    def sides(value, dim):
        size = value.shape[dim]
        up = jnp.where(masks[dim][0], pltpu.roll(value, size - 1, dim), 0.0)
        down = jnp.where(masks[dim][1], pltpu.roll(value, 1, dim), 0.0)
        return up, down

    centre = list(psi) + [kap]
    result = []
    for f in range(fields):
        total = jac(0, f) * psi[0]
        for k in range(1, fields):
            total = total + jac(k, f) * psi[k]
        result.append(total - src(f))
    spread = None
    for d in range(3):
        pair = list(zip(above, below)) if d == 0 else [sides(v, d - 1) for v in centre]
        scale = 0.5 * face(d)
        diff = [scale * (pair[k][0] - pair[k][1]) for k in range(fields)]
        up = 0.5 * (kap + pair[fields][0])
        down = 0.5 * (kap + pair[fields][1])
        spread = up + down if spread is None else spread + up + down
        for f in range(fields):
            total = result[f]
            for k in range(fields):
                total = total + conv(k, d, f) * diff[k]
            result[f] = total - up * pair[f][0] - down * pair[f][1]
    return [result[f] + spread * psi[f] for f in range(fields)]


def sweep_kernel(
    adj_ref,
    jac_ref,
    fill_ref,
    face_ref,
    kap_ref,
    src_ref,
    out_hbm,
    edge_ref,
    out_ref,
    out_sems,
):
    fields, planes = adj_ref.shape[:2]
    steps = 4
    cuts = [planes * i // steps for i in range(steps + 1)]
    pieces = [slice(a, b) for a, b in zip(cuts[:-1], cuts[1:])]
    nothing = [jnp.zeros(kap_ref.shape[1:], F32)] * (fields + 1)
    sent = []
    for i, p in enumerate(pieces):
        for x in range(p.start, p.stop):
            def at(y):
                if 0 <= y < planes:
                    return [adj_ref[f, y] for f in range(fields)] + [kap_ref[y]]
                return nothing

            here = at(x)
            planes_of = plane_residual(
                here[:fields],
                here[fields],
                at(x - 1),
                at(x + 1),
                lambda k, f: jac_ref[k, f, x],
                lambda d: face_ref[d, x],
                lambda f: src_ref[f, x],
                lambda k, d, f: fill_ref[k, d, f],
            )
            for f in range(fields):
                out_ref[f, x] = planes_of[f]
            if x in (0, planes - 1):
                e = 0 if x == 0 else 2 * fields + 2
                for f in range(fields):
                    edge_ref[e + f] = planes_of[f]
                    edge_ref[e + fields + f] = here[f]
                edge_ref[e + 2 * fields] = here[fields]
                edge_ref[e + 2 * fields + 1] = face_ref[0, x]
        copy = pltpu.make_async_copy(out_ref.at[:, p], out_hbm.at[:, p], out_sems.at[i])
        copy.start()
        sent.append(copy)
    for k in range(fields):
        for f in range(fields):
            edge_ref[4 * fields + 4 + k * fields + f] = fill_ref[k, 0, f]
    wait_all(sent)


def edge_kernel(edge_ref, mate_ref, other_ref, after_ref, part_hbm, res_hbm, res_ref, out_sems):
    del after_ref, part_hbm
    fields, planes = res_hbm.shape[:2]
    even = on_even()
    copies = []
    for e in (0, 1):
        beyond = [jnp.where(even == (e == 0), other_ref[f], mate_ref[f]) for f in range(fields + 1)]
        base = e * (2 * fields + 2)
        kap = edge_ref[base + 2 * fields]
        scale = edge_ref[base + 2 * fields + 1] * (0.5 if e else -0.5)
        terms = [scale * beyond[k] for k in range(fields)]
        weight = 0.5 * (kap + beyond[fields])
        extra = 0.5 * beyond[fields]
        for f in range(fields):
            total = edge_ref[base + f] - weight * beyond[f] + extra * edge_ref[base + fields + f]
            for k in range(fields):
                total = total + edge_ref[4 * fields + 4 + k * fields + f] * terms[k]
            res_ref[e, f] = total
        copy = pltpu.make_async_copy(res_ref.at[e], res_hbm.at[:, e * (planes - 1)], out_sems.at[e])
        copy.start()
        copies.append(copy)
    wait_all(copies)


def sum_kernel(got_ref, out_ref):
    sources, _, cuts, width = got_ref.shape
    cap = cuts * width
    inner = LAT - 1
    points = lax.broadcasted_iota(jnp.int32, (LAT, cap), 0).astype(F32)
    both = jnp.zeros((6 * LAT, LAT * LAT), F32)
    for s in range(sources):
        block = jnp.concatenate([got_ref[s, :, i, :] for i in range(cuts)], 1)
        cell = block[6:7]
        first = jnp.floor((cell + 0.5) * (1.0 / (inner * inner)))
        rest = cell - first * (inner * inner)
        second = jnp.floor((rest + 0.5) * (1.0 / inner))
        third = rest - second * inner
        tent = []
        for d, low in enumerate((first, second, third)):
            u = block[3 + d:4 + d]
            tent.append(
                jnp.where(points == low, 1.0 - u, 0.0) + jnp.where(points == low + 1.0, u, 0.0)
            )
        left = jnp.concatenate([tent[0] * block[c:c + 1] for c in range(3)], 0)
        right = jnp.concatenate([tent[1][b:b + 1] * tent[2] for b in range(LAT)], 0)
        left_hi, left_lo = split_two(left)
        right_hi, right_lo = split_two(right)
        lhs = jnp.concatenate([left_hi, left_lo], 0)
        both = both + lax.dot_general(lhs, right_hi, NT, preferred_element_type=F32)
        both = both + lax.dot_general(lhs, right_lo, NT, preferred_element_type=F32)
    result = both[:3 * LAT] + both[3 * LAT:]
    for c in range(3):
        for a in range(LAT):
            out_ref[c:c + 1, a * LAT * LAT:(a + 1) * LAT * LAT] = result[c * LAT + a:c * LAT + a + 1]


def local(
    adjoint,
    jac_diag,
    conv_mats,
    face_scale,
    kappa,
    source,
    box_of_row,
    lattice_cell,
    lattice_frac,
    dres_dx,
    dobj_dx,
):
    boxes = lax.axis_size("blk")
    rows = box_of_row.shape[0]
    cap = 2 * rows // boxes
    fields, planes = adjoint.shape[:2]
    plane = adjoint.shape[2:]
    vmem = pl.BlockSpec(memory_space=pltpu.VMEM)
    hbm = pl.BlockSpec(memory_space=pltpu.HBM)
    params = pltpu.CompilerParams(vmem_limit_bytes=SMALL)
    conv = conv_mats.transpose(1, 0, 2)
    box_row = box_of_row.reshape(1, rows)
    cell_row = lattice_cell.reshape(1, rows)
    box_row, cell_row, conv, adjoint, jac_diag, face_scale, kappa, source = stay(
        box_row, cell_row, conv, adjoint, jac_diag, face_scale, kappa, source
    )
    lattice_frac, dres_dx, dobj_dx = stay(lattice_frac, dres_dx, dobj_dx)

    width = min(128, cap)
    payload = (boxes, ROW, cap // width, width)

    def shape(*dims):
        return jax.ShapeDtypeStruct(dims, F32)

    halo = shape(fields + 1, *plane)
    packed, to_mate, to_other, adj, kap, fill, jac, src, face = pl.pallas_call(
        functools.partial(pack_kernel, boxes, cap),
        out_shape=(
            shape(*payload),
            halo,
            halo,
            shape(*adjoint.shape),
            shape(*kappa.shape),
            shape(*conv.shape, *plane),
            shape(*jac_diag.shape),
            shape(*source.shape),
            shape(*face_scale.shape),
        ),
        in_specs=[hbm] * 11,
        out_specs=(hbm,) + (vmem,) * 8,
        scratch_shapes=[
            pltpu.VMEM(payload, F32),
            pltpu.SMEM(conv.shape, F32),
            pltpu.VMEM((1, rows), jnp.int32),
            pltpu.VMEM((1, rows), jnp.int32),
            pltpu.VMEM(lattice_frac.shape, F32),
            pltpu.VMEM(dres_dx.shape, F32),
            pltpu.VMEM(dobj_dx.shape, F32),
            pltpu.VMEM((1, rows), F32),
            pltpu.SemaphoreType.DMA((11,)),
            pltpu.SemaphoreType.DMA,
        ],
        compiler_params=params,
        name="pack_rows",
    )(
        adjoint,
        kappa,
        box_row,
        cell_row,
        lattice_frac,
        dres_dx,
        dobj_dx,
        conv,
        jac_diag,
        source,
        face_scale,
    )
    got = lax.all_to_all(packed, "blk", 0, 0, axis_index_groups=[spread(boxes)], tiled=True)

    pairs = [(i, i + 1) for i in range(boxes - 1)]
    both_ways = [[p for i, j in pairs if i % 2 == turn for p in ((i, j), (j, i))] for turn in (0, 1)]
    mate = lax.ppermute(to_mate, "blk", both_ways[0])
    other = lax.ppermute(to_other, "blk", both_ways[1])

    inner, edge = pl.pallas_call(
        sweep_kernel,
        out_shape=(
            shape(*adjoint.shape),
            shape(2 * (2 * fields + 2) + fields * fields, *plane),
        ),
        in_specs=[vmem] * 6,
        out_specs=(hbm, vmem),
        scratch_shapes=[
            pltpu.VMEM(adjoint.shape, F32),
            pltpu.SemaphoreType.DMA((4,)),
        ],
        compiler_params=params,
        name="sweep_planes",
    )(adj, jac, fill, face, kap, src)

    box_sens = pl.pallas_call(
        sum_kernel,
        out_shape=shape(3, LAT**3),
        in_specs=[vmem],
        out_specs=vmem,
        compiler_params=params,
        name="sum_rows",
    )(got)

    residual = pl.pallas_call(
        edge_kernel,
        out_shape=shape(*adjoint.shape),
        in_specs=[vmem] * 3 + [hbm, hbm],
        out_specs=hbm,
        scratch_shapes=[
            pltpu.VMEM((2, fields) + plane, F32),
            pltpu.SemaphoreType.DMA((2,)),
        ],
        input_output_aliases={4: 0},
        compiler_params=params,
        name="edge_planes",
    )(edge, mate, other, *stay(box_sens), inner)
    return residual, box_sens


def solution(mesh):
    in_specs = (
        P("group", "blk", None, None),
        P("group", None, "blk", None, None),
        P(),
        P("group", "blk", None, None),
        P(("group", "blk"), None, None),
        P("group", "blk", None, None),
        P(("group", "blk"), None),
        P(("group", "blk")),
        P(None, ("group", "blk")),
        P(None, None, ("group", "blk")),
        P(None, ("group", "blk")),
    )
    out_specs = (P("group", "blk", None, None), P("group", "blk"))
    return jax.shard_map(local, mesh=mesh, in_specs=in_specs, out_specs=out_specs, check_vma=False)
```

```python
import functools

import jax
import jax.numpy as jnp
from jax import lax
from jax.experimental import pallas as pl
from jax.experimental.pallas import tpu as pltpu
from jax.sharding import PartitionSpec as P

LAT = 16
CHUNK = 256
ROW = 7
SMALL = 12 * 2**20
F32 = jnp.float32
BF16 = jnp.bfloat16
NT = (((1,), (1,)), ((), ()))
NN = (((1,), (0,)), ((), ()))


def split_two(x):
    hi = x.astype(BF16)
    lo = (x - hi.astype(F32)).astype(BF16)
    return hi, lo


def on_even():
    return lax.axis_index("blk") % 2 == 0


def stay(*arrays):
    return [pltpu.with_memory_space_constraint(a, pltpu.HBM) for a in arrays]


def spread(count):
    quarter = count // 4
    order = []
    for k in range(quarter):
        order += [
            count - 1 - k,
            (k + 2) % quarter,
            2 * quarter + (k + 3) % quarter,
            quarter + (k + 1) % quarter,
        ]
    return order


def start_all(copies):
    for copy in copies:
        copy.start()
    return copies


def wait_all(copies):
    for copy in copies:
        copy.wait()


def pack_kernel(
    boxes,
    cap,
    adj_hbm,
    kap_hbm,
    box_hbm,
    cell_hbm,
    frac_hbm,
    dres_hbm,
    dobj_hbm,
    conv_hbm,
    jac_hbm,
    src_hbm,
    face_hbm,
    out_hbm,
    mate_ref,
    other_ref,
    adj_ref,
    kap_ref,
    fill_ref,
    jac_ref,
    src_ref,
    face_ref,
    out_ref,
    conv_ref,
    box_ref,
    cell_ref,
    frac_ref,
    dres_ref,
    dobj_ref,
    ranks_ref,
    sems,
    out_sem,
):
    fields, planes, _, lanes = adj_hbm.shape
    rows = planes * lanes
    moves = [(box_hbm, box_ref), (dres_hbm, dres_ref), (adj_hbm, adj_ref)]
    moves += [(dobj_hbm, dobj_ref), (frac_hbm, frac_ref), (cell_hbm, cell_ref)]
    moves += [(kap_hbm, kap_ref), (conv_hbm, conv_ref), (jac_hbm, jac_ref)]
    moves += [(src_hbm, src_ref), (face_hbm, face_ref)]
    copies = start_all(
        [pltpu.make_async_copy(src, dst, sems.at[i]) for i, (src, dst) in enumerate(moves)]
    )
    copies[0].wait()
    box = box_ref[...]

    chunks = rows // CHUNK
    names = lax.broadcasted_iota(jnp.int32, (boxes, CHUNK), 0)
    hot = [(box[:, j * CHUNK:(j + 1) * CHUNK] == names).astype(F32) for j in range(chunks)]
    earlier = (
        lax.broadcasted_iota(jnp.int32, (CHUNK, CHUNK), 0)
        < lax.broadcasted_iota(jnp.int32, (CHUNK, CHUNK), 1)
    ).astype(F32).astype(BF16)
    counts = lax.dot_general(
        jnp.concatenate(hot, 0).astype(BF16), earlier, NN, preferred_element_type=F32
    )
    offset = jnp.zeros((boxes, 1), F32)
    for j in range(chunks):
        here = counts[j * boxes:(j + 1) * boxes]
        ranks_ref[:, j * CHUNK:(j + 1) * CHUNK] = jnp.sum(
            hot[j] * (here + offset), axis=0, keepdims=True
        )
        offset = offset + here[:, CHUNK - 1:] + hot[j][:, CHUNK - 1:]

    wait_all(copies[1:7])
    even = on_even()
    for f in range(fields + 1):
        first = adj_ref[f, 0] if f < fields else kap_ref[0]
        last = adj_ref[f, planes - 1] if f < fields else kap_ref[planes - 1]
        mate_ref[f] = jnp.where(even, last, first)
        other_ref[f] = jnp.where(even, first, last)

    total = jnp.zeros((boxes * 16, cap), F32)
    slots = lax.broadcasted_iota(jnp.int32, (cap, CHUNK), 0).astype(F32)
    per = CHUNK // lanes
    for j in range(chunks):
        part = slice(j * CHUNK, (j + 1) * CHUNK)
        acc = dobj_ref[:, part]
        for k in range(fields):
            psi = jnp.concatenate(
                [adj_ref[k, x, 0:1, :] for x in range(j * per, (j + 1) * per)], 1
            )
            acc = acc - dres_ref[k, :, part] * psi
        values = jnp.concatenate(
            [acc, frac_ref[:, part], cell_ref[:, part].astype(F32), jnp.zeros((1, CHUNK), F32)], 0
        )
        hi = values.astype(BF16).astype(F32)
        both = jnp.concatenate([hi, values - hi], 0)
        mine = box[:, part]
        lhs = jnp.concatenate(
            [jnp.where(mine == b, both, 0.0) for b in spread(boxes)], 0
        ).astype(BF16)
        rhs = (slots == ranks_ref[:, part]).astype(F32).astype(BF16)
        total = total + lax.dot_general(lhs, rhs, NT, preferred_element_type=F32)
    width = out_ref.shape[-1]
    for b in range(boxes):
        block = total[b * 16:b * 16 + ROW] + total[b * 16 + 8:b * 16 + 8 + ROW]
        for i in range(cap // width):
            out_ref[b, :, i, :] = block[:, i * width:(i + 1) * width]
    out_copy = pltpu.make_async_copy(out_ref, out_hbm, out_sem)
    out_copy.start()
    wait_all(copies[7:])
    for k in range(fields):
        for d in range(3):
            for f in range(fields):
                fill_ref[k, d, f] = jnp.full(kap_ref.shape[1:], conv_ref[k, d, f], F32)
    out_copy.wait()


def plane_residual(psi, kap, below, above, jac, face, src, conv):
    fields = len(psi)
    rows, lanes = kap.shape
    row = lax.broadcasted_iota(jnp.int32, (rows, lanes), 0)
    lane = lax.broadcasted_iota(jnp.int32, (rows, lanes), 1)
    masks = ((row < rows - 1, row > 0), (lane < lanes - 1, lane > 0))

    def sides(value, dim):
        size = value.shape[dim]
        up = jnp.where(masks[dim][0], pltpu.roll(value, size - 1, dim), 0.0)
        down = jnp.where(masks[dim][1], pltpu.roll(value, 1, dim), 0.0)
        return up, down

    centre = list(psi) + [kap]
    result = []
    for f in range(fields):
        total = jac(0, f) * psi[0]
        for k in range(1, fields):
            total = total + jac(k, f) * psi[k]
        result.append(total - src(f))
    spread = None
    for d in range(3):
        pair = list(zip(above, below)) if d == 0 else [sides(v, d - 1) for v in centre]
        scale = 0.5 * face(d)
        diff = [scale * (pair[k][0] - pair[k][1]) for k in range(fields)]
        up = 0.5 * (kap + pair[fields][0])
        down = 0.5 * (kap + pair[fields][1])
        spread = up + down if spread is None else spread + up + down
        for f in range(fields):
            total = result[f]
            for k in range(fields):
                total = total + conv(k, d, f) * diff[k]
            result[f] = total - up * pair[f][0] - down * pair[f][1]
    return [result[f] + spread * psi[f] for f in range(fields)]


def sweep_kernel(
    adj_ref,
    jac_ref,
    fill_ref,
    face_ref,
    kap_ref,
    src_ref,
    out_hbm,
    edge_ref,
    out_ref,
    out_sems,
):
    fields, planes = adj_ref.shape[:2]
    steps = 4
    cuts = [planes * i // steps for i in range(steps + 1)]
    pieces = [slice(a, b) for a, b in zip(cuts[:-1], cuts[1:])]
    nothing = [jnp.zeros(kap_ref.shape[1:], F32)] * (fields + 1)
    sent = []
    for i, p in enumerate(pieces):
        for x in range(p.start, p.stop):
            def at(y):
                if 0 <= y < planes:
                    return [adj_ref[f, y] for f in range(fields)] + [kap_ref[y]]
                return nothing

            here = at(x)
            planes_of = plane_residual(
                here[:fields],
                here[fields],
                at(x - 1),
                at(x + 1),
                lambda k, f: jac_ref[k, f, x],
                lambda d: face_ref[d, x],
                lambda f: src_ref[f, x],
                lambda k, d, f: fill_ref[k, d, f],
            )
            for f in range(fields):
                out_ref[f, x] = planes_of[f]
            if x in (0, planes - 1):
                e = 0 if x == 0 else 2 * fields + 2
                for f in range(fields):
                    edge_ref[e + f] = planes_of[f]
                    edge_ref[e + fields + f] = here[f]
                edge_ref[e + 2 * fields] = here[fields]
                edge_ref[e + 2 * fields + 1] = face_ref[0, x]
        copy = pltpu.make_async_copy(out_ref.at[:, p], out_hbm.at[:, p], out_sems.at[i])
        copy.start()
        sent.append(copy)
    for k in range(fields):
        for f in range(fields):
            edge_ref[4 * fields + 4 + k * fields + f] = fill_ref[k, 0, f]
    wait_all(sent)


def edge_kernel(edge_ref, mate_ref, other_ref, after_ref, part_hbm, res_hbm, res_ref, out_sems):
    del after_ref, part_hbm
    fields, planes = res_hbm.shape[:2]
    even = on_even()
    copies = []
    for e in (0, 1):
        beyond = [jnp.where(even == (e == 0), other_ref[f], mate_ref[f]) for f in range(fields + 1)]
        base = e * (2 * fields + 2)
        kap = edge_ref[base + 2 * fields]
        scale = edge_ref[base + 2 * fields + 1] * (0.5 if e else -0.5)
        terms = [scale * beyond[k] for k in range(fields)]
        weight = 0.5 * (kap + beyond[fields])
        extra = 0.5 * beyond[fields]
        for f in range(fields):
            total = edge_ref[base + f] - weight * beyond[f] + extra * edge_ref[base + fields + f]
            for k in range(fields):
                total = total + edge_ref[4 * fields + 4 + k * fields + f] * terms[k]
            res_ref[e, f] = total
        copy = pltpu.make_async_copy(res_ref.at[e], res_hbm.at[:, e * (planes - 1)], out_sems.at[e])
        copy.start()
        copies.append(copy)
    wait_all(copies)


def sum_kernel(got_ref, out_ref):
    sources, _, cuts, width = got_ref.shape
    cap = cuts * width
    inner = LAT - 1
    points = lax.broadcasted_iota(jnp.int32, (LAT, cap), 0).astype(F32)
    both = jnp.zeros((6 * LAT, LAT * LAT), F32)
    fine = jnp.zeros((3 * LAT, LAT * LAT), F32)
    for s in range(sources):
        block = jnp.concatenate([got_ref[s, :, i, :] for i in range(cuts)], 1)
        cell = block[6:7]
        first = jnp.floor((cell + 0.5) * (1.0 / (inner * inner)))
        rest = cell - first * (inner * inner)
        second = jnp.floor((rest + 0.5) * (1.0 / inner))
        third = rest - second * inner
        tent = []
        for d, low in enumerate((first, second, third)):
            u = block[3 + d:4 + d]
            tent.append(
                jnp.where(points == low, 1.0 - u, 0.0) + jnp.where(points == low + 1.0, u, 0.0)
            )
        left = jnp.concatenate([tent[0] * block[c:c + 1] for c in range(3)], 0)
        right = jnp.concatenate([tent[1][b:b + 1] * tent[2] for b in range(LAT)], 0)
        left_hi, left_lo = split_two(left)
        right_hi, right_lo = split_two(right)
        lhs = jnp.concatenate([left_hi, left_lo], 0)
        both = both + lax.dot_general(lhs, right_hi, NT, preferred_element_type=F32)
        fine = fine + lax.dot_general(left_hi, right_lo, NT, preferred_element_type=F32)
    result = both[:3 * LAT] + (both[3 * LAT:] + fine)
    for c in range(3):
        for a in range(LAT):
            out_ref[c:c + 1, a * LAT * LAT:(a + 1) * LAT * LAT] = result[c * LAT + a:c * LAT + a + 1]


def local(
    adjoint,
    jac_diag,
    conv_mats,
    face_scale,
    kappa,
    source,
    box_of_row,
    lattice_cell,
    lattice_frac,
    dres_dx,
    dobj_dx,
):
    boxes = lax.axis_size("blk")
    rows = box_of_row.shape[0]
    cap = 2 * rows // boxes
    fields, planes = adjoint.shape[:2]
    plane = adjoint.shape[2:]
    vmem = pl.BlockSpec(memory_space=pltpu.VMEM)
    hbm = pl.BlockSpec(memory_space=pltpu.HBM)
    params = pltpu.CompilerParams(vmem_limit_bytes=SMALL)
    conv = conv_mats.transpose(1, 0, 2)
    box_row = box_of_row.reshape(1, rows)
    cell_row = lattice_cell.reshape(1, rows)
    box_row, cell_row, conv, adjoint, jac_diag, face_scale, kappa, source = stay(
        box_row, cell_row, conv, adjoint, jac_diag, face_scale, kappa, source
    )
    lattice_frac, dres_dx, dobj_dx = stay(lattice_frac, dres_dx, dobj_dx)

    width = min(128, cap)
    payload = (boxes, ROW, cap // width, width)

    def shape(*dims):
        return jax.ShapeDtypeStruct(dims, F32)

    halo = shape(fields + 1, *plane)
    packed, to_mate, to_other, adj, kap, fill, jac, src, face = pl.pallas_call(
        functools.partial(pack_kernel, boxes, cap),
        out_shape=(
            shape(*payload),
            halo,
            halo,
            shape(*adjoint.shape),
            shape(*kappa.shape),
            shape(*conv.shape, *plane),
            shape(*jac_diag.shape),
            shape(*source.shape),
            shape(*face_scale.shape),
        ),
        in_specs=[hbm] * 11,
        out_specs=(hbm,) + (vmem,) * 8,
        scratch_shapes=[
            pltpu.VMEM(payload, F32),
            pltpu.SMEM(conv.shape, F32),
            pltpu.VMEM((1, rows), jnp.int32),
            pltpu.VMEM((1, rows), jnp.int32),
            pltpu.VMEM(lattice_frac.shape, F32),
            pltpu.VMEM(dres_dx.shape, F32),
            pltpu.VMEM(dobj_dx.shape, F32),
            pltpu.VMEM((1, rows), F32),
            pltpu.SemaphoreType.DMA((11,)),
            pltpu.SemaphoreType.DMA,
        ],
        compiler_params=params,
        name="pack_rows",
    )(
        adjoint,
        kappa,
        box_row,
        cell_row,
        lattice_frac,
        dres_dx,
        dobj_dx,
        conv,
        jac_diag,
        source,
        face_scale,
    )
    got = lax.all_to_all(packed, "blk", 0, 0, axis_index_groups=[spread(boxes)], tiled=True)

    pairs = [(i, i + 1) for i in range(boxes - 1)]
    both_ways = [[p for i, j in pairs if i % 2 == turn for p in ((i, j), (j, i))] for turn in (0, 1)]
    mate = lax.ppermute(to_mate, "blk", both_ways[0])
    other = lax.ppermute(to_other, "blk", both_ways[1])

    inner, edge = pl.pallas_call(
        sweep_kernel,
        out_shape=(
            shape(*adjoint.shape),
            shape(2 * (2 * fields + 2) + fields * fields, *plane),
        ),
        in_specs=[vmem] * 6,
        out_specs=(hbm, vmem),
        scratch_shapes=[
            pltpu.VMEM(adjoint.shape, F32),
            pltpu.SemaphoreType.DMA((4,)),
        ],
        compiler_params=params,
        name="sweep_planes",
    )(adj, jac, fill, face, kap, src)

    box_sens = pl.pallas_call(
        sum_kernel,
        out_shape=shape(3, LAT**3),
        in_specs=[vmem],
        out_specs=vmem,
        compiler_params=params,
        name="sum_rows",
    )(got)

    residual = pl.pallas_call(
        edge_kernel,
        out_shape=shape(*adjoint.shape),
        in_specs=[vmem] * 3 + [hbm, hbm],
        out_specs=hbm,
        scratch_shapes=[
            pltpu.VMEM((2, fields) + plane, F32),
            pltpu.SemaphoreType.DMA((2,)),
        ],
        input_output_aliases={4: 0},
        compiler_params=params,
        name="edge_planes",
    )(edge, mate, other, *stay(box_sens), inner)
    return residual, box_sens


def solution(mesh):
    in_specs = (
        P("group", "blk", None, None),
        P("group", None, "blk", None, None),
        P(),
        P("group", "blk", None, None),
        P(("group", "blk"), None, None),
        P("group", "blk", None, None),
        P(("group", "blk"), None),
        P(("group", "blk")),
        P(None, ("group", "blk")),
        P(None, None, ("group", "blk")),
        P(None, ("group", "blk")),
    )
    out_specs = (P("group", "blk", None, None), P("group", "blk"))
    return jax.shard_map(local, mesh=mesh, in_specs=in_specs, out_specs=out_specs, check_vma=False)
```
